128 devices in a mesh: fsdp: 16 (over y, z), seq: 8 (over x, core).
Axes of the slice: x: 4, y: 4, z: 4, core: 2. Of those that a mesh axis runs over, the one named last changes fastest.
Arguments:
- tokens: bfloat16 [16384, 2048], P(('fsdp', 'seq')), may hold values from -6 to 6
- segments: int32 [16, 1024], P('fsdp'), may hold values from 0 to 2, as said below
- adapter_index: int32 [16], P('fsdp'), may hold values from 0 to 7
- attn_gain: float32 [2048], replicated, may hold values from 0.5 to 1.5
- w_qkv: bfloat16 [2048, 6144], P(None, 'fsdp'), may hold values from -0.125 to 0.125
- w_beta: bfloat16 [2048, 16], replicated, may hold values from -0.125 to 0.125
- conv_weight: float32 [4, 16, 384], replicated, may hold values from -3 to 3
- head_gain: float32 [128], replicated, may hold values from 0.5 to 1.5
- w_out: bfloat16 [2048, 2048], P(None, 'fsdp'), may hold values from -0.125 to 0.125
- ffn_gain: float32 [2048], replicated, may hold values from 0.5 to 1.5
- w_gateup: bfloat16 [2048, 11264], P(None, 'fsdp'), may hold values from -0.125 to 0.125
- w_down: bfloat16 [5632, 2048], P(None, 'fsdp'), may hold values from -0.078125 to 0.078125
- qkv_down: bfloat16 [8, 2048, 16], replicated, may hold values from -0.125 to 0.125
- qkv_up: bfloat16 [8, 16, 6144], replicated, may hold values from -0.75 to 0.75
- mixout_down: bfloat16 [8, 2048, 16], replicated, may hold values from -0.125 to 0.125
- mixout_up: bfloat16 [8, 16, 2048], replicated, may hold values from -0.75 to 0.75
- gateup_down: bfloat16 [8, 2048, 16], replicated, may hold values from -0.125 to 0.125
- gateup_up: bfloat16 [8, 16, 11264], replicated, may hold values from -0.75 to 0.75
- ffnout_down: bfloat16 [8, 5632, 16], replicated, may hold values from -0.078125 to 0.078125
- ffnout_up: bfloat16 [8, 16, 2048], replicated, may hold values from -0.75 to 0.75
- cotangent: bfloat16 [16384, 2048], P(('fsdp', 'seq')), may hold values from -6 to 6
Outputs:
- layer_out: bfloat16 [16384, 2048], P(('fsdp', 'seq'))
- input_grad: bfloat16 [16384, 2048], P(('fsdp', 'seq'))
- grad_qkvdown: float32 [8, 2048, 16], replicated
- grad_qkvup: float32 [8, 16, 6144], replicated
- grad_mixdown: float32 [8, 2048, 16], replicated
- grad_mixup: float32 [8, 16, 2048], replicated
- grad_gudown: float32 [8, 2048, 16], replicated
- grad_guup: float32 [8, 16, 11264], replicated
- grad_ffdown: float32 [8, 5632, 16], replicated
- grad_ffup: float32 [8, 16, 2048], replicated
The draws below stay inside these ranges and needn't reach their ends.
Inputs may be any that keep to these rules, and one draw needn't show every extreme that they name: `segments`: each row holds exactly three documents, ids 0, 1, 2, never falling; document 1 starts within the first 128 tokens and ends within the last 128.
All inputs are finite; a program needn't handle non-finite values.
Results may differ from the reference program's by a relative error of at most 0.017.
Values may be sent and summed in bfloat16 or wider, within the bound.
A program may use at most 320 MiB of HBM per device.

```python
import jax
import jax.numpy as jnp
from jax import lax

D = 2048
H = 16
HD = 128
FF = 5632
KERNEL = 4
BLOCK = 64
RANK = 16
ADAPTERS = 8
SHARD = 128
SEQ_LEN = 1024
TOKENS = 16384
N_FSDP = 16


def draw_segments(key, part):
    key = jax.random.fold_in(key, 7)
    first_key, last_key = jax.random.split(key)
    opening = jax.random.randint(first_key, (N_FSDP, 1), 1, SHARD)
    closing = jax.random.randint(last_key, (N_FSDP, 1), SEQ_LEN - SHARD + 1, SEQ_LEN)
    places = jnp.arange(SEQ_LEN, dtype=jnp.int32)[None, :]
    return (places >= opening).astype(jnp.int32) + (places >= closing).astype(jnp.int32)


def set_ends(values, rng, least, largest):
    longest = values.shape.index(max(values.shape))
    spots = []
    for shift in (0, 1):
        where = [jax.random.randint(jax.random.fold_in(rng, axis), (), 0, length) for axis, length in enumerate(values.shape)]
        where[longest] = (where[longest] + shift) % values.shape[longest]
        spots.append(tuple(where))
    return values.at[spots[0]].set(least).at[spots[1]].set(largest)


def steps_of(rng, dims, pieces, low, top_value):
    loudness = 1.0
    for dim, blocks in pieces:
        draws = jax.random.uniform(jax.random.fold_in(jax.random.fold_in(rng, 6), dim), (blocks,), jnp.float32, low / len(pieces), top_value / len(pieces))
        loudness = loudness * jnp.repeat(jnp.exp(draws), dims[dim] // blocks).reshape((-1,) + (1,) * (len(dims) - 1 - dim))
    return loudness


def gaussian(key, dims, scale, bound, pieces=(), kind=jnp.bfloat16):
    level = steps_of(key, dims, pieces, -0.22, 0.18) if pieces else 1.0
    drawn = jax.random.normal(key, dims, jnp.float32) * scale * level
    return jnp.minimum(jnp.maximum(drawn, -bound), bound).astype(kind)


def setup_inputs(seed: int = 0) -> dict:
    key_list = jax.random.split(jax.random.key(seed), 22)
    tokens = gaussian(key_list[0], (TOKENS, D), 1.0, 6.0, ((0, 128),))
    segments = draw_segments(jax.random.fold_in(key_list[21], 71), 0)
    adapter_index = set_ends(jax.random.randint(key_list[2], (N_FSDP,), 0, ADAPTERS), jax.random.fold_in(key_list[2], 1), 0, ADAPTERS - 1).astype(jnp.int32)
    attn_gain = jnp.clip(1.0 + 0.1 * jax.random.normal(key_list[3], (D,), jnp.float32), 0.5, 1.5)
    w_qkv = gaussian(key_list[4], (D, 3 * D), D ** -0.5, 0.125, ((1, 16),))
    w_beta = gaussian(key_list[5], (D, H), D ** -0.5, 0.125)
    conv_weight = gaussian(key_list[6], (KERNEL, H, 3 * HD), KERNEL ** -0.5, 3.0, (), jnp.float32)
    head_gain = jnp.clip(1.0 + 0.1 * jax.random.normal(key_list[7], (HD,), jnp.float32), 0.5, 1.5)
    w_out = gaussian(key_list[8], (D, D), D ** -0.5, 0.125, ((1, 16),))
    ffn_gain = jnp.clip(1.0 + 0.1 * jax.random.normal(key_list[9], (D,), jnp.float32), 0.5, 1.5)
    w_gateup = gaussian(key_list[10], (D, 2 * FF), D ** -0.5, 0.125, ((1, 16),))
    w_down = gaussian(key_list[11], (FF, D), FF ** -0.5, 0.078125, ((1, 16),))
    qkv_down = gaussian(key_list[12], (ADAPTERS, D, RANK), D ** -0.5, 0.125)
    qkv_up = gaussian(key_list[13], (ADAPTERS, RANK, 3 * D), (4 * RANK) ** -0.5, 0.75)
    mixout_down = gaussian(key_list[14], (ADAPTERS, D, RANK), D ** -0.5, 0.125)
    mixout_up = gaussian(key_list[15], (ADAPTERS, RANK, D), (4 * RANK) ** -0.5, 0.75)
    gateup_down = gaussian(key_list[16], (ADAPTERS, D, RANK), D ** -0.5, 0.125)
    gateup_up = gaussian(key_list[17], (ADAPTERS, RANK, 2 * FF), (4 * RANK) ** -0.5, 0.75)
    ffnout_down = gaussian(key_list[18], (ADAPTERS, FF, RANK), FF ** -0.5, 0.078125)
    ffnout_up = gaussian(key_list[19], (ADAPTERS, RANK, D), (4 * RANK) ** -0.5, 0.75)
    cotangent = gaussian(key_list[20], (TOKENS, D), 1.0, 6.0, ((0, 128),))
    return dict(tokens=tokens, segments=segments, adapter_index=adapter_index, attn_gain=attn_gain, w_qkv=w_qkv, w_beta=w_beta, conv_weight=conv_weight, head_gain=head_gain, w_out=w_out, ffn_gain=ffn_gain, w_gateup=w_gateup, w_down=w_down, qkv_down=qkv_down, qkv_up=qkv_up, mixout_down=mixout_down, mixout_up=mixout_up, gateup_down=gateup_down, gateup_up=gateup_up, ffnout_down=ffnout_down, ffnout_up=ffnout_up, cotangent=cotangent)


HIGH = lax.Precision.HIGHEST

@jax.custom_vjp
def low(v):
    return lax.optimization_barrier(v.astype(jnp.bfloat16)).astype(jnp.float32)

@jax.custom_vjp
def low_back(v):
    return v

def low_keep(v):
    return (low(v), None)

def low_pass(kept, grad):
    return (grad,)

def back_keep(v):
    return (v, None)

def back_low(kept, grad):
    return (low(grad),)
low.defvjp(low_keep, low_pass)
low_back.defvjp(back_keep, back_low)

def rms_scale(values, gain):
    return values * lax.rsqrt(lax.optimization_barrier(jnp.mean(values * values, axis=-1, keepdims=True)) + 1e-05) * gain

def matmul(left, right):
    return jnp.dot(left.astype(jnp.float32), right.astype(jnp.float32), precision=HIGH, preferred_element_type=jnp.float32)

def delta_block(state, block):
    query, keys, values, strength, doc_ids, enter = block
    size = doc_ids.shape[0]
    live = (doc_ids == enter).astype(jnp.float32)
    same = (doc_ids[:, None] == doc_ids[None, :]).astype(jnp.float32)
    row_pos = lax.broadcasted_iota(jnp.int32, (size, size), 0)
    col_pos = lax.broadcasted_iota(jnp.int32, (size, size), 1)
    strict = same * (row_pos > col_pos).astype(jnp.float32)
    causal = same * (row_pos >= col_pos).astype(jnp.float32)
    inner = jnp.einsum('ihd,jhd->hij', keys, keys, precision=HIGH)
    lower = jnp.transpose(strength)[:, :, None] * inner * strict[None]
    recalled = jnp.einsum('ihd,hde->ihe', keys, state, precision=HIGH)
    target = strength[:, :, None] * (values - live[:, None, None] * recalled)
    target = jnp.transpose(target, (1, 0, 2))
    update = jax.scipy.linalg.solve_triangular(lower, target, lower=True, unit_diagonal=True)
    scores = jnp.einsum('ihd,jhd->hij', query, keys, precision=HIGH) * causal[None]
    output = live[:, None, None] * jnp.einsum('ihd,hde->ihe', query, state, precision=HIGH)
    output = output + jnp.einsum('hij,hje->ihe', scores, update, precision=HIGH)
    tail = (doc_ids == doc_ids[size - 1]).astype(jnp.float32)
    state = live[size - 1] * state + jnp.einsum('jhd,j,hje->hde', keys, tail, update, precision=HIGH)
    return (state, output)

def mixer(joined, beta_raw, conv_w, head_gain, doc_ids):
    length = joined.shape[0]
    kernel = conv_w.shape[0]
    mixed = conv_w[kernel - 1] * joined
    for lag in range(1, kernel):
        shifted = jnp.concatenate([jnp.zeros((lag,) + joined.shape[1:], jnp.float32), joined[:length - lag]], axis=0)
        keep = jnp.concatenate([jnp.zeros((lag,), jnp.float32), (doc_ids[lag:] == doc_ids[:length - lag]).astype(jnp.float32)])
        mixed = mixed + conv_w[kernel - 1 - lag] * shifted * keep[:, None, None]
    active = jax.nn.silu(mixed)
    width = joined.shape[-1] // 3
    heads = joined.shape[1]
    query = active[..., :width]
    keys = active[..., width:2 * width]
    values = active[..., 2 * width:]
    query = query * lax.rsqrt(lax.optimization_barrier(jnp.sum(query * query, axis=-1, keepdims=True)) + 1e-06) * width ** (-0.5)
    keys = keys * lax.rsqrt(lax.optimization_barrier(jnp.sum(keys * keys, axis=-1, keepdims=True)) + 1e-06)
    strength = jax.nn.sigmoid(beta_raw[..., 0])
    blocks = length // BLOCK
    previous = jnp.concatenate([jnp.full((1,), -1, jnp.int32), doc_ids[:-1].astype(jnp.int32)])
    enter = previous.reshape(blocks, BLOCK)[:, 0]

    def cut(array):
        return array.reshape((blocks, BLOCK) + array.shape[1:])
    start_state = jnp.zeros((heads, width, width), jnp.float32)
    final_state, outputs = lax.scan(jax.checkpoint(delta_block), start_state, (cut(query), cut(keys), cut(values), cut(strength), cut(doc_ids.astype(jnp.int32)), enter))
    result = outputs.reshape(length, heads, width)
    return rms_scale(result, head_gain)

def adapted(inputs, down, upper, which):
    inner = low_back(low(matmul(inputs, down[which])))
    return matmul(inner, upper[which])

def layer(rows, doc_ids, which, frozen, adapters):
    attn_gain, w_qkv, w_beta, conv_weight, head_gain, w_out, ffn_gain, w_gateup, w_down = frozen
    qkv_down, qkv_up, mix_down, mix_up, gu_down, gu_up, ff_down, ff_up = adapters
    length = rows.shape[0]
    normed = low(rms_scale(rows, attn_gain))
    joined = low_back(low(matmul(normed, w_qkv) + adapted(normed, qkv_down, qkv_up, which)))
    raw_beta = low_back(low(matmul(normed, w_beta)))
    mixed = mixer(joined.reshape(length, H, 3 * HD), raw_beta.reshape(length, H, 1), conv_weight, head_gain, doc_ids)
    mixed = low_back(low(mixed.reshape(length, D)))
    branch = low_back(matmul(mixed, w_out) + adapted(mixed, mix_down, mix_up, which))
    middle = rows + branch
    normed2 = low(rms_scale(middle, ffn_gain))
    gateup = low_back(matmul(normed2, w_gateup) + adapted(normed2, gu_down, gu_up, which))
    hidden = low(jax.nn.silu(gateup[:, :FF]) * gateup[:, FF:])
    return middle + low_back(matmul(hidden, w_down) + adapted(hidden, ff_down, ff_up, which))

def reference(tokens, segments, adapter_index, attn_gain, w_qkv, w_beta, conv_weight, head_gain, w_out, ffn_gain, w_gateup, w_down, qkv_down, qkv_up, mixout_down, mixout_up, gateup_down, gateup_up, ffnout_down, ffnout_up, cotangent):
    frozen = tuple((item.astype(jnp.float32) for item in (attn_gain, w_qkv, w_beta, conv_weight, head_gain, w_out, ffn_gain, w_gateup, w_down)))
    adapters = tuple((item.astype(jnp.float32) for item in (qkv_down, qkv_up, mixout_down, mixout_up, gateup_down, gateup_up, ffnout_down, ffnout_up)))
    inputs = tokens.astype(jnp.float32).reshape(N_FSDP, SEQ_LEN, D)
    grads_in = cotangent.astype(jnp.float32).reshape(N_FSDP, SEQ_LEN, D)

    def one(totals, item):
        rows, doc_ids, which, grad_rows = item

        def forward(rows_in, adapt_in):
            return layer(rows_in, doc_ids, which, frozen, adapt_in)
        result, pullback = jax.vjp(forward, rows, adapters)
        grad_row, grad_adapt = pullback(grad_rows)
        totals = jax.tree.map(jnp.add, totals, grad_adapt)
        return (totals, (result.astype(jnp.bfloat16), grad_row.astype(jnp.bfloat16)))
    zeros = tuple((jnp.zeros_like(item) for item in adapters))
    totals, (results, grad_rows) = lax.scan(one, zeros, (inputs, segments.astype(jnp.int32), adapter_index.astype(jnp.int32), grads_in))
    return (results.reshape(TOKENS, D), grad_rows.reshape(TOKENS, D), totals[0], totals[1], totals[2], totals[3], totals[4], totals[5], totals[6], totals[7])
```

```python
import functools
import jax
import jax.numpy as jnp
from jax import lax
from jax.experimental import pallas as pl
from jax.experimental.pallas import tpu as pltpu
from jax.sharding import PartitionSpec as P

F32 = jnp.float32
BF16 = jnp.bfloat16
CH = 128
PAD = 16


def mm(a, b):
    return jnp.dot(a.astype(BF16), b.astype(BF16), preferred_element_type=F32)


def mm_nt(a, b):
    return lax.dot_general(
        a.astype(BF16), b.astype(BF16), (((1,), (1,)), ((), ())), preferred_element_type=F32
    )


def mm_tn(a, b):
    return lax.dot_general(
        a.astype(BF16), b.astype(BF16), (((0,), (0,)), ((), ())), preferred_element_type=F32
    )


def split(a):
    high = a.astype(BF16)
    return high, (a - high.astype(F32)).astype(BF16)


def mm_fine(a, b):
    ah, al = split(a)
    bh, bl = split(b)
    return jnp.dot(
        jnp.concatenate([ah, al, ah], axis=1),
        jnp.concatenate([bh, bh, bl], axis=0),
        preferred_element_type=F32,
    )


def unit_lower_inverse(lower, row, col, product):
    near = jnp.where((row >> 3) == (col >> 3), lower, 0.0)
    eye = (row == col).astype(F32)
    second = product(near, near)
    fourth = product(second, second)
    inverse = eye - near + second - product(near, second)
    inverse = inverse + product(inverse, fourth)
    for bits in (3, 4, 5, 6):
        joining = ((row >> (bits + 1)) == (col >> (bits + 1))) & ((row >> bits) != (col >> bits))
        below = jnp.where(joining, lower, 0.0)
        inverse = inverse - product(inverse, product(below, inverse))
    return inverse


def sigmoid(v):
    return 1.0 / (1.0 + jnp.exp(-v))


def chunk_masks(c, dcol, drow):
    start = pl.multiple_of(c * CH, CH)
    docs = dcol[pl.ds(start + PAD, CH), :]
    before = dcol[pl.ds(start + PAD - 8, 8), :][7:8, :]
    last = docs[CH - 1 :, :]
    same = docs == drow[pl.ds(c, 1), :]
    live = (docs == before).astype(F32)
    tail = (docs == last).astype(F32)
    live_last = (last == before).astype(F32)
    return docs, same, live, tail, live_last


def conv_chunk(c, joined, dcol, taps, docs):
    start = pl.multiple_of(c * CH, CH)
    window = joined[pl.ds(start, CH + PAD), : taps.shape[1]].astype(F32)
    ids = dcol[pl.ds(start, CH + PAD), :]
    total = window[PAD:, :] * taps[3:4, :]
    for lag in (1, 2, 3):
        keep = (ids[PAD - lag : PAD - lag + CH, :] == docs).astype(F32)
        keep = jnp.concatenate([keep] * (taps.shape[1] // CH), axis=1)
        total = total + window[PAD - lag : PAD - lag + CH, :] * keep * taps[3 - lag : 4 - lag, :]
    return total


def raw_chunk(c, joined, taps):
    rows = pl.ds(pl.multiple_of(c * CH + PAD, PAD), CH)
    return joined[rows, taps.shape[1] :].astype(F32)


def bring(source, joined, sem):
    copy = pltpu.make_async_copy(source, joined.at[pl.ds(PAD, source.shape[0]), :], sem)
    copy.start()
    joined[pl.ds(0, PAD), :] = jnp.zeros((PAD, joined.shape[1]), joined.dtype)
    copy.wait()


def normal_parts(act):
    query, keys, values = act[:, :CH], act[:, CH : 2 * CH], act[:, 2 * CH :]
    q_scale = lax.rsqrt(jnp.sum(query * query, axis=-1, keepdims=True) + 1e-06)
    k_scale = lax.rsqrt(jnp.sum(keys * keys, axis=-1, keepdims=True) + 1e-06)
    return query * q_scale * CH**-0.5, keys * k_scale, values, q_scale, k_scale


def mixer_fwd_kernel(
    heads, chunks, source, dcol, drow, taps, gain,
    mixed, o_out, t_out, d_out, s_out,
    joined, q_s, k_s, u_s, w_s, p_s, sem,
):
    bring(source, joined, sem)
    row = lax.broadcasted_iota(jnp.int32, (CH, CH), 0)
    col = lax.broadcasted_iota(jnp.int32, (CH, CH), 1)

    def prepare(c, h, docs, same, live, act, raws):
        start = pl.multiple_of(c * CH, CH)
        rows = pl.ds(start, CH)
        query, keys, values, _, _ = normal_parts(act[:, h * 3 * CH : (h + 1) * 3 * CH])
        beta = sigmoid(raws[:, h : h + 1])
        inner = mm_nt(keys, keys)
        lower = jnp.where(same & (row > col), inner * beta, 0.0)
        inverse = unit_lower_inverse(lower, row, col, mm_fine)
        t_out[h, rows, :] = inverse
        both = mm(inverse, jnp.concatenate([values * beta, keys * (beta * live)], axis=1))
        u_s[h, rows, :] = both[:, :CH]
        w_s[h, rows, :] = both[:, CH:].astype(BF16)
        scores = jnp.where(same & (row >= col), mm_nt(query, keys), 0.0)
        p_s[h, rows, :] = scores.astype(BF16)
        q_s[h, rows, :] = (query * live).astype(BF16)
        k_s[h, rows, :] = keys

    def first(step, carry):
        for part in range(2):
            c = step * 2 + part
            docs, same, live, tail, live_last = chunk_masks(c, dcol, drow)
            conv = conv_chunk(c, joined, dcol, taps, docs)
            act = conv * sigmoid(conv)
            raws = raw_chunk(c, joined, taps)
            for h in range(heads):
                prepare(c, h, docs, same, live, act, raws)
        return carry

    lax.fori_loop(0, chunks // 2, first, 0)

    def second(c, states):
        rows = pl.ds(pl.multiple_of(c * CH, CH), CH)
        docs, same, live, tail, live_last = chunk_masks(c, dcol, drow)
        after = []
        for h in range(heads):
            state = states[h]
            s_out[h, rows, :] = state
            update = u_s[h, rows, :] - mm(w_s[h, rows, :], state)
            d_out[h, rows, :] = update
            after.append(state * live_last + mm_tn(k_s[h, rows, :] * tail, update))
        return tuple(after)

    zero = jnp.zeros((CH, CH), F32)
    lax.fori_loop(0, chunks, second, (zero,) * heads)

    def third(c, carry):
        rows = pl.ds(pl.multiple_of(c * CH, CH), CH)
        for h in range(heads):
            out = mm(
                jnp.concatenate([q_s[h, rows, :], p_s[h, rows, :]], axis=1),
                jnp.concatenate(
                    [s_out[h, rows, :].astype(BF16), d_out[h, rows, :].astype(BF16)], axis=0
                ),
            )
            o_out[h, rows, :] = out
            scale = lax.rsqrt(jnp.mean(out * out, axis=-1, keepdims=True) + 1e-05)
            mixed[rows, h * CH : (h + 1) * CH] = (out * scale * gain[...]).astype(BF16)
        return carry

    lax.fori_loop(0, chunks, third, 0)


def mixer_fwd(joined, dcol, drow, taps, gain):
    tokens, wide = joined.shape
    heads = wide // (3 * CH)
    chunks = tokens // CH
    square = jax.ShapeDtypeStruct((heads, tokens, CH), F32)
    return pl.pallas_call(
        functools.partial(mixer_fwd_kernel, heads, chunks),
        out_shape=(jax.ShapeDtypeStruct((tokens, heads * CH), BF16), square, square, square, square),
        in_specs=[pl.BlockSpec(memory_space=pl.ANY)] + [pl.BlockSpec(memory_space=pltpu.VMEM)] * 4,
        out_specs=(pl.BlockSpec(memory_space=pltpu.VMEM),) * 5,
        scratch_shapes=[
            pltpu.VMEM((tokens + PAD, wide), BF16),
            pltpu.VMEM((heads, tokens, CH), BF16),
            pltpu.VMEM((heads, tokens, CH), F32),
            pltpu.VMEM((heads, tokens, CH), F32),
            pltpu.VMEM((heads, tokens, CH), BF16),
            pltpu.VMEM((heads, tokens, CH), BF16),
            pltpu.SemaphoreType.DMA,
        ],
        compiler_params=pltpu.CompilerParams(vmem_limit_bytes=48 << 20),
        name="mixer_fwd",
    )(joined, dcol, drow, taps, gain)


def mixer_bwd_kernel(
    heads, chunks, source, dcol, drow, taps, gain, grad, o_in, t_in, d_in, s_in,
    dj_out,
    joined, e_s, f_s, w_s, x_s, ds_s, go_s, dc_s, sem,
):
    bring(source, joined, sem)
    row = lax.broadcasted_iota(jnp.int32, (CH, CH), 0)
    col = lax.broadcasted_iota(jnp.int32, (CH, CH), 1)
    width = 3 * CH

    def revive(c):
        docs, same, live, tail, live_last = chunk_masks(c, dcol, drow)
        conv = conv_chunk(c, joined, dcol, taps, docs)
        raws = raw_chunk(c, joined, taps)
        return docs, same, live, tail, live_last, conv, raws

    def first(c, carry):
        docs, same, live, tail, live_last, conv, raws = revive(c)
        act = conv * sigmoid(conv)
        rows = pl.ds(pl.multiple_of(c * CH, CH), CH)
        for h in range(heads):
            query, keys, values, _, _ = normal_parts(act[:, h * width : (h + 1) * width])
            beta = sigmoid(raws[:, h : h + 1])
            out = o_in[h, rows, :]
            weighted = grad[rows, h * CH : (h + 1) * CH].astype(F32) * gain[...]
            scale = lax.rsqrt(jnp.mean(out * out, axis=-1, keepdims=True) + 1e-05)
            grad_o = scale * weighted - out * (
                scale * scale * scale * jnp.mean(weighted * out, axis=-1, keepdims=True)
            )
            go_s[h, rows, :] = grad_o
            scores = jnp.where(same & (row >= col), mm_nt(query, keys), 0.0)
            ef = mm_tn(jnp.concatenate([scores, query * live], axis=1), grad_o)
            e_s[h, rows, :] = ef[:CH]
            f_s[h, rows, :] = ef[CH:]
            w_s[h, rows, :] = mm(t_in[h, rows, :], keys * (beta * live)).astype(BF16)
            x_s[h, rows, :] = keys * tail
        return carry

    lax.fori_loop(0, chunks, first, 0)

    def second(step, states):
        c = chunks - 1 - step
        rows = pl.ds(pl.multiple_of(c * CH, CH), CH)
        docs, same, live, tail, live_last = chunk_masks(c, dcol, drow)
        before = []
        for h in range(heads):
            state = states[h]
            ds_s[h, rows, :] = state
            grad_update = e_s[h, rows, :] + mm(x_s[h, rows, :], state)
            x_s[h, rows, :] = grad_update
            before.append(
                state * live_last + f_s[h, rows, :] - mm_tn(w_s[h, rows, :], grad_update)
            )
        return tuple(before)

    zero = jnp.zeros((CH, CH), F32)
    lax.fori_loop(0, chunks, second, (zero,) * heads)

    dc_s[pl.ds(chunks * CH, PAD), :] = jnp.zeros((PAD, heads * width), F32)

    def third(c, carry):
        docs, same, live, tail, live_last, conv, raws = revive(c)
        gate = sigmoid(conv)
        act = conv * gate
        slope = gate * (1.0 + conv * (1.0 - gate))
        rows = pl.ds(pl.multiple_of(c * CH, CH), CH)
        lane = lax.broadcasted_iota(jnp.int32, (CH, CH), 1)
        grad_raw = jnp.zeros((CH, CH), F32)
        for h in range(heads):
            part = act[:, h * width : (h + 1) * width]
            query, keys, values, q_scale, k_scale = normal_parts(part)
            beta = sigmoid(raws[:, h : h + 1])
            state, update, state_grad = s_in[h, rows, :], d_in[h, rows, :], ds_s[h, rows, :]
            grad_o = go_s[h, rows, :]
            grad_target = mm_tn(t_in[h, rows, :], x_s[h, rows, :])
            pair = mm_nt(jnp.concatenate([grad_target, grad_o], axis=0), update)
            grad_lower = jnp.where(same & (row > col), -pair[:CH], 0.0)
            grad_scores = jnp.where(same & (row >= col), pair[CH:], 0.0)
            inner = mm_nt(keys, keys)
            recalled = mm(keys, state)
            grad_beta = jnp.sum(
                grad_lower * inner + grad_target * (values - live * recalled),
                axis=-1,
                keepdims=True,
            )
            grad_inner = grad_lower * beta
            back = mm_nt(
                jnp.concatenate([grad_o * live, -grad_target * (beta * live)], axis=0), state
            )
            grad_query = back[:CH] + mm(grad_scores, keys)
            grad_keys = (
                back[CH:]
                + mm_tn(
                    jnp.concatenate([grad_scores, grad_inner], axis=0),
                    jnp.concatenate([query, keys], axis=0),
                )
                + mm(grad_inner, keys)
                + mm_nt(update * tail, state_grad)
            )
            grad_values = grad_target * beta
            raw_q, raw_k = part[:, :CH], part[:, CH : 2 * CH]
            grad_query = grad_query * CH**-0.5
            grad_q = q_scale * grad_query - raw_q * (
                q_scale * q_scale * q_scale * jnp.sum(grad_query * raw_q, axis=-1, keepdims=True)
            )
            grad_k = k_scale * grad_keys - raw_k * (
                k_scale * k_scale * k_scale * jnp.sum(grad_keys * raw_k, axis=-1, keepdims=True)
            )
            dc_s[rows, h * width : (h + 1) * width] = (
                jnp.concatenate([grad_q, grad_k, grad_values], axis=1)
                * slope[:, h * width : (h + 1) * width]
            )
            grad_raw = jnp.where(lane == h, grad_beta * beta * (1.0 - beta), grad_raw)
        dj_out[rows, heads * width :] = grad_raw.astype(BF16)
        return carry

    lax.fori_loop(0, chunks, third, 0)

    def fourth(c, carry):
        start = pl.multiple_of(c * CH, CH)
        rows = pl.ds(start, CH)
        window = dc_s[pl.ds(start, CH + PAD), :]
        ids = dcol[pl.ds(start + PAD, CH + PAD), :]
        total = window[:CH] * taps[3:4, :]
        for lag in (1, 2, 3):
            keep = (ids[lag : lag + CH] == ids[:CH]).astype(F32)
            keep = jnp.concatenate([keep] * (heads * 3), axis=1)
            total = total + window[lag : lag + CH] * keep * taps[3 - lag : 4 - lag, :]
        dj_out[rows, : heads * width] = total.astype(BF16)
        return carry

    lax.fori_loop(0, chunks, fourth, 0)


def mixer_bwd(joined, dcol, drow, taps, gain, grad, o, t, d, s):
    tokens, wide = joined.shape
    heads = wide // (3 * CH)
    chunks = tokens // CH
    square = (heads, tokens, CH)
    return pl.pallas_call(
        functools.partial(mixer_bwd_kernel, heads, chunks),
        out_shape=jax.ShapeDtypeStruct((tokens, wide), BF16),
        in_specs=[pl.BlockSpec(memory_space=pl.ANY)] + [pl.BlockSpec(memory_space=pltpu.VMEM)] * 9,
        out_specs=pl.BlockSpec(memory_space=pltpu.VMEM),
        scratch_shapes=[
            pltpu.VMEM((tokens + PAD, wide), BF16),
            pltpu.VMEM(square, F32),
            pltpu.VMEM(square, F32),
            pltpu.VMEM(square, BF16),
            pltpu.VMEM(square, F32),
            pltpu.VMEM(square, F32),
            pltpu.VMEM(square, F32),
            pltpu.VMEM((tokens + PAD, heads * 3 * CH), F32),
            pltpu.SemaphoreType.DMA,
        ],
        compiler_params=pltpu.CompilerParams(vmem_limit_bytes=48 << 20),
        name="mixer_bwd",
    )(joined, dcol, drow, taps, gain, grad, o, t, d, s)

MESH = pl.DeviceIdType.MESH
SIDE = 128


class Line:
    def __init__(self, send_sems, recv_sems, local_sems):
        self.send_sems, self.recv_sems, self.local_sems = send_sems, recv_sems, local_sems
        self.used, self.used_local = 0, 0

    def make(self, src, dst, device):
        at = self.used
        self.used += 1
        return pltpu.make_async_remote_copy(
            src_ref=src, dst_ref=dst, send_sem=self.send_sems.at[at],
            recv_sem=self.recv_sems.at[at], device_id=device, device_id_type=MESH,
        )

    def send(self, src, dst, device):
        copy = self.make(src, dst, device)
        copy.start()
        return copy

    def local(self, src, dst):
        at = self.used_local
        self.used_local += 1
        copy = pltpu.make_async_copy(src, dst, self.local_sems.at[at])
        copy.start()
        return copy


def seq_places():
    s = lax.axis_index("seq")
    x, core = s // 2, lax.rem(s, 2)
    there = lambda d: lax.rem(x + d, 4) * 2 + core
    return s, x * 2 + 1 - core, there(1), there(3), there(2)


def greet(seq_peers, plane_peers):
    barrier = pltpu.get_barrier_semaphore()
    for p in seq_peers:
        pl.semaphore_signal(barrier, inc=1, device_id={"seq": p}, device_id_type=MESH)
    for p in plane_peers:
        pl.semaphore_signal(barrier, inc=1, device_id={"fsdp": p}, device_id_type=MESH)
    pl.semaphore_wait(barrier, len(seq_peers) + len(plane_peers))


class RingGather:
    def __init__(self, line, block, out):
        self.line, self.block, self.out = line, block, out
        half = block.shape[0] // 2
        self.low, self.high = pl.ds(0, half), pl.ds(half, half)

    def pass_on(self, s, rows, peer):
        return self.line.send(self.out.at[s, rows], self.out.at[s, rows], {"seq": peer})

    def start(self):
        s, partner, right, left, far = seq_places()
        send = lambda rows, p: self.line.send(
            self.block.at[rows], self.out.at[s, rows], {"seq": p}
        )
        self.a0, self.b0 = send(self.low, right), send(self.high, left)
        self.a1, self.b1 = send(self.high, right), send(self.low, left)
        self.p = self.line.send(self.block, self.out.at[s], {"seq": partner})
        self.own = self.line.local(self.block, self.out.at[s])

    def middle(self):
        s, partner, right, left, far = seq_places()
        self.a0.wait_recv()
        self.f0 = self.pass_on(left, self.low, right)
        self.g = [self.pass_on(left, self.low, partner)]
        self.b0.wait_recv()
        self.f1 = self.pass_on(right, self.high, left)
        self.g.append(self.pass_on(right, self.high, partner))
        self.a1.wait_recv()
        self.g.append(self.pass_on(left, self.high, partner))
        self.b1.wait_recv()
        self.g.append(self.pass_on(right, self.low, partner))

    def finish(self):
        s, partner, right, left, far = seq_places()
        self.f0.wait_recv()
        self.g.append(self.pass_on(far, self.low, partner))
        self.f1.wait_recv()
        self.g.append(self.pass_on(far, self.high, partner))
        for copy in (self.a0, self.b0, self.a1, self.b1, self.f0, self.f1):
            copy.wait_send()
        for copy in [self.p] + self.g:
            copy.wait()
        self.own.wait()


RING_COPIES = 13


def plane_places():
    f = lax.axis_index("fsdp")
    return f, f // 4, lax.rem(f, 4)


class PlaneGather:
    COPIES = 30

    def __init__(self, line, place):
        self.line, self.place = line, place

    def to(self, y, z):
        return lax.rem(y, 4) * 4 + lax.rem(z, 4)

    def first(self):
        f, y, z = plane_places()
        self.one = []
        for half in (0, 1):
            ref = self.place(f, half)
            row = []
            for d in (1, 3, 2):
                peer = self.to(y, z + d) if half == 0 else self.to(y + d, z)
                row.append(self.line.send(ref, ref, {"fsdp": peer}))
            self.one.append(row)

    def second(self):
        f, y, z = plane_places()
        self.two = []
        for k, d in enumerate((0, 1, 3, 2)):
            for half in (0, 1):
                if k:
                    self.one[half][k - 1].wait_recv()
                source = self.to(y, z + 4 - d) if half == 0 else self.to(y + 4 - d, z)
                ref = self.place(source, half)
                for e in (1, 3, 2):
                    peer = self.to(y + e, z) if half == 0 else self.to(y, z + e)
                    self.two.append(self.line.send(ref, ref, {"fsdp": peer}))

    def finish(self):
        for row in self.one:
            for copy in row:
                copy.wait_send()
        for copy in self.two:
            copy.wait()


class Scatter:
    COPIES = 17

    def __init__(self, line, sources, source_block, into):
        self.line, self.sources = line, sources
        self.source_block, self.into = source_block, into

    def start(self):
        f, _, _ = plane_places()
        line = self.line
        self.at = line.used
        line.used += self.COPIES
        self.local_at = line.used_local
        line.used_local += 2
        for j, source in enumerate(self.sources):
            @pl.when(f == source)
            def _():
                for d in range(1, 16):
                    self.copy(j, d, lax.rem(f + d, 16)).start()
                self.keep(j).start()

    def copy(self, j, d, t):
        line = self.line
        return pltpu.make_async_remote_copy(
            src_ref=self.source_block(t), dst_ref=self.into(t, j),
            send_sem=line.send_sems.at[self.at + d], recv_sem=line.recv_sems.at[self.at + j],
            device_id={"fsdp": t}, device_id_type=MESH,
        )

    def keep(self, j):
        f, _, _ = plane_places()
        return pltpu.make_async_copy(
            self.source_block(f), self.into(f, j), self.line.local_sems.at[self.local_at + j]
        )

    def arrive(self):
        f, _, _ = plane_places()
        for j, source in enumerate(self.sources):
            @pl.when(f == source)
            def _():
                self.keep(j).wait()

            @pl.when(f != source)
            def _():
                ref = self.into(f, j)
                pltpu.make_async_remote_copy(
                    src_ref=ref, dst_ref=ref, send_sem=self.line.send_sems.at[self.at],
                    recv_sem=self.line.recv_sems.at[self.at + j],
                    device_id={"fsdp": lax.rem(f + 1, 16)}, device_id_type=MESH,
                ).wait_recv()

    def finish(self):
        f, _, _ = plane_places()
        for j, source in enumerate(self.sources):
            @pl.when(f == source)
            def _():
                for d in range(1, 16):
                    self.copy(j, d, lax.rem(f + d, 16)).wait_send()


def all_plane():
    f = lax.axis_index("fsdp")
    return [lax.rem(f + d, 16) for d in range(1, 16)]


def line_peers():
    f, y, z = plane_places()
    return [y * 4 + lax.rem(z + d, 4) for d in (1, 2, 3)] + [
        lax.rem(y + d, 4) * 4 + z for d in (1, 2, 3)
    ]


def sems(copies, local):
    return [
        pltpu.SemaphoreType.DMA((copies,)),
        pltpu.SemaphoreType.DMA((copies,)),
        pltpu.SemaphoreType.DMA((local,)),
    ]


ANY = pl.BlockSpec(memory_space=pl.ANY)
VMEM = pl.BlockSpec(memory_space=pltpu.VMEM)


def columns_place(out):
    rows = out.shape[0] // 2
    return lambda f, half: out.at[pl.ds(half * rows, rows), pl.ds(pl.multiple_of(f * 128, 128), 128)]


def block_of(ref, t):
    return ref.at[:, pl.ds(pl.multiple_of(t * 128, 128), 128)]


def start_kernel(
    payload, w_qkv, w_out, q_side, beta_side, out_side, everyone, wq, wo, send, recv, local
):
    s, partner, right, left, far = seq_places()
    f, _, _ = plane_places()
    greet([partner, right, left], all_plane())
    line = Line(send, recv, local)
    depth, width = w_qkv.shape
    scatter = Scatter(
        line, (2 * s, 2 * s + 1),
        lambda t: w_qkv.at[pl.ds(t * 128, 128), :],
        lambda t, j: wq.at[pl.ds(t * 128, 128), pl.ds(j * width, width)],
    )
    scatter.start()
    ring = RingGather(line, payload, everyone)
    ring.start()
    share = wo.shape[0]
    mine = line.local(w_out.at[pl.ds(s * share, share), :], block_of(wo, f))
    sides = [
        line.local(q_side, wq.at[pl.ds(depth, SIDE), :]),
        line.local(beta_side, wq.at[pl.ds(0, depth), pl.ds(2 * width, SIDE)]),
        line.local(out_side, wo.at[:, pl.ds(wo.shape[1] - SIDE, SIDE)]),
    ]
    qkv = PlaneGather(
        line,
        lambda t, half: wq.at[pl.ds(t * 128 + half * 64, 64), pl.ds(0, 2 * width)],
    )
    out = PlaneGather(line, columns_place(wo))
    scatter.arrive()
    qkv.first()
    mine.wait()
    out.first()
    ring.middle()
    qkv.second()
    out.second()
    ring.finish()
    for item in [scatter, qkv, out]:
        item.finish()
    for copy in sides:
        copy.wait()


def start_gather(payload, w_qkv, w_out, q_side, beta_side, out_side):
    seq, wide = lax.axis_size("seq"), payload.shape[1]
    copies = RING_COPIES + Scatter.COPIES + 2 * PlaneGather.COPIES
    return pl.pallas_call(
        start_kernel,
        out_shape=(
            jax.ShapeDtypeStruct((seq,) + payload.shape, BF16),
            jax.ShapeDtypeStruct((wide, q_side.shape[1]), BF16),
            jax.ShapeDtypeStruct((out_side.shape[0], wide), BF16),
        ),
        in_specs=[ANY] * 6,
        out_specs=(ANY,) * 3,
        scratch_shapes=sems(copies, 8),
        compiler_params=pltpu.CompilerParams(collective_id=0, has_side_effects=True),
        name="start_gather",
    )(payload, w_qkv, w_out, q_side, beta_side, out_side)


def feed_kernel(
    cot, gate_t, down, g_side, u_side, f_side, everyone, wg, wu, wd, send, recv, local
):
    s, partner, right, left, far = seq_places()
    f, _, _ = plane_places()
    greet([partner, right, left], all_plane())
    line = Line(send, recv, local)
    scatters = [
        Scatter(line, (source,), lambda t: block_of(gate_t, t), lambda t, j, o=o: block_of(o, t))
        for source, o in ((s, wg), (s + 8, wu))
    ]
    for item in scatters:
        item.start()
    ring = RingGather(line, cot, everyone)
    ring.start()
    share = wd.shape[0]
    mine = line.local(down.at[pl.ds(s * share, share), :], block_of(wd, f))
    last = pl.ds(wd.shape[1] - SIDE, SIDE)
    sides = [
        line.local(side, o.at[:, last]) for side, o in ((g_side, wg), (u_side, wu), (f_side, wd))
    ]
    gathers = [PlaneGather(line, columns_place(o)) for o in (wg, wu, wd)]
    for item, gather in zip(scatters, gathers):
        item.arrive()
        gather.first()
    mine.wait()
    gathers[2].first()
    ring.middle()
    for gather in gathers:
        gather.second()
    ring.finish()
    for item in scatters + gathers:
        item.finish()
    for copy in sides:
        copy.wait()


def feed_gather(cot, gate_t, down, g_side, u_side, f_side):
    seq, wide = lax.axis_size("seq"), cot.shape[1]
    copies = RING_COPIES + 2 * Scatter.COPIES + 3 * PlaneGather.COPIES
    weight = jax.ShapeDtypeStruct((g_side.shape[0], wide), BF16)
    return pl.pallas_call(
        feed_kernel,
        out_shape=(jax.ShapeDtypeStruct((seq,) + cot.shape, BF16), weight, weight, weight),
        in_specs=[ANY] * 6,
        out_specs=(ANY,) * 4,
        scratch_shapes=sems(copies, 10),
        compiler_params=pltpu.CompilerParams(collective_id=1, has_side_effects=True),
        name="feed_gather",
    )(cot, gate_t, down, g_side, u_side, f_side)


ADD_ROWS = 16


def add_rows(dst, sources, first, count):
    def step(i, carry):
        rows = pl.ds(pl.multiple_of(first + i * ADD_ROWS, ADD_ROWS), ADD_ROWS)
        total = None
        for source, offset in sources:
            at = pl.ds(pl.multiple_of(first - offset + i * ADD_ROWS, ADD_ROWS), ADD_ROWS)
            item = source[at, :].astype(F32)
            total = item if total is None else total + item
        dst[rows, :] = total.astype(dst.dtype)
        return carry

    lax.fori_loop(0, count // ADD_ROWS, step, 0)


class RingSum:
    COPIES = 10

    def __init__(self, line, partial, buffers):
        self.line, self.partial = line, partial
        self.own, self.stage, self.relay, self.away, self.back = buffers
        self.rows = partial.shape[1]
        self.half = self.rows // 2
        self.low, self.high = pl.ds(0, self.half), pl.ds(self.half, self.half)

    def start(self):
        s, partner, right, left, far = seq_places()
        twin = lambda p: p + partner - s
        self.near, self.kept = [], []
        for k, p in enumerate((far, right, left, s)):
            self.near.append(
                self.line.send(self.partial.at[twin(p)], self.stage.at[k], {"seq": partner})
            )
            self.kept.append(self.line.local(self.partial.at[p], self.own.at[k]))

    def ready(self, k):
        self.near[k].wait_recv()
        self.kept[k].wait()

    def go(self, src, dst, peer):
        return self.line.send(src, dst, {"seq": peer})

    def middle(self):
        s, partner, right, left, far = seq_places()
        half = self.half
        pair = lambda k: [(self.own.at[k], 0), (self.stage.at[k], 0)]
        away, relay, back = self.away, self.relay, self.back
        self.ready(0)
        add_rows(away.at[0], pair(0), 0, half)
        self.r0 = self.go(away.at[0, self.low], relay.at[0], right)
        add_rows(away.at[0], pair(0), half, half)
        self.r1 = self.go(away.at[0, self.high], relay.at[1], left)
        self.ready(1)
        add_rows(away.at[1], pair(1), half, half)
        self.s0 = self.go(away.at[1, self.high], back.at[0, self.high], right)
        self.ready(2)
        add_rows(away.at[2], pair(2), 0, half)
        self.s1 = self.go(away.at[2, self.low], back.at[1, self.low], left)

    def last(self):
        s, partner, right, left, far = seq_places()
        half = self.half
        pair = lambda k: [(self.own.at[k], 0), (self.stage.at[k], 0)]
        away, relay, back = self.away, self.relay, self.back
        self.r0.wait_recv()
        add_rows(away.at[1], pair(1) + [(relay.at[0], 0)], 0, half)
        self.s2 = self.go(away.at[1, self.low], back.at[0, self.low], right)
        self.r1.wait_recv()
        add_rows(away.at[2], pair(2) + [(relay.at[1], half)], half, half)
        self.s3 = self.go(away.at[2, self.high], back.at[1, self.high], left)

    def finish(self, total):
        self.ready(3)
        for copy in (self.s0, self.s1, self.s2, self.s3):
            copy.wait_recv()
        add_rows(
            total,
            [(self.own.at[3], 0), (self.stage.at[3], 0), (self.back.at[0], 0), (self.back.at[1], 0)],
            0, self.rows,
        )
        for copy in self.near + [self.r0, self.r1, self.s0, self.s1, self.s2, self.s3]:
            copy.wait_send()


def sum_buffers(rows, width):
    return [
        pltpu.VMEM((4, rows, width), BF16),
        pltpu.VMEM((4, rows, width), BF16),
        pltpu.VMEM((2, rows // 2, width), BF16),
        pltpu.VMEM((3, rows, width), BF16),
        pltpu.VMEM((2, rows, width), BF16),
    ]


MID_ROWS = 32


def by_rows(rows, step):
    def run(i, carry):
        step(pl.ds(pl.multiple_of(i * MID_ROWS, MID_ROWS), MID_ROWS))
        return carry

    lax.fori_loop(0, rows // MID_ROWS, run, 0)


def norm_back_rows(values, gain, grad):
    scale = lax.rsqrt(jnp.mean(values * values, axis=-1, keepdims=True) + 1e-05)
    weighted = grad * gain
    return scale * weighted - values * (
        scale * scale * scale * jnp.mean(weighted * values, axis=-1, keepdims=True)
    )


def branch_kernel(
    partial, tokens, up, gain, down, middle, everyone,
    payload, total, own, stage, relay, away, back, send, recv, local,
):
    s, partner, right, left, far = seq_places()
    greet([partner, right, left], [])
    line = Line(send, recv, local)
    ring = RingSum(line, partial, (own, stage, relay, away, back))
    ring.start()
    ring.middle()
    ring.last()
    ring.finish(total)
    width = tokens.shape[1]

    def step(rows):
        inner = total[rows, width:].astype(BF16)
        value = tokens[rows, :].astype(F32) + (total[rows, :width] + mm(inner, up[...]))
        middle[rows, :] = value
        scale = lax.rsqrt(jnp.mean(value * value, axis=-1, keepdims=True) + 1e-05)
        normed = (value * scale * gain[...]).astype(BF16)
        payload[rows, :width] = normed
        payload[rows, width:] = (inner.astype(F32) + mm_nt(normed, down[...])).astype(BF16)

    by_rows(tokens.shape[0], step)
    gather = RingGather(line, payload, everyone)
    gather.start()
    gather.middle()
    gather.finish()


def back_kernel(
    partial, cot, values, down, gain, up, grad_middle, everyone,
    payload, total, own, stage, relay, away, back, send, recv, local,
):
    s, partner, right, left, far = seq_places()
    greet([partner, right, left], [])
    line = Line(send, recv, local)
    ring = RingSum(line, partial, (own, stage, relay, away, back))
    ring.start()
    ring.middle()
    ring.last()
    ring.finish(total)
    width = cot.shape[1]

    def step(rows):
        inner = total[rows, width:].astype(BF16)
        grad = total[rows, :width] + mm(inner, down[...])
        result = cot[rows, :].astype(F32) + norm_back_rows(values[rows, :], gain[...], grad)
        grad_middle[rows, :] = result
        low = result.astype(BF16)
        payload[rows, :width] = low
        payload[rows, width:] = (inner.astype(F32) + mm_nt(low, up[...])).astype(BF16)

    by_rows(cot.shape[0], step)
    gather = RingGather(line, payload, everyone)
    gather.start()
    gather.middle()
    gather.finish()


def sum_and_gather(kernel, cid, name, partial, operands):
    seq, rows, wide = partial.shape
    return pl.pallas_call(
        kernel,
        out_shape=(
            jax.ShapeDtypeStruct((rows, wide - SIDE), F32),
            jax.ShapeDtypeStruct((seq, rows, wide), BF16),
        ),
        in_specs=[ANY] + [VMEM] * len(operands),
        out_specs=(VMEM, ANY),
        scratch_shapes=[pltpu.VMEM((rows, wide), BF16), pltpu.VMEM((rows, wide), F32)]
        + sum_buffers(rows, wide)
        + sems(RingSum.COPIES + RING_COPIES, 5),
        compiler_params=pltpu.CompilerParams(
            collective_id=cid, has_side_effects=True, vmem_limit_bytes=48 << 20
        ),
        name=name,
    )(partial, *operands)


def layer_kernel(
    partial, values, up, layer_out, inner_out,
    total, own, stage, relay, away, back, send, recv, local,
):
    s, partner, right, left, far = seq_places()
    greet([partner, right, left], [])
    line = Line(send, recv, local)
    ring = RingSum(line, partial, (own, stage, relay, away, back))
    ring.start()
    ring.middle()
    ring.last()
    ring.finish(total)
    width = values.shape[1]

    def step(rows):
        inner = total[rows, width:].astype(BF16)
        inner_out[rows, :] = inner
        layer_out[rows, :] = (
            values[rows, :] + (total[rows, :width] + mm(inner, up[...]))
        ).astype(BF16)

    by_rows(values.shape[0], step)


def input_kernel(
    partial, tokens, grad_middle, down, gain, input_grad, inner_out,
    total, own, stage, relay, away, back, send, recv, local,
):
    s, partner, right, left, far = seq_places()
    greet([partner, right, left], [])
    line = Line(send, recv, local)
    ring = RingSum(line, partial, (own, stage, relay, away, back))
    ring.start()
    ring.middle()
    ring.last()
    ring.finish(total)
    width = tokens.shape[1]

    def step(rows):
        inner = total[rows, width:].astype(BF16)
        inner_out[rows, :] = inner
        grad = total[rows, :width] + mm(inner, down[...])
        input_grad[rows, :] = (
            grad_middle[rows, :]
            + norm_back_rows(tokens[rows, :].astype(F32), gain[...], grad)
        ).astype(BF16)

    by_rows(tokens.shape[0], step)


def sum_only(kernel, cid, name, partial, operands):
    seq, rows, wide = partial.shape
    return pl.pallas_call(
        kernel,
        out_shape=(
            jax.ShapeDtypeStruct((rows, wide - SIDE), BF16),
            jax.ShapeDtypeStruct((rows, SIDE), BF16),
        ),
        in_specs=[ANY] + [VMEM] * len(operands),
        out_specs=(VMEM, VMEM),
        scratch_shapes=[pltpu.VMEM((rows, wide), F32)]
        + sum_buffers(rows, wide)
        + sems(RingSum.COPIES, 4),
        compiler_params=pltpu.CompilerParams(
            collective_id=cid, has_side_effects=True, vmem_limit_bytes=48 << 20
        ),
        name=name,
    )(partial, *operands)


BOTH = ("fsdp", "seq")


def rms_scale(values, gain):
    return values * lax.rsqrt(jnp.mean(values * values, axis=-1, keepdims=True) + 1e-05) * gain


def norm_back(values, gain, grad):
    scale = lax.rsqrt(jnp.mean(values * values, axis=-1, keepdims=True) + 1e-05)
    weighted = grad * gain
    return scale * weighted - values * scale * scale * scale * jnp.mean(
        weighted * values, axis=-1, keepdims=True
    )


def dot(a, b):
    return jnp.dot(a, b, preferred_element_type=F32)


def dot_nt(a, b):
    return lax.dot_general(a, b, (((1,), (1,)), ((), ())), preferred_element_type=F32)


def dot_tn(a, b):
    return lax.dot_general(a, b, (((0,), (0,)), ((), ())), preferred_element_type=F32)


def body(
    tokens,
    segments,
    adapter_index,
    attn_gain,
    w_qkv,
    w_beta,
    conv_weight,
    head_gain,
    w_out,
    ffn_gain,
    w_gateup,
    w_down,
    qkv_down,
    qkv_up,
    mixout_down,
    mixout_up,
    gateup_down,
    gateup_up,
    ffnout_down,
    ffnout_up,
    cotangent,
):
    seq = lax.axis_size("seq")
    s = lax.axis_index("seq")
    width = tokens.shape[1]
    heads = w_beta.shape[1] // seq
    rank = qkv_down.shape[2]
    count = qkv_down.shape[0]
    hidden_width = w_down.shape[0]
    share = hidden_width // seq
    columns = heads * 3 * CH
    outs = heads * CH
    which = adapter_index[0]
    docs = segments[0]
    length = docs.shape[0]

    def pick(array):
        return lax.dynamic_index_in_dim(array, which, 0, keepdims=False)

    def mine(array, size, axis):
        return lax.dynamic_slice_in_dim(array, s * size, size, axis)

    def lanes(array, first=0):
        return jnp.pad(array, ((0, 0), (first, SIDE - first - array.shape[1])))

    def lines(array, first=0):
        return jnp.pad(array, ((first, SIDE - first - array.shape[0]), (0, 0)))

    q_down, q_up = pick(qkv_down), mine(pick(qkv_up), columns, 1)
    m_down, m_up = mine(pick(mixout_down), outs, 0), pick(mixout_up)
    g_down, g_up = pick(gateup_down), pick(gateup_up)
    gate_up = mine(g_up[:, :hidden_width], share, 1)
    upper_up = mine(g_up[:, hidden_width:], share, 1)
    f_down, f_up = mine(pick(ffnout_down), share, 0), pick(ffnout_up)
    beta_w = mine(w_beta, heads, 1)

    base = tokens.astype(F32)
    normed_own = rms_scale(base, attn_gain).astype(BF16)
    payload = jnp.concatenate([normed_own, dot(normed_own, lanes(q_down, rank)).astype(BF16)], axis=1)
    normed, wq, wo = start_gather(
        payload, w_qkv, w_out,
        jnp.pad(q_up, ((rank, SIDE - 2 * rank), (0, SIDE))), lanes(beta_w), lanes(m_down),
    )
    normed = normed.reshape(length, -1)
    joined = dot(normed, wq).astype(BF16)

    ids = jnp.pad(docs, (PAD, PAD), constant_values=-1)
    dcol = jnp.broadcast_to(ids[:, None], (length + 2 * PAD, CH))
    drow = docs.reshape(length // CH, CH)
    taps = mine(conv_weight, heads, 1).reshape(-1, columns)
    fixed = (joined, dcol, drow, taps, head_gain[None])
    mixed, o_kept, t_kept, d_kept, s_kept = mixer_fwd(*fixed)

    payload = jnp.concatenate([cotangent, dot_nt(cotangent, lines(f_up)).astype(BF16)], axis=1)
    cot, wg, wu, wd = feed_gather(
        payload, w_gateup.T, w_down,
        lanes(gate_up.T, rank), lanes(upper_up.T, rank), lanes(f_down),
    )
    cot = cot.reshape(length, -1)

    blocks = lambda partial: partial.astype(BF16).reshape(seq, -1, partial.shape[1])
    middle, normed2 = sum_and_gather(
        branch_kernel, 2, "branch", blocks(dot(mixed, wo)),
        (tokens, lines(m_up), ffn_gain[None], lines(g_down.T, rank)),
    )
    normed2 = normed2.reshape(length, -1)

    gate = dot_nt(normed2, wg)
    upper = dot_nt(normed2, wu)
    sigma = jax.nn.sigmoid(gate)
    hidden = (gate * sigma * upper).astype(BF16)
    layer_out, f_inner = sum_only(
        layer_kernel, 3, "layer", blocks(dot(hidden, wd)), (middle, lines(f_up))
    )

    grad_hidden = dot_nt(cot, wd)
    grad_gate = (grad_hidden * upper * sigma * (1.0 + gate * (1.0 - sigma))).astype(BF16)
    grad_upper = (grad_hidden * gate * sigma).astype(BF16)
    grad_middle, branch = sum_and_gather(
        back_kernel, 4, "back", blocks(dot(grad_gate, wg) + dot(grad_upper, wu)),
        (cotangent, middle, lines(g_down.T, rank), ffn_gain[None], lines(m_up)),
    )
    branch = branch.reshape(length, -1)

    grad_mixed = dot_nt(branch, wo).astype(BF16)
    grad_joined = mixer_bwd(*fixed, grad_mixed, o_kept, t_kept, d_kept, s_kept)
    input_grad, q_dinner = sum_only(
        input_kernel, 5, "input", blocks(dot_nt(grad_joined, wq)),
        (tokens, grad_middle, lines(q_down.T, rank), attn_gain[None]),
    )

    inner = lax.all_gather(
        jnp.concatenate([f_inner[:, :rank], q_dinner[:, rank : 2 * rank]], axis=1),
        "seq", axis=0, tiled=True,
    )
    low = lambda rows: rows[:, width : width + rank]
    high = lambda rows: rows[:, width + rank : width + 2 * rank]
    part = lambda rows: mine(rows, width // seq, 1)
    early = (
        dot_tn(high(normed2), grad_gate),
        dot_tn(high(normed2), grad_upper),
        dot_tn(low(cot), hidden),
        dot_tn(low(branch), mixed),
        dot_tn(low(normed2), part(branch)),
        dot_tn(high(branch), part(normed2)),
    )
    late = (
        dot_tn(high(normed), grad_joined[:, :columns]),
        dot_tn(inner[:, :rank], part(cot)),
        dot_tn(inner[:, rank:], part(normed)),
    )

    match = (lax.all_gather(adapter_index, "fsdp", axis=0, tiled=True)[None, :] == jnp.arange(count, dtype=jnp.int32)[:, None]).astype(F32)

    def total(pieces):
        sizes = [p.shape[1] for p in pieces]
        piece = jnp.concatenate(pieces, axis=1).astype(BF16)
        plane = lax.all_gather(piece, "fsdp", axis=0)
        by_adapter = jnp.einsum("af,frn->arn", match, plane.astype(F32)).astype(BF16)
        whole = lax.all_gather(by_adapter, "seq", axis=0)
        result, at = [], 0
        for size in sizes:
            item = whole[..., at : at + size].astype(F32)
            result.append(jnp.transpose(item, (1, 2, 0, 3)).reshape(count, rank, seq * size))
            at += size
        return result

    gate_g, upper_g, ffdown_g, mixdown_g, mixup_g, gudown_g = total(early)
    qkvup_g, ffup_g, qkvdown_g = total(late)
    flip = lambda v: jnp.swapaxes(v, 1, 2)
    return (
        layer_out,
        input_grad,
        flip(qkvdown_g),
        qkvup_g,
        flip(mixdown_g),
        mixup_g,
        flip(gudown_g),
        jnp.concatenate([gate_g, upper_g], axis=2),
        flip(ffdown_g),
        ffup_g,
    )


def solution(mesh):
    tokens, columns = P(BOTH, None), P(None, "fsdp")
    placed = (
        tokens, P("fsdp", None), P("fsdp"), P(), columns, P(), P(), P(), columns, P(), columns,
        columns, P(), P(), P(), P(), P(), P(), P(), P(), tokens,
    )
    return jax.shard_map(
        body,
        mesh=mesh,
        in_specs=placed,
        out_specs=(tokens, tokens) + (P(),) * 8,
        check_vma=False,
    )
```

```python
import functools
import jax
import jax.numpy as jnp
from jax import lax
from jax.experimental import pallas as pl
from jax.experimental.pallas import tpu as pltpu
from jax.sharding import PartitionSpec as P

F32 = jnp.float32
BF16 = jnp.bfloat16
CH = 128
PAD = 16


def mm(a, b):
    return jnp.dot(a.astype(BF16), b.astype(BF16), preferred_element_type=F32)


def mm_nt(a, b):
    return lax.dot_general(
        a.astype(BF16), b.astype(BF16), (((1,), (1,)), ((), ())), preferred_element_type=F32
    )


def mm_tn(a, b):
    return lax.dot_general(
        a.astype(BF16), b.astype(BF16), (((0,), (0,)), ((), ())), preferred_element_type=F32
    )


def split(a):
    high = a.astype(BF16)
    return high, (a - high.astype(F32)).astype(BF16)


def mm_fine(a, b):
    ah, al = split(a)
    bh, bl = split(b)
    return jnp.dot(
        jnp.concatenate([ah, al, ah], axis=1),
        jnp.concatenate([bh, bh, bl], axis=0),
        preferred_element_type=F32,
    )


def unit_lower_inverse(lower, row, col, product):
    near = jnp.where((row >> 3) == (col >> 3), lower, 0.0)
    eye = (row == col).astype(F32)
    second = product(near, near)
    fourth = product(second, second)
    inverse = eye - near + second - product(near, second)
    inverse = inverse + product(inverse, fourth)
    for bits in (3, 4, 5, 6):
        joining = ((row >> (bits + 1)) == (col >> (bits + 1))) & ((row >> bits) != (col >> bits))
        below = jnp.where(joining, lower, 0.0)
        inverse = inverse - product(inverse, product(below, inverse))
    return inverse


def sigmoid(v):
    return 1.0 / (1.0 + jnp.exp(-v))


def chunk_masks(c, dcol, drow):
    start = pl.multiple_of(c * CH, CH)
    docs = dcol[pl.ds(start + PAD, CH), :]
    before = dcol[pl.ds(start + PAD - 8, 8), :][7:8, :]
    last = docs[CH - 1 :, :]
    same = docs == drow[pl.ds(c, 1), :]
    live = (docs == before).astype(F32)
    tail = (docs == last).astype(F32)
    live_last = (last == before).astype(F32)
    return docs, same, live, tail, live_last


def conv_chunk(c, joined, dcol, taps, docs):
    start = pl.multiple_of(c * CH, CH)
    window = joined[pl.ds(start, CH + PAD), : taps.shape[1]].astype(F32)
    ids = dcol[pl.ds(start, CH + PAD), :]
    total = window[PAD:, :] * taps[3:4, :]
    for lag in (1, 2, 3):
        keep = (ids[PAD - lag : PAD - lag + CH, :] == docs).astype(F32)
        keep = jnp.concatenate([keep] * (taps.shape[1] // CH), axis=1)
        total = total + window[PAD - lag : PAD - lag + CH, :] * keep * taps[3 - lag : 4 - lag, :]
    return total


def raw_chunk(c, joined, taps):
    rows = pl.ds(pl.multiple_of(c * CH + PAD, PAD), CH)
    return joined[rows, taps.shape[1] :].astype(F32)


def normal_parts(act):
    query, keys, values = act[:, :CH], act[:, CH : 2 * CH], act[:, 2 * CH :]
    q_scale = lax.rsqrt(jnp.sum(query * query, axis=-1, keepdims=True) + 1e-06)
    k_scale = lax.rsqrt(jnp.sum(keys * keys, axis=-1, keepdims=True) + 1e-06)
    return query * q_scale * CH**-0.5, keys * k_scale, values, q_scale, k_scale


def mixer_fwd_kernel(
    heads, chunks, normed, weight, cot, gate_t, w_out, g_side, out_side,
    dcol, drow, taps, gain,
    mixed, o_out, t_out, d_out, s_out, partial, joined_out, everyone, wg, upper, wo,
    joined, rows_v, weight_v, wo_v, q_s, k_s, u_s, w_s, p_s, sem, send, recv, local,
):
    loads = [
        pltpu.make_async_copy(weight, weight_v, sem.at[0]),
        pltpu.make_async_copy(normed, rows_v, sem.at[1]),
    ]
    for copy in loads:
        copy.start()
    greet(ring_peers(), all_plane())
    feed = Feed(
        Line(send, recv, local), cot, gate_t, w_out, (out_side, g_side), everyone, wg, wo, upper
    )
    feed.start()
    joined[pl.ds(0, PAD), :] = jnp.zeros((PAD, joined.shape[1]), BF16)
    for copy in loads:
        copy.wait()
    batch = 2 * CH

    def project(step):
        rows = pl.multiple_of(step * batch, batch)
        joined[pl.ds(rows + PAD, batch), :] = mm(
            rows_v[pl.ds(rows, batch), :], weight_v[...]
        ).astype(BF16)

    project(0)
    row = lax.broadcasted_iota(jnp.int32, (CH, CH), 0)
    col = lax.broadcasted_iota(jnp.int32, (CH, CH), 1)

    def prepare(c, h, docs, same, live, act, raws):
        start = pl.multiple_of(c * CH, CH)
        rows = pl.ds(start, CH)
        query, keys, values, _, _ = normal_parts(act[:, h * 3 * CH : (h + 1) * 3 * CH])
        beta = sigmoid(raws[:, h : h + 1])
        inner = mm_nt(keys, keys)
        lower = jnp.where(same & (row > col), inner * beta, 0.0)
        inverse = unit_lower_inverse(lower, row, col, mm_fine)
        t_out[h, rows, :] = inverse
        both = mm(inverse, jnp.concatenate([values * beta, keys * (beta * live)], axis=1))
        u_s[h, rows, :] = both[:, :CH]
        w_s[h, rows, :] = both[:, CH:].astype(BF16)
        scores = jnp.where(same & (row >= col), mm_nt(query, keys), 0.0)
        p_s[h, rows, :] = scores.astype(BF16)
        q_s[h, rows, :] = (query * live).astype(BF16)
        k_s[h, rows, :] = keys

    def first(step, carry):
        feed.stage(step)
        parts = []
        for part in range(2):
            c = step * 2 + part
            docs, same, live, tail, live_last = chunk_masks(c, dcol, drow)
            conv = conv_chunk(c, joined, dcol, taps, docs)
            act = conv * sigmoid(conv)
            parts.append((c, docs, same, live, act, raw_chunk(c, joined, taps)))
        project(jnp.minimum(step + 1, chunks // 2 - 1))
        for c, docs, same, live, act, raws in parts:
            for h in range(heads):
                prepare(c, h, docs, same, live, act, raws)
        return carry

    lax.fori_loop(0, chunks // 2, first, 0)
    kept = pltpu.make_async_copy(joined.at[pl.ds(PAD, chunks * CH), :], joined_out, sem.at[0])
    kept.start()
    feed.third()

    def second(c, states):
        rows = pl.ds(pl.multiple_of(c * CH, CH), CH)
        docs, same, live, tail, live_last = chunk_masks(c, dcol, drow)
        after = []
        for h in range(heads):
            state = states[h]
            s_out[h, rows, :] = state
            update = u_s[h, rows, :] - mm(w_s[h, rows, :], state)
            d_out[h, rows, :] = update
            after.append(state * live_last + mm_tn(k_s[h, rows, :] * tail, update))
        return tuple(after)

    zero = jnp.zeros((CH, CH), F32)
    lax.fori_loop(0, chunks, second, (zero,) * heads)
    feed.fourth()
    last = pltpu.make_async_copy(wo, wo_v, sem.at[1])
    last.start()
    last.wait()

    def third(c, carry):
        rows = pl.ds(pl.multiple_of(c * CH, CH), CH)
        for h in range(heads):
            out = mm(
                jnp.concatenate([q_s[h, rows, :], p_s[h, rows, :]], axis=1),
                jnp.concatenate(
                    [s_out[h, rows, :].astype(BF16), d_out[h, rows, :].astype(BF16)], axis=0
                ),
            )
            o_out[h, rows, :] = out
            scale = lax.rsqrt(jnp.mean(out * out, axis=-1, keepdims=True) + 1e-05)
            mixed[rows, h * CH : (h + 1) * CH] = (out * scale * gain[...]).astype(BF16)
        partial[c] = mm(mixed[rows, :], wo_v[...]).astype(BF16)
        return carry

    lax.fori_loop(0, chunks, third, 0)
    kept.wait()
    feed.finish()


def mixer_fwd(
    normed, weight, cot, gate_t, w_out, g_side, out_side, dcol, drow, taps, gain
):
    tokens, across = normed.shape
    wide = weight.shape[1]
    heads = wide // (3 * CH)
    chunks = tokens // CH
    seq = lax.axis_size("seq")
    square = jax.ShapeDtypeStruct((heads, tokens, CH), F32)
    out = lambda *shape: jax.ShapeDtypeStruct(shape, BF16)
    share, part = g_side.shape[0], out_side.shape[0]
    return pl.pallas_call(
        functools.partial(mixer_fwd_kernel, heads, chunks),
        out_shape=(
            out(tokens, heads * CH), square, square, square, square,
            out(chunks, CH, across), out(tokens, wide), out(seq, *cot.shape),
            out(share, across), out(share, 128), out(part, across),
        ),
        in_specs=[ANY] * 7 + [VMEM] * 4,
        out_specs=(VMEM,) * 6 + (ANY,) * 5,
        scratch_shapes=[
            pltpu.VMEM((tokens + PAD, wide), BF16),
            pltpu.VMEM((tokens, across), BF16),
            pltpu.VMEM((across, wide), BF16),
            pltpu.VMEM((part, across), BF16),
            pltpu.VMEM((heads, tokens, CH), BF16),
            pltpu.VMEM((heads, tokens, CH), F32),
            pltpu.VMEM((heads, tokens, CH), F32),
            pltpu.VMEM((heads, tokens, CH), BF16),
            pltpu.VMEM((heads, tokens, CH), BF16),
            pltpu.SemaphoreType.DMA((2,)),
        ]
        + sems(Feed.COPIES, Feed.LOCAL),
        compiler_params=comm_params(1, 56),
        name="mixer_fwd",
    )(normed, weight, cot, gate_t, w_out, g_side, out_side, dcol, drow, taps, gain)


def mixer_bwd_kernel(
    heads, chunks, source, partial, early, normed, weight, q_side, values, up,
    dcol, drow, taps, gain, grad, o_in, t_in, d_in, s_in,
    back_partial, up_out, layer_out, inner_out, early_out,
    joined, e_s, f_s, w_s, x_s, ds_s, go_s, dj_s, side_v, weight_v, sem,
    total, own, stage, relay, away, back, early_pieces, early_sum, send, recv, local,
):
    loads = [
        pltpu.make_async_copy(source, joined.at[pl.ds(PAD, source.shape[0]), :], sem.at[0]),
        pltpu.make_async_copy(weight, weight_v, sem.at[1]),
        pltpu.make_async_copy(
            normed.at[:, pl.ds(normed.shape[1] - SIDE, SIDE)], side_v, sem.at[2]
        ),
    ]
    for copy in loads:
        copy.start()
    greet(ring_peers(), line_peers())
    line = Line(send, recv, local)
    ring = RingSum(line, partial, (own, stage, relay, away, back))
    sums = EarlySum(line, early, early_pieces, early_sum, early_out)
    ring.start()
    sums.start()
    joined[pl.ds(0, PAD), :] = jnp.zeros((PAD, joined.shape[1]), BF16)
    dj_s[pl.ds((chunks - 1) * CH, CH), :] = jnp.zeros((CH, dj_s.shape[1]), BF16)
    for copy in loads:
        copy.wait()
    row = lax.broadcasted_iota(jnp.int32, (CH, CH), 0)
    col = lax.broadcasted_iota(jnp.int32, (CH, CH), 1)
    width = 3 * CH

    def revive(c):
        docs, same, live, tail, live_last = chunk_masks(c, dcol, drow)
        conv = conv_chunk(c, joined, dcol, taps, docs)
        raws = raw_chunk(c, joined, taps)
        return docs, same, live, tail, live_last, conv, raws

    def first(c, carry):
        pl.when(c == chunks // 2)(sums.plane.second)
        docs, same, live, tail, live_last, conv, raws = revive(c)
        act = conv * sigmoid(conv)
        rows = pl.ds(pl.multiple_of(c * CH, CH), CH)
        for h in range(heads):
            query, keys, values, _, _ = normal_parts(act[:, h * width : (h + 1) * width])
            beta = sigmoid(raws[:, h : h + 1])
            out = o_in[h, rows, :]
            weighted = grad[rows, h * CH : (h + 1) * CH].astype(F32) * gain[...]
            scale = lax.rsqrt(jnp.mean(out * out, axis=-1, keepdims=True) + 1e-05)
            grad_o = scale * weighted - out * (
                scale * scale * scale * jnp.mean(weighted * out, axis=-1, keepdims=True)
            )
            go_s[h, rows, :] = grad_o
            scores = jnp.where(same & (row >= col), mm_nt(query, keys), 0.0)
            ef = mm_tn(jnp.concatenate([scores, query * live], axis=1), grad_o)
            e_s[h, rows, :] = ef[:CH]
            f_s[h, rows, :] = ef[CH:]
            w_s[h, rows, :] = mm(t_in[h, rows, :], keys * (beta * live)).astype(BF16)
            x_s[h, rows, :] = keys * tail
        return carry

    lax.fori_loop(0, chunks, first, 0)
    ring.middle()
    sums.plane.third()

    def second(step, states):
        c = chunks - 1 - step
        rows = pl.ds(pl.multiple_of(c * CH, CH), CH)
        docs, same, live, tail, live_last = chunk_masks(c, dcol, drow)
        before = []
        for h in range(heads):
            state = states[h]
            ds_s[h, rows, :] = state
            grad_update = e_s[h, rows, :] + mm(x_s[h, rows, :], state)
            x_s[h, rows, :] = grad_update
            before.append(
                state * live_last + f_s[h, rows, :] - mm_tn(w_s[h, rows, :], grad_update)
            )
        return tuple(before)

    zero = jnp.zeros((CH, CH), F32)
    lax.fori_loop(0, chunks, second, (zero,) * heads)

    sums.plane.fourth()

    def project(c):
        rows = pl.ds(pl.multiple_of(c * CH, CH), CH)
        grads = dj_s[rows, :]
        back_partial[c] = mm_nt(grads, weight_v[...]).astype(BF16)

    def third(step, after):
        c = chunks - 1 - step
        pl.when(step == chunks // 4)(ring.last)
        pl.when(step == chunks // 4)(sums.add)
        pl.when(step == chunks - 1)(sums.ring.middle)
        project(jnp.minimum(c + 1, chunks - 1))
        docs, same, live, tail, live_last, conv, raws = revive(c)
        gate = sigmoid(conv)
        act = conv * gate
        slope = gate * (1.0 + conv * (1.0 - gate))
        rows = pl.ds(pl.multiple_of(c * CH, CH), CH)
        lane = lax.broadcasted_iota(jnp.int32, (CH, CH), 1)
        grad_raw = jnp.zeros((CH, CH), F32)
        grads = []
        for h in range(heads):
            part = act[:, h * width : (h + 1) * width]
            query, keys, values, q_scale, k_scale = normal_parts(part)
            beta = sigmoid(raws[:, h : h + 1])
            state, update, state_grad = s_in[h, rows, :], d_in[h, rows, :], ds_s[h, rows, :]
            grad_o = go_s[h, rows, :]
            grad_target = mm_tn(t_in[h, rows, :], x_s[h, rows, :])
            pair = mm_nt(jnp.concatenate([grad_target, grad_o], axis=0), update)
            grad_lower = jnp.where(same & (row > col), -pair[:CH], 0.0)
            grad_scores = jnp.where(same & (row >= col), pair[CH:], 0.0)
            inner = mm_nt(keys, keys)
            recalled = mm(keys, state)
            grad_beta = jnp.sum(
                grad_lower * inner + grad_target * (values - live * recalled),
                axis=-1,
                keepdims=True,
            )
            grad_inner = grad_lower * beta
            back = mm_nt(
                jnp.concatenate([grad_o * live, -grad_target * (beta * live)], axis=0), state
            )
            grad_query = back[:CH] + mm(grad_scores, keys)
            grad_keys = (
                back[CH:]
                + mm_tn(
                    jnp.concatenate([grad_scores, grad_inner], axis=0),
                    jnp.concatenate([query, keys], axis=0),
                )
                + mm(grad_inner, keys)
                + mm_nt(update * tail, state_grad)
            )
            grad_values = grad_target * beta
            raw_q, raw_k = part[:, :CH], part[:, CH : 2 * CH]
            grad_query = grad_query * CH**-0.5
            grad_q = q_scale * grad_query - raw_q * (
                q_scale * q_scale * q_scale * jnp.sum(grad_query * raw_q, axis=-1, keepdims=True)
            )
            grad_k = k_scale * grad_keys - raw_k * (
                k_scale * k_scale * k_scale * jnp.sum(grad_keys * raw_k, axis=-1, keepdims=True)
            )
            grads += [grad_q, grad_k, grad_values]
            grad_raw = jnp.where(lane == h, grad_beta * beta * (1.0 - beta), grad_raw)
        dj_s[rows, heads * width :] = grad_raw.astype(BF16)
        grads = jnp.concatenate(grads, axis=1) * slope
        window = jnp.concatenate([grads, after], axis=0)
        ids = dcol[pl.ds(pl.multiple_of(c * CH + PAD, PAD), CH + PAD), :]
        total_ = grads * taps[3:4, :]
        for lag in (1, 2, 3):
            keep = (ids[lag : lag + CH] == ids[:CH]).astype(F32)
            keep = jnp.concatenate([keep] * (heads * 3), axis=1)
            total_ = total_ + window[lag : lag + CH] * keep * taps[3 - lag : 4 - lag, :]
        dj_s[rows, : heads * width] = total_.astype(BF16)
        return grads[:8]

    lax.fori_loop(0, chunks, third, jnp.zeros((8, heads * width), F32))
    project(0)
    up_out[...] = mm_tn(side_v[...], dj_s[:, : heads * width])[
        up_out.shape[0] : 2 * up_out.shape[0]
    ].astype(BF16)
    sums.ring.finish()
    ring.finish(total)
    across = values.shape[1]
    rank, n = inner_out.shape[1:]
    q_inner = mm_nt(q_side[...], dj_s[...])[rank : 2 * rank].astype(BF16)
    f_inner = total[:, across:].T[:rank].astype(BF16)
    inner_out[0] = q_inner[:, :n]
    rest = 2 * n - q_inner.shape[1] - f_inner.shape[1]
    inner_out[1] = jnp.concatenate(
        [q_inner[:, n:], f_inner, jnp.zeros((rank, rest), BF16)], axis=1
    )

    def step(rows):
        inner = total[rows, across:].astype(BF16)
        layer_out[rows, :] = (
            values[rows, :] + (total[rows, :across] + mm(inner, up[...]))
        ).astype(BF16)

    by_rows(values.shape[0], step)


def mixer_bwd(
    joined, partial, early, normed, weight, q_side, values, up, dcol, drow, taps, gain,
    grad, o, t, d, s,
):
    tokens, wide = joined.shape
    heads = wide // (3 * CH)
    chunks = tokens // CH
    square = (heads, tokens, CH)
    rows, across = values.shape
    seq, rank = lax.axis_size("seq"), early.shape[2]
    out = lambda *shape: jax.ShapeDtypeStruct(shape, BF16)
    return pl.pallas_call(
        functools.partial(mixer_bwd_kernel, heads, chunks),
        out_shape=(
            out(chunks, CH, across + SIDE), out(rank, heads * 3 * CH),
            out(rows, across), out(2, rank, 640), out(seq, *early.shape[1:]),
        ),
        in_specs=[ANY] * 5 + [VMEM] * 12,
        out_specs=(VMEM,) * 4 + (ANY,),
        scratch_shapes=[
            pltpu.VMEM((tokens + PAD, wide), BF16),
            pltpu.VMEM(square, F32),
            pltpu.VMEM(square, F32),
            pltpu.VMEM(square, BF16),
            pltpu.VMEM(square, F32),
            pltpu.VMEM(square, F32),
            pltpu.VMEM(square, F32),
            pltpu.VMEM((tokens, wide), BF16),
            pltpu.VMEM((tokens, SIDE), BF16),
            pltpu.VMEM(weight.shape, BF16),
            pltpu.SemaphoreType.DMA((3,)),
            pltpu.VMEM((rows, across + SIDE), F32),
        ]
        + sum_buffers(rows, across + SIDE)
        + [pltpu.VMEM((16,) + early.shape, BF16), pltpu.VMEM(early.shape[1:], BF16)]
        + sems(RingSum.COPIES + EarlySum.COPIES, RingSum.LOCAL + EarlySum.LOCAL),
        compiler_params=comm_params(5, 60),
        name="mixer_bwd",
    )(
        joined, partial, early, normed, weight, q_side, values, up, dcol, drow, taps, gain,
        grad, o, t, d, s,
    )

MESH = pl.DeviceIdType.MESH
SIDE = 128
ANY = pl.BlockSpec(memory_space=pl.ANY)
VMEM = pl.BlockSpec(memory_space=pltpu.VMEM)
SMEM = pl.BlockSpec(memory_space=pltpu.SMEM)


class Line:
    def __init__(self, send_sems, recv_sems, local_sems):
        self.send_sems, self.recv_sems, self.local_sems = send_sems, recv_sems, local_sems
        self.used, self.used_local = 0, 0

    def take(self, copies, local=0):
        at = self.used, self.used_local
        self.used += copies
        self.used_local += local
        return at

    def copy(self, at, src, dst, device):
        return pltpu.make_async_remote_copy(
            src_ref=src, dst_ref=dst, send_sem=self.send_sems.at[at],
            recv_sem=self.recv_sems.at[at], device_id=device, device_id_type=MESH,
        )

    def local(self, at, src, dst):
        return pltpu.make_async_copy(src, dst, self.local_sems.at[at])


def sems(copies, local):
    return [
        pltpu.SemaphoreType.DMA((copies,)),
        pltpu.SemaphoreType.DMA((copies,)),
        pltpu.SemaphoreType.DMA((local,)),
    ]


def seq_places():
    s = lax.axis_index("seq")
    x, core = s // 2, lax.rem(s, 2)
    there = lambda d: lax.rem(x + d, 4) * 2 + core
    return s, x * 2 + 1 - core, there(1), there(3), there(2)


def plane_places():
    f = lax.axis_index("fsdp")
    return f, f // 4, lax.rem(f, 4)


def ring_peers():
    s, partner, right, left, far = seq_places()
    return [partner, right, left]


def all_plane():
    f = lax.axis_index("fsdp")
    return [lax.rem(f + d, 16) for d in range(1, 16)]


def line_peers():
    f, y, z = plane_places()
    return [y * 4 + lax.rem(z + d, 4) for d in (1, 3)] + [
        lax.rem(y + d, 4) * 4 + z for d in (1, 3)
    ]


def greet(seq_peers, plane_peers):
    barrier = pltpu.get_barrier_semaphore()
    for p in seq_peers:
        pl.semaphore_signal(barrier, inc=1, device_id={"seq": p}, device_id_type=MESH)
    for p in plane_peers:
        pl.semaphore_signal(barrier, inc=1, device_id={"fsdp": p}, device_id_type=MESH)
    pl.semaphore_wait(barrier, len(seq_peers) + len(plane_peers))


class RingGather:
    COPIES, LOCAL = 13, 1

    def __init__(self, line, block, out, first=0, rows=None):
        self.line, self.placed, self.out = line, block is None, out
        self.block = out.at[lax.axis_index("seq")] if self.placed else block
        rows = rows or self.block.shape[0]
        half = rows // 2
        self.low, self.high = pl.ds(first, half), pl.ds(first + half, half)
        self.all = pl.ds(first, rows)
        self.at, self.local_at = line.take(self.COPIES, self.LOCAL)

    def mine(self, i, rows, peer):
        s = lax.axis_index("seq")
        return self.line.copy(
            self.at + i, self.block.at[rows], self.out.at[s, rows], {"seq": peer}
        )

    def pass_on(self, i, s, rows, peer):
        ref = self.out.at[s, rows]
        return self.line.copy(self.at + i, ref, ref, {"seq": peer})

    def copy(self, i):
        s, partner, right, left, far = seq_places()
        low, high = self.low, self.high
        if i < 4:
            return self.mine(i, *((low, right), (high, left), (high, right), (low, left))[i])
        if i == 4:
            return self.mine(4, self.all, partner)
        return self.pass_on(
            i,
            *(
                (left, low, right), (left, low, partner), (right, high, left),
                (right, high, partner), (left, high, partner), (right, low, partner),
                (far, low, partner), (far, high, partner),
            )[i - 5],
        )

    def own(self):
        s = lax.axis_index("seq")
        return self.line.local(self.local_at, self.block, self.out.at[s])

    def start(self):
        for i in range(5):
            self.copy(i).start()
        if not self.placed:
            self.own().start()

    def middle(self):
        for arrived, onward in ((0, (5, 6)), (1, (7, 8)), (2, (9,)), (3, (10,))):
            self.copy(arrived).wait_recv()
            for i in onward:
                self.copy(i).start()

    def finish(self):
        self.copy(5).wait_recv()
        self.copy(11).start()
        self.copy(7).wait_recv()
        self.copy(12).start()
        for i in (0, 1, 2, 3, 5, 7):
            self.copy(i).wait_send()
        for i in (4, 6, 8, 9, 10, 11, 12):
            self.copy(i).wait()
        if not self.placed:
            self.own().wait()

    def reach(self, step):
        @pl.when(step == 0)
        def _():
            self.copy(4).wait_recv()

        @pl.when(step == 1)
        def _():
            self.middle()
            self.copy(8).wait_recv()
            self.copy(10).wait_recv()

        @pl.when(step == 2)
        def _():
            self.copy(6).wait_recv()
            self.copy(9).wait_recv()

        @pl.when(step == 3)
        def _():
            self.copy(5).wait_recv()
            self.copy(11).start()
            self.copy(7).wait_recv()
            self.copy(12).start()
            self.copy(11).wait_recv()
            self.copy(12).wait_recv()

    def sent(self):
        for i in range(self.COPIES):
            self.copy(i).wait_send()


class PlaneGather:
    COPIES, LOCAL = 40, 0

    def __init__(self, line, place):
        self.line, self.place = line, place
        self.at, _ = line.take(self.COPIES)

    def by(self, half, along, across):
        f, y, z = plane_places()
        dy, dz = (across, along) if half == 0 else (along, across)
        return lax.rem(y + dy + 4, 4) * 4 + lax.rem(z + dz + 4, 4)

    def send(self, at, ref, peer):
        return self.line.copy(self.at + at, ref, ref, {"fsdp": peer})

    def one(self, half, i):
        ref = self.place(lax.axis_index("fsdp"), half, None)
        return self.send(half * 20 + i, ref, self.by(half, (1, -1)[i], 0))

    def one_on(self, half, i):
        d = (1, -1)[i]
        ref = self.place(self.by(half, -d, 0), half, i)
        return self.send(half * 20 + 2 + i, ref, self.by(half, d, 0))

    def two(self, half, k, i):
        ref = self.place(self.by(half, (0, -1, 1, 2)[k], 0), half, None)
        return self.send(half * 20 + 4 + k * 2 + i, ref, self.by(half, 0, (1, -1)[i]))

    def two_on(self, half, k, i):
        d = (1, -1)[i]
        ref = self.place(self.by(half, (0, -1, 1, 2)[k], -d), half, i)
        return self.send(half * 20 + 12 + k * 2 + i, ref, self.by(half, 0, d))

    def first(self):
        for half in (0, 1):
            for i in (0, 1):
                self.one(half, i).start()

    def second(self):
        for half in (0, 1):
            for i in (0, 1):
                self.two(half, 0, i).start()
        for half in (0, 1):
            for i in (0, 1):
                self.one(half, i).wait_recv()
                self.one_on(half, i).start()
                for j in (0, 1):
                    self.two(half, 1 + i, j).start()

    def third(self):
        for half in (0, 1):
            for i in (0, 1):
                self.one_on(half, i).wait_recv()
            for i in (0, 1):
                self.two(half, 3, i).start()
        for k in range(3):
            for half in (0, 1):
                self.cross(half, k)

    def cross(self, half, k):
        for i in (0, 1):
            self.two(half, k, i).wait_recv()
            self.two_on(half, k, i).start()

    def fourth(self):
        for half in (0, 1):
            self.cross(half, 3)

    def finish(self):
        for half in (0, 1):
            for i in (0, 1):
                self.one(half, i).wait_send()
                self.one_on(half, i).wait_send()
                for k in range(4):
                    self.two(half, k, i).wait_send()
                    self.two_on(half, k, i).wait()


class Scatter:
    COPIES, LOCAL = 17, 2

    def __init__(self, line, sources, source_block, into):
        self.line, self.sources = line, sources
        self.source_block, self.into = source_block, into
        self.at, self.local_at = line.take(self.COPIES, self.LOCAL)

    def copy(self, j, d):
        f, _, _ = plane_places()
        t = lax.rem(f + d, 16)
        line = self.line
        return pltpu.make_async_remote_copy(
            src_ref=self.source_block(t), dst_ref=self.into(t, j),
            send_sem=line.send_sems.at[self.at + d], recv_sem=line.recv_sems.at[self.at + j],
            device_id={"fsdp": t}, device_id_type=MESH,
        )

    def keep(self, j):
        f, _, _ = plane_places()
        return self.line.local(self.local_at + j, self.source_block(f), self.into(f, j))

    def start(self):
        f, _, _ = plane_places()
        for j, source in enumerate(self.sources):
            @pl.when(f == source)
            def _():
                for d in range(1, 16):
                    self.copy(j, d).start()
                self.keep(j).start()

    def arrive(self):
        f, _, _ = plane_places()
        for j, source in enumerate(self.sources):
            @pl.when(f == source)
            def _():
                self.keep(j).wait()

            @pl.when(f != source)
            def _():
                ref = self.into(f, j)
                pltpu.make_async_remote_copy(
                    src_ref=ref, dst_ref=ref, send_sem=self.line.send_sems.at[self.at],
                    recv_sem=self.line.recv_sems.at[self.at + j],
                    device_id={"fsdp": lax.rem(f + 1, 16)}, device_id_type=MESH,
                ).wait_recv()

    def finish(self):
        f, _, _ = plane_places()
        for j, source in enumerate(self.sources):
            @pl.when(f == source)
            def _():
                for d in range(1, 16):
                    self.copy(j, d).wait_send()


def rows_of(total, half, quarter):
    if quarter is None:
        return pl.ds(half * (total // 2), total // 2)
    return pl.ds(half * (total // 2) + quarter * (total // 4), total // 4)


def columns_place(out):
    return lambda f, half, quarter: out.at[
        rows_of(out.shape[0], half, quarter), pl.ds(pl.multiple_of(f * 128, 128), 128)
    ]


def block_of(ref, t):
    return ref.at[:, pl.ds(pl.multiple_of(t * 128, 128), 128)]


ADD_ROWS = 16


def add_rows(dst, sources, first, count):
    def step(i, carry):
        rows = pl.ds(pl.multiple_of(first + i * ADD_ROWS, ADD_ROWS), ADD_ROWS)
        total = None
        for source, offset in sources:
            at = pl.ds(pl.multiple_of(first - offset + i * ADD_ROWS, ADD_ROWS), ADD_ROWS)
            item = source[at, :].astype(F32)
            total = item if total is None else total + item
        dst[rows, :] = total.astype(dst.dtype)
        return carry

    lax.fori_loop(0, count // ADD_ROWS, step, 0)


class RingSum:
    COPIES, LOCAL = 10, 4

    def __init__(self, line, partial, buffers, first=0):
        self.line, self.partial, self.first = line, partial, first
        self.own, self.stage, self.relay, self.away, self.back = buffers
        self.rows = self.stage.shape[1]
        self.block = pl.ds(first, self.rows)
        self.half = self.rows // 2
        self.low, self.high = pl.ds(0, self.half), pl.ds(self.half, self.half)
        self.at, self.local_at = line.take(self.COPIES, self.LOCAL)

    def near(self, k):
        s, partner, right, left, far = seq_places()
        p = (far, right, left, s)[k]
        return self.line.copy(
            self.at + k, self.partial.at[p + partner - s, self.block], self.stage.at[k],
            {"seq": partner},
        )

    def kept(self, k):
        s, partner, right, left, far = seq_places()
        p = (far, right, left, s)[k]
        return self.line.local(self.local_at + k, self.partial.at[p, self.block], self.own.at[k])

    def go(self, i):
        s, partner, right, left, far = seq_places()
        away, relay, back, low, high = self.away, self.relay, self.back, self.low, self.high
        src, dst, peer = (
            (away.at[0, low], relay.at[0], right),
            (away.at[0, high], relay.at[1], left),
            (away.at[1, high], back.at[0, high], right),
            (away.at[2, low], back.at[1, low], left),
            (away.at[1, low], back.at[0, low], right),
            (away.at[2, high], back.at[1, high], left),
        )[i]
        return self.line.copy(self.at + 4 + i, src, dst, {"seq": peer})

    def start(self):
        for k in range(4):
            self.near(k).start()
            if self.own is not None:
                self.kept(k).start()

    def ready(self, k):
        self.near(k).wait_recv()
        if self.own is not None:
            self.kept(k).wait()

    def pair(self, k):
        if self.own is not None:
            return [(self.own.at[k], 0), (self.stage.at[k], 0)]
        s, partner, right, left, far = seq_places()
        return [(self.partial.at[(far, right, left, s)[k]], -self.first), (self.stage.at[k], 0)]

    def far(self):
        half, away = self.half, self.away
        self.ready(0)
        add_rows(away.at[0], self.pair(0), 0, half)
        self.go(0).start()
        add_rows(away.at[0], self.pair(0), half, half)
        self.go(1).start()

    def beside(self, k):
        half = self.half
        self.ready(k)
        add_rows(self.away.at[k], self.pair(k), half if k == 1 else 0, half)
        self.go(1 + k).start()

    def middle(self):
        self.far()
        self.beside(1)
        self.beside(2)

    def send_step(self, step):
        @pl.when(step == 0)
        def _():
            self.near(3).start()

        @pl.when(step == 1)
        def _():
            self.near(1).start()

        @pl.when(step == 2)
        def _():
            self.near(2).start()
            self.beside(1)

        @pl.when(step == 3)
        def _():
            self.near(0).start()
            self.beside(2)

    def last(self):
        half, away, relay = self.half, self.away, self.relay
        self.go(0).wait_recv()
        add_rows(away.at[1], self.pair(1) + [(relay.at[0], 0)], 0, half)
        self.go(4).start()
        self.go(1).wait_recv()
        add_rows(away.at[2], self.pair(2) + [(relay.at[1], half)], half, half)
        self.go(5).start()

    def finish(self, total):
        self.ready(3)
        for i in (2, 3, 4, 5):
            self.go(i).wait_recv()
        sources = self.pair(3) + [(self.back.at[0], 0), (self.back.at[1], 0)]
        add_rows(total.at[self.block], sources, 0, self.rows)
        for k in range(4):
            self.near(k).wait_send()
        for i in range(6):
            self.go(i).wait_send()


def sum_buffers(rows, width):
    return [
        pltpu.VMEM((4, rows, width), BF16),
        pltpu.VMEM((4, rows, width), BF16),
        pltpu.VMEM((2, rows // 2, width), BF16),
        pltpu.VMEM((3, rows, width), BF16),
        pltpu.VMEM((2, rows, width), BF16),
    ]


MID_ROWS = 32


def by_rows(rows, step, first=0):
    def run(i, carry):
        step(pl.ds(pl.multiple_of(first + i * MID_ROWS, MID_ROWS), MID_ROWS))
        return carry

    lax.fori_loop(0, rows // MID_ROWS, run, 0)


def norm_back_rows(values, gain, grad):
    scale = lax.rsqrt(jnp.mean(values * values, axis=-1, keepdims=True) + 1e-05)
    weighted = grad * gain
    return scale * weighted - values * (
        scale * scale * scale * jnp.mean(weighted * values, axis=-1, keepdims=True)
    )


def comm_params(cid, limit=48):
    return pltpu.CompilerParams(
        collective_id=cid, has_side_effects=True, vmem_limit_bytes=limit << 20
    )


def start_kernel(payload, w_qkv, q_side, beta_side, everyone, wq, send, recv, local):
    s = lax.axis_index("seq")
    greet(ring_peers(), all_plane())
    line = Line(send, recv, local)
    depth, width = w_qkv.shape
    scatter = Scatter(
        line, (2 * s, 2 * s + 1),
        lambda t: w_qkv.at[pl.ds(t * 128, 128), :],
        lambda t, j: wq.at[pl.ds(t * 128, 128), pl.ds(j * width, width)],
    )
    ring = RingGather(line, payload, everyone)
    _, at = line.take(0, 2)
    sides = [
        line.local(at, q_side, wq.at[pl.ds(depth, SIDE), :]),
        line.local(at + 1, beta_side, wq.at[pl.ds(0, depth), pl.ds(2 * width, SIDE)]),
    ]

    def place(t, half, quarter):
        size = 64 if quarter is None else 32
        return wq.at[
            pl.ds(t * 128 + half * 64 + (quarter or 0) * 32, size), pl.ds(0, 2 * width)
        ]

    qkv = PlaneGather(line, place)
    scatter.start()
    ring.start()
    for copy in sides:
        copy.start()
    scatter.arrive()
    qkv.first()
    qkv.second()
    ring.middle()
    qkv.third()
    qkv.fourth()
    ring.finish()
    scatter.finish()
    qkv.finish()
    for copy in sides:
        copy.wait()


def start_gather(payload, w_qkv, q_side, beta_side):
    seq, wide = lax.axis_size("seq"), payload.shape[1]
    copies = RingGather.COPIES + Scatter.COPIES + PlaneGather.COPIES
    return pl.pallas_call(
        start_kernel,
        out_shape=(
            jax.ShapeDtypeStruct((seq,) + payload.shape, BF16),
            jax.ShapeDtypeStruct((wide, q_side.shape[1]), BF16),
        ),
        in_specs=[ANY] * 4,
        out_specs=(ANY,) * 2,
        scratch_shapes=sems(copies, 10),
        compiler_params=comm_params(0),
        name="start_gather",
    )(payload, w_qkv, q_side, beta_side)


class Feed:
    COPIES = RingGather.COPIES + 2 * Scatter.COPIES + 2 * PlaneGather.COPIES
    LOCAL = RingGather.LOCAL + 2 * Scatter.LOCAL + 3

    def __init__(self, line, cot, gate_t, w_out, sides, everyone, wg, wo, upper):
        s = lax.axis_index("seq")
        self.line, self.w_out, self.sides = line, w_out, sides
        self.outs = (wo, wg)
        self.ring = RingGather(line, cot, everyone)
        self.scatters = [
            Scatter(line, (source,), lambda t: block_of(gate_t, t), into)
            for source, into in ((s, lambda t, j: block_of(wg, t)), (s + 8, lambda t, j: upper))
        ]
        self.out, self.gate = [PlaneGather(line, columns_place(o)) for o in self.outs]
        _, self.at = line.take(0, 3)

    def place(self, i):
        s, f = lax.axis_index("seq"), lax.axis_index("fsdp")
        if i == 2:
            wo = self.outs[0]
            share = wo.shape[0]
            src = self.w_out.at[pl.ds(pl.multiple_of(s * share, 16), share), :]
            dst = block_of(wo, f)
        else:
            src, out = self.sides[i], self.outs[i]
            dst = out.at[:, pl.ds(out.shape[1] - SIDE, SIDE)]
        return self.line.local(self.at + i, src, dst)

    def start(self):
        for item in self.scatters:
            item.start()
        for i in range(3):
            self.place(i).start()
        self.ring.start()
        self.place(2).wait()
        self.out.first()

    def stage(self, step):
        @pl.when(step == 2)
        def _():
            self.out.second()
            self.scatters[0].arrive()
            self.gate.first()

        @pl.when(step == 3)
        def _():
            self.out.third()
            self.ring.middle()
            self.gate.second()

    def third(self):
        self.out.fourth()
        self.gate.third()

    def fourth(self):
        self.out.finish()
        self.place(0).wait()
        self.gate.fourth()

    def finish(self):
        self.ring.finish()
        self.gate.finish()
        self.place(1).wait()
        self.scatters[1].arrive()
        for item in self.scatters:
            item.finish()


def chip_at(step):
    x = lax.axis_index("seq") // 2
    d = jnp.where(step == 2, 3, jnp.where(step == 3, 2, step))
    return lax.rem(x + d, 4)


def feed_forward_kernel(
    partial, down_w, f_side, u_side, upper_block, wg_in, cot_in,
    tokens, cot, mixed, wo, up, gain, down, chosen,
    middle, grad_middle, partial_down, grad_mixed, early,
    rows2, rows3, cots, wg, wu, wd, partial2, total,
    gate_s, upper_s, hidden_s, gg_s, gu_s, gate_e, upper_e, down_e, *rest,
):
    greet(ring_peers(), line_peers())
    buffers, (send, recv, local) = rest[:-3], rest[-3:]
    line = Line(send, recv, local)
    s = lax.axis_index("seq")
    f = lax.axis_index("fsdp")
    rows = tokens.shape[0]
    firsts = (0, rows // 2)
    first_sum = [
        RingSum(line, partial, buffers[5 * i : 5 * i + 5], first)
        for i, first in enumerate(firsts)
    ]
    second_sum = [
        RingSum(line, partial2, (None,) + buffers[10 + 4 * i : 14 + 4 * i], first)
        for i, first in enumerate(firsts)
    ]
    first_gather = [RingGather(line, None, rows2, first, rows // 2) for first in firsts]
    second_gather = [RingGather(line, None, rows3, first, rows // 2) for first in firsts]
    weights = [PlaneGather(line, columns_place(o)) for o in (wu, wd)]
    share = wd.shape[0]
    width = tokens.shape[1]
    _, at = line.take(0, 6)
    mine = [
        line.local(at, upper_block, block_of(wu, f)),
        line.local(
            at + 1, down_w.at[pl.ds(pl.multiple_of(s * share, 16), share), :], block_of(wd, f)
        ),
    ]
    others = [
        line.local(at + 2, u_side, wu.at[:, pl.ds(width, SIDE)]),
        line.local(at + 3, f_side, wd.at[:, pl.ds(width, SIDE)]),
        line.local(at + 4, wg_in, wg),
        line.local(at + 5, cot_in, cots),
    ]
    for copy in mine:
        copy.start()
    for item in first_sum:
        item.start()
    for copy, item in zip(mine, weights):
        copy.wait()
        item.first()
    for copy in others:
        copy.start()
    for item in first_sum:
        item.middle()
    for item in weights:
        item.second()
    for item in first_sum:
        item.last()

    def norm_rows(rows):
        inner = total[rows, width:].astype(BF16)
        value = tokens[rows, :].astype(F32) + (total[rows, :width] + mm(inner, up[...]))
        middle[rows, :] = value
        scale = lax.rsqrt(jnp.mean(value * value, axis=-1, keepdims=True) + 1e-05)
        normed = (value * scale * gain[...]).astype(BF16)
        rows2[s, rows, :width] = normed
        rows2[s, rows, width:] = (inner.astype(F32) + mm_nt(normed, down[...])).astype(BF16)

    first_sum[0].finish(total)
    by_rows(rows // 2, norm_rows)
    first_gather[0].start()
    for item in weights:
        item.third()
    first_sum[1].finish(total)
    by_rows(rows // 2, norm_rows, rows // 2)
    first_gather[1].start()
    for item in weights:
        item.fourth()
    for item in weights:
        item.finish()
    for copy in others:
        copy.wait()
    gate_e[...] = jnp.zeros_like(gate_e)
    upper_e[...] = jnp.zeros_like(upper_e)
    down_e[...] = jnp.zeros_like(down_e)
    pair = 2 * rows

    def chip(step, carry):
        for item in first_gather:
            item.reach(step)
        k = chip_at(step)
        both = pl.ds(k * 2, 2)
        normed = rows2[both].reshape(pair, width + SIDE)
        grads = cots[both].reshape(pair, width + SIDE)
        gate_s[...] = mm_nt(normed, wg[...])
        upper_s[...] = mm_nt(normed, wu[...])
        hidden = mm_nt(grads, wd[...])
        gate, upper = gate_s[...], upper_s[...]
        sigma = sigmoid(gate)
        silu = gate * sigma
        hidden_s[...] = (silu * upper).astype(BF16)
        gg_s[...] = (hidden * upper * sigma * (1.0 + gate * (1.0 - sigma))).astype(BF16)
        gu_s[...] = (hidden * silu).astype(BF16)
        partial2[both] = (
            (mm(gg_s[...], wg[...]) + mm(gu_s[...], wu[...]))
            .astype(BF16)
            .reshape(2, pair // 2, width + SIDE)
        )
        for item in second_sum:
            item.send_step(step)
        partial_down[both] = (
            mm(hidden_s[...], wd[...]).astype(BF16).reshape(2, pair // 2, width + SIDE)
        )
        side = normed[:, width:]
        gate_e[...] += mm_tn(side, gg_s[...])
        upper_e[...] += mm_tn(side, gu_s[...])
        down_e[...] += mm_tn(grads[:, width:], hidden_s[...])
        return carry

    lax.fori_loop(0, 4, chip, 0)
    for item in second_sum:
        item.far()
    for item in second_sum:
        item.last()

    def back_rows(rows):
        inner = total[rows, width:].astype(BF16)
        grad = total[rows, :width] + mm(inner, down[...])
        result = cot[rows, :].astype(F32) + norm_back_rows(middle[rows, :], gain[...], grad)
        grad_middle[rows, :] = result
        low = result.astype(BF16)
        rows3[s, rows, :width] = low
        rows3[s, rows, width:] = (inner.astype(F32) + mm_nt(low, up[...])).astype(BF16)

    second_sum[0].finish(total)
    by_rows(rows // 2, back_rows)
    second_gather[0].start()
    second_sum[1].finish(total)
    by_rows(rows // 2, back_rows, rows // 2)
    second_gather[1].start()
    for item in first_gather:
        item.sent()

    def out_back(step, carry):
        for item in second_gather:
            item.reach(step)
        k = chip_at(step)
        grads = rows3[pl.ds(k * 2, 2)].reshape(pair, width + SIDE)
        grad_mixed[pl.ds(pl.multiple_of(k * pair, pair), pair), :] = mm_nt(grads, wo[...]).astype(
            BF16
        )
        return carry

    lax.fori_loop(0, 4, out_back, 0)
    rank = early.shape[2]
    part = mixed.shape[1]
    own_part = pl.ds(pl.multiple_of(s * part, 128), part)
    flat = lambda v: v.reshape(-1, v.shape[-1])
    side2, side3 = flat(rows2[:, :, width:]), flat(rows3[:, :, width:])
    first = [
        gate_e[rank : 2 * rank, :].astype(BF16),
        upper_e[rank : 2 * rank, :].astype(BF16),
        chosen[...],
    ]
    second = [
        mm_tn(side3, mixed[...])[:rank].astype(BF16),
        mm_tn(side2, flat(rows3[:, :, own_part]))[:rank].astype(BF16),
        mm_tn(side3, flat(rows2[:, :, own_part]))[rank : 2 * rank].astype(BF16),
        down_e[:rank, :].astype(BF16),
        chosen[:, : SIDE // 2],
    ]
    n = early.shape[3]
    for half, parts in enumerate((first, second)):
        piece = jnp.concatenate(parts, axis=1)
        early[half, 0] = piece[:, :n]
        early[half, 1] = piece[:, n:]
    for item in second_gather:
        item.sent()


def feed_forward(
    partial, down_w, f_side, u_side, upper, wg, cots,
    tokens, cot, mixed, wo, up, gain, down, chosen,
):
    seq, rows, wide = partial.shape
    share = f_side.shape[0]
    rank, part = chosen.shape[0], mixed.shape[1]
    whole = pltpu.VMEM((seq, rows, wide), BF16)
    weight = pltpu.VMEM((share, wide), BF16)
    buffers = sum_buffers(rows // 2, wide)
    f32_rows = pltpu.VMEM((2 * rows, share), F32)
    bf16_rows = pltpu.VMEM((2 * rows, share), BF16)
    extra = pltpu.VMEM((SIDE, share), F32)
    return pl.pallas_call(
        feed_forward_kernel,
        out_shape=(
            jax.ShapeDtypeStruct((rows, wide - SIDE), F32),
            jax.ShapeDtypeStruct((rows, wide - SIDE), F32),
            jax.ShapeDtypeStruct((seq, rows, wide), BF16),
            jax.ShapeDtypeStruct((seq * rows, part), BF16),
            jax.ShapeDtypeStruct((2, 2, rank, share + SIDE // 2), BF16),
        ),
        in_specs=[ANY] * 7 + [VMEM] * 8,
        out_specs=(VMEM,) * 5,
        scratch_shapes=[whole, whole, whole, weight, weight, weight, whole]
        + [pltpu.VMEM((rows, wide), F32)]
        + [f32_rows, f32_rows, bf16_rows, bf16_rows, bf16_rows, extra, extra, extra]
        + buffers * 2
        + buffers[1:] * 2
        + sems(4 * RingSum.COPIES + 4 * RingGather.COPIES + 2 * PlaneGather.COPIES, 26),
        compiler_params=comm_params(2, 63),
        name="feed_forward",
    )(
        partial, down_w, f_side, u_side, upper, wg, cots,
        tokens, cot, mixed, wo, up, gain, down, chosen,
    )


class EarlySum:
    COPIES, LOCAL = PlaneGather.COPIES + RingGather.COPIES, 1 + RingGather.LOCAL

    def __init__(self, line, early, pieces, total, out):
        self.line, self.early, self.pieces, self.total = line, early, pieces, total
        _, self.local_at = line.take(0, 1)
        self.ring = RingGather(line, total, out)

        def place(f, half, quarter):
            return pieces.at[f, half] if quarter is None else pieces.at[f, half, quarter]

        self.plane = PlaneGather(line, place)

    def start(self):
        own = self.line.local(
            self.local_at, self.early, self.pieces.at[lax.axis_index("fsdp")]
        )
        own.start()
        own.wait()
        self.plane.first()

    def add(self):
        self.plane.finish()
        f = lax.axis_index("fsdp")
        half = lax.rem(f, 2)
        lane = lax.broadcasted_iota(jnp.int32, (1, SIDE), 1)
        mark = jnp.where(half == 0, 0, SIDE // 2) + f // 2
        totals = [None, None]
        for t in range(16):
            pair = [self.pieces[t, half, q].astype(F32) for q in (0, 1)]
            marks = pair[1][:1, -SIDE:]
            uses = jnp.sum(jnp.where(lane == mark, marks, 0.0), axis=1, keepdims=True)
            totals = [
                p * uses if total is None else total + p * uses for p, total in zip(pair, totals)
            ]
        self.total[0] = totals[0].astype(BF16)
        self.total[1] = totals[1].astype(BF16)
        self.ring.start()


def by_adapter(plane, out):
    count, wide = out.shape[0], out.shape[2]
    parts, n = plane.shape[1], plane.shape[3]
    for q in range(parts):
        cut = min(n, wide - q * n)
        for a in range(count):
            total = None
            for f in range(plane.shape[0]):
                at = wide - (parts - 1) * n + a
                uses = plane[f, parts - 1].astype(F32)[:1, at : at + 1]
                item = plane[f, q].astype(F32)[:, :cut] * uses
                total = item if total is None else total + item
            out[a, :, q * n : q * n + cut] = total.astype(BF16)


def finale_kernel(
    partial, normed, cot, early, up, inner, tokens, grad_middle, down, gain, chosen,
    input_grad, early_whole, late_whole,
    total, own, stage, relay, away, back, inners, sides, pieces, late, send, recv, local,
):
    greet(ring_peers(), line_peers())
    line = Line(send, recv, local)
    s, partner, _, _, _ = seq_places()
    f = lax.axis_index("fsdp")
    core = lax.rem(s, 2)
    rank, columns = up.shape
    ring = RingSum(line, partial, (own, stage, relay, away, back))
    inner_ring = RingGather(line, inner, inners)
    late_ring = RingGather(line, late, late_whole)

    def early_place(t, half, quarter):
        first = core * 4 + half * 2 + (quarter or 0)
        return early_whole.at[t, pl.ds(first, 2 if quarter is None else 1)]

    def late_place(t, half, quarter):
        first = half * 2 + (quarter or 0)
        return pieces.at[t, pl.ds(first, 2 if quarter is None else 1)]

    early_plane, late_plane = PlaneGather(line, early_place), PlaneGather(line, late_place)
    at, local_at = line.take(1, 3)
    half_slices = pl.ds(core * 4, 4)
    keep = line.local(local_at, early.at[half_slices], early_whole.at[f, half_slices])
    share = line.copy(
        at, early_whole.at[:, half_slices], early_whole.at[:, half_slices], {"seq": partner}
    )
    part = sides.shape[1] // 2
    mine = pl.ds(pl.multiple_of(s * part, 128), part)
    fetch = [
        line.local(local_at + 1, normed.at[:, mine], sides.at[:, pl.ds(0, part)]),
        line.local(local_at + 2, cot.at[:, mine], sides.at[:, pl.ds(part, part)]),
    ]
    inner_ring.start()
    ring.start()
    keep.start()
    for copy in fetch:
        copy.start()
    keep.wait()
    early_plane.first()
    inner_ring.middle()
    ring.middle()
    inner_ring.finish()
    tokens_here = tokens.shape[0]
    n = inners.shape[3]
    ahead = sides.shape[0] - n
    sums, beside = [None, None], []
    for t in range(inners.shape[0]):
        parts = inners[t, 0].astype(F32), inners[t, 1].astype(F32)[:, :ahead]
        sums = [p if total_ is None else total_ + p for p, total_ in zip(parts, sums)]
        beside.append(inners[t, 1][:, ahead : ahead + tokens_here])
    for copy in fetch:
        copy.wait()
    down_piece = mm(jnp.concatenate(sums, axis=1), sides[:, :part])
    up_piece = mm(jnp.concatenate(beside, axis=1), sides[:, part:])
    piece = jnp.concatenate(
        [up[...], down_piece.astype(BF16), up_piece.astype(BF16), chosen[...], chosen[...]], axis=1
    )
    wide = pieces.shape[3]
    for q in range(4):
        pieces[f, q] = piece[:, q * wide : (q + 1) * wide]
    late_plane.first()
    early_plane.second()
    ring.last()
    late_plane.second()
    late_plane.third()
    early_plane.third()
    late_plane.fourth()
    late_plane.finish()
    by_adapter(pieces, late)
    late_ring.start()
    early_plane.fourth()
    ring.finish(total)
    width = tokens.shape[1]

    def step(rows):
        grad = total[rows, :width] + mm(total[rows, width:], down[...])
        input_grad[rows, :] = (
            grad_middle[rows, :]
            + norm_back_rows(tokens[rows, :].astype(F32), gain[...], grad)
        ).astype(BF16)

    by_rows(tokens_here, step)
    early_plane.finish()
    share.start()
    late_ring.middle()
    late_ring.finish()
    share.wait()


def finale_call(
    partial, normed, cot, early, up, inner, tokens, grad_middle, down, gain, chosen, count
):
    seq, rows, wide = partial.shape
    fsdp = 16
    rank, columns = up.shape
    part = (wide - SIDE) // seq
    bf16 = lambda *shape: pltpu.VMEM(shape, BF16)
    out = lambda *shape: jax.ShapeDtypeStruct(shape, BF16)
    late = columns + 2 * part
    copies = RingSum.COPIES + 2 * RingGather.COPIES + 2 * PlaneGather.COPIES + 1
    return pl.pallas_call(
        finale_kernel,
        out_shape=(
            out(rows, wide - SIDE), out(fsdp, *early.shape), out(seq, count, rank, late),
        ),
        in_specs=[ANY] * 4 + [VMEM, ANY] + [VMEM] * 5,
        out_specs=(VMEM, ANY, ANY),
        scratch_shapes=[pltpu.VMEM((rows, wide), F32)]
        + sum_buffers(rows, wide)
        + [
            bf16(seq, *inner.shape), bf16(seq * rows, 2 * part),
            bf16(fsdp, 4, rank, (late + 2 * SIDE) // 4), bf16(count, rank, late),
        ]
        + sems(copies, 4 + 2 + 3),
        compiler_params=comm_params(4),
        name="finale",
    )(partial, normed, cot, early, up, inner, tokens, grad_middle, down, gain, chosen)


def lay_out_early(whole, share, part):
    fsdp, seq, _, rank, n = whole.shape
    count = fsdp // 2

    def kernel(whole, gateup, mix_down, mix_up, gu_down, ff_down):
        for t in range(seq):
            first = jnp.concatenate([whole[0, t, 0], whole[0, t, 1]], axis=1).astype(F32)
            gateup[0, :, t * share : (t + 1) * share] = first[:, :share]
            at = (seq + t) * share
            gateup[0, :, at : at + share] = first[:, share : 2 * share]
            second = jnp.concatenate([whole[1, t, 0], whole[1, t, 1]], axis=1).astype(F32)
            for i, out in enumerate((mix_down, mix_up, gu_down)):
                out[0, :, t * part : (t + 1) * part] = second[:, i * part : (i + 1) * part]
            ff_down[0, :, t * share : (t + 1) * share] = second[:, 3 * part : 3 * part + share]

    widths = (2 * share * seq,) + (part * seq,) * 3 + (share * seq,)
    return pl.pallas_call(
        kernel,
        grid=(count,),
        out_shape=tuple(jax.ShapeDtypeStruct((count, rank, w), F32) for w in widths),
        in_specs=[pl.BlockSpec((2, seq, 2, rank, n), lambda a: (a, 0, 0, 0, 0))],
        out_specs=tuple(pl.BlockSpec((1, rank, w), lambda a: (a, 0, 0)) for w in widths),
        compiler_params=pltpu.CompilerParams(vmem_limit_bytes=32 << 20),
        name="lay_out_early",
    )(whole)


def lay_out_late(whole, columns, part):
    seq, count, rank, wide = whole.shape

    def kernel(whole, qkv_up, qkv_down, ff_up):
        for t in range(seq):
            qkv_up[0, :, t * columns : (t + 1) * columns] = whole[t, 0, :, :columns].astype(F32)
            for i, out in enumerate((qkv_down, ff_up)):
                at = columns + i * part
                out[0, :, t * part : (t + 1) * part] = whole[t, 0, :, at : at + part].astype(F32)

    widths = (columns * seq, part * seq, part * seq)
    return pl.pallas_call(
        kernel,
        grid=(count,),
        out_shape=tuple(jax.ShapeDtypeStruct((count, rank, w), F32) for w in widths),
        in_specs=[pl.BlockSpec((seq, 1, rank, wide), lambda a: (0, a, 0, 0))],
        out_specs=tuple(pl.BlockSpec((1, rank, w), lambda a: (a, 0, 0)) for w in widths),
        compiler_params=pltpu.CompilerParams(vmem_limit_bytes=32 << 20),
        name="lay_out_late",
    )(whole)


def prepare_kernel(
    places, tokens, cot, gain, q_down, q_up, m_down, m_up, g_down, gu_up, f_down, f_up, w_beta,
    conv, docs,
    payload, cots, q_side, beta_side, out_side, g_side, u_side, f_side,
    m_lines, g_lines, f_lines, q_lines, dcol, drow, taps, chosen,
):
    which, s = places[0], places[1]
    rank, width = q_down.shape[1], tokens.shape[1]
    share = g_side.shape[0]

    def lines(out, block, first):
        parts = [jnp.zeros((first, width), BF16)] if first else []
        parts += [block, jnp.zeros((SIDE - first - rank, width), BF16)]
        out[...] = jnp.concatenate(parts, axis=0)

    lines(m_lines, m_up[0], 0)
    lines(g_lines, g_down[0], rank)
    lines(f_lines, f_up[0], 0)
    lines(q_lines, q_down[0], rank)

    def turned(block, first):
        n = block.shape[1]
        parts = [jnp.zeros((first, n), F32)] if first else []
        parts += [block.astype(F32), jnp.zeros((SIDE - first - block.shape[0], n), F32)]
        return jnp.concatenate(parts, axis=0).T.astype(BF16)

    def window(ref, base):
        size = -(-share // 128) * 128
        tile = base // 128 + (s * share) // 128
        wide = ref[0, :, pl.ds(pl.multiple_of(tile * 128, 128), size)].astype(F32)
        late = jnp.concatenate([wide[:, 64:], wide[:, :64]], axis=1)
        return jnp.where(lax.rem(s, 2) == 1, late, wide)

    g_side[...] = turned(window(gu_up, 0), rank)[:share]
    u_side[...] = turned(window(gu_up, f_down.shape[2]), rank)[:share]
    f_side[...] = turned(window(f_down, 0), 0)[:share]
    out_side[...] = turned(m_down[0], 0)
    heads = taps.shape[1] // conv.shape[2]
    row = lax.broadcasted_iota(jnp.int32, w_beta.shape, 0)
    beta = w_beta[...].astype(F32)
    rows = [
        jnp.sum(jnp.where(row == s * heads + h, beta, 0.0), axis=0, keepdims=True)
        for h in range(heads)
    ]
    beta_side[...] = turned(jnp.concatenate(rows, axis=0), 0)
    q_side[...] = jnp.zeros_like(q_side)
    q_side[rank : 2 * rank, : q_up.shape[2]] = q_up[0]

    value = tokens[...].astype(F32)
    scale = lax.rsqrt(jnp.mean(value * value, axis=-1, keepdims=True) + 1e-05)
    normed = (value * scale * gain[...]).astype(BF16)
    payload[:, :width] = normed
    payload[:, width:] = mm_nt(normed, q_lines[...]).astype(BF16)
    cots[:, :width] = cot[...]
    cots[:, width:] = mm_nt(cot[...], f_lines[...]).astype(BF16)

    chunks = drow.shape[0]
    dcol[:PAD, :] = jnp.full((PAD, CH), -1, jnp.int32)
    dcol[PAD + chunks * CH :, :] = jnp.full((PAD, CH), -1, jnp.int32)
    for c in range(chunks):
        line = docs[:, c * CH : (c + 1) * CH]
        drow[c : c + 1, :] = line
        square = jnp.broadcast_to(line.astype(F32), (CH, CH)).T
        dcol[PAD + c * CH : PAD + (c + 1) * CH, :] = square.astype(jnp.int32)
    third = conv.shape[2]
    for t in range(conv.shape[0]):
        for h in range(heads):
            taps[t : t + 1, h * third : (h + 1) * third] = conv[t, pl.ds(s * heads + h, 1), :]
    lane = lax.broadcasted_iota(jnp.int32, chosen.shape, 1)
    chosen[...] = (lane == which).astype(F32).astype(BF16)


def prepare(
    places, tokens, cot, gain, q_down, q_up, m_down, m_up, g_down, gu_up, f_down, f_up, w_beta,
    conv, docs, seq,
):
    rows, width = tokens.shape
    rank = q_down.shape[1]
    columns, part, share = q_up.shape[2] // seq, width // seq, f_down.shape[2] // seq
    length = docs.shape[1]
    one = lambda n: pl.BlockSpec((1, rank, n), lambda i, p: (p[0], 0, 0))
    mine = lambda n: pl.BlockSpec((1, rank, n), lambda i, p: (p[0], 0, p[1]))
    full = lambda a: pl.BlockSpec(a.shape, lambda i, p, a=a: (0,) * a.ndim)
    S = jax.ShapeDtypeStruct
    outs = (
        S((rows, width + SIDE), BF16), S((rows, width + SIDE), BF16),
        S((SIDE, columns + SIDE), BF16), S((width, SIDE), BF16), S((part, SIDE), BF16),
        S((share, SIDE), BF16), S((share, SIDE), BF16), S((share, SIDE), BF16),
        S((SIDE, width), BF16), S((SIDE, width), BF16), S((SIDE, width), BF16),
        S((SIDE, width), BF16),
        S((length + 2 * PAD, CH), jnp.int32), S((length // CH, CH), jnp.int32),
        S((conv.shape[0], columns), F32), S((rank, SIDE), BF16),
    )
    return pl.pallas_call(
        prepare_kernel,
        out_shape=outs,
        grid_spec=pltpu.PrefetchScalarGridSpec(
            num_scalar_prefetch=1,
            grid=(1,),
            in_specs=[
                full(tokens), full(cot), full(gain), one(width), mine(columns), mine(part),
                one(width), one(width), one(gu_up.shape[2]), one(f_down.shape[2]), one(width),
                full(w_beta), full(conv), full(docs),
            ],
            out_specs=[pl.BlockSpec(o.shape, lambda i, p, o=o: (0,) * len(o.shape)) for o in outs],
        ),
        compiler_params=pltpu.CompilerParams(vmem_limit_bytes=62 << 20),
        name="prepare",
    )(places, tokens, cot, gain, q_down, q_up, m_down, m_up, g_down, gu_up, f_down, f_up, w_beta,
      conv, docs)


BOTH = ("fsdp", "seq")


def body(
    tokens,
    segments,
    adapter_index,
    attn_gain,
    w_qkv,
    w_beta,
    conv_weight,
    head_gain,
    w_out,
    ffn_gain,
    w_gateup,
    w_down,
    qkv_down,
    qkv_up,
    mixout_down,
    mixout_up,
    gateup_down,
    gateup_up,
    ffnout_down,
    ffnout_up,
    cotangent,
):
    seq = lax.axis_size("seq")
    s = lax.axis_index("seq")
    width = tokens.shape[1]
    heads = w_beta.shape[1] // seq
    count = qkv_down.shape[0]
    columns = heads * 3 * CH
    which = adapter_index[0]
    length = segments.shape[1]

    turn = lambda v: jnp.swapaxes(v, 1, 2)
    (
        payload, cots, q_side, beta_side, out_side, g_side, u_side, f_side,
        m_lines, g_lines, f_lines, q_lines, dcol, drow, taps, chosen,
    ) = prepare(
        jnp.stack([which, s]), tokens, cotangent, attn_gain[None],
        turn(qkv_down), qkv_up, turn(mixout_down), mixout_up, turn(gateup_down), gateup_up,
        turn(ffnout_down), ffnout_up, w_beta.T, conv_weight, segments, seq,
    )

    normed, wq = start_gather(payload, w_qkv, q_side, beta_side)
    normed = normed.reshape(length, -1)
    fixed = (dcol, drow, taps, head_gain[None])
    mixed, o_kept, t_kept, d_kept, s_kept, partial, joined, cot, wg, upper, wo = mixer_fwd(
        normed, wq, cots, w_gateup.T, w_out, g_side, out_side, *fixed
    )

    middle, grad_middle, partial_down, grad_mixed, early = feed_forward(
        partial, w_down, f_side, u_side, upper, wg, cot, tokens, cotangent, mixed, wo,
        m_lines, ffn_gain[None], g_lines, chosen,
    )

    partial, up, layer_out, inner, early = mixer_bwd(
        joined, partial_down, early, normed, wq, q_side, middle, f_lines, *fixed,
        grad_mixed, o_kept, t_kept, d_kept, s_kept,
    )
    input_grad, early, late = finale_call(
        partial, normed, cot.reshape(length, -1), early, up, inner,
        tokens, grad_middle, q_lines, attn_gain[None], chosen, count,
    )
    gateup_g, mixdown_g, mixup_g, gudown_g, ffdown_g = lay_out_early(
        early, w_down.shape[0] // seq, width // seq
    )
    qkvup_g, qkvdown_g, ffup_g = lay_out_late(late, columns, width // seq)
    return (
        layer_out,
        input_grad,
        turn(qkvdown_g),
        qkvup_g,
        turn(mixdown_g),
        mixup_g,
        turn(gudown_g),
        gateup_g,
        turn(ffdown_g),
        ffup_g,
    )


def solution(mesh):
    tokens, columns = P(BOTH, None), P(None, "fsdp")
    placed = (
        tokens, P("fsdp", None), P("fsdp"), P(), columns, P(), P(), P(), columns, P(), columns,
        columns, P(), P(), P(), P(), P(), P(), P(), P(), tokens,
    )
    return jax.shard_map(
        body,
        mesh=mesh,
        in_specs=placed,
        out_specs=(tokens, tokens) + (P(),) * 8,
        check_vma=False,
    )
```

```python
import functools
import jax
import jax.numpy as jnp
from jax import lax
from jax.experimental import pallas as pl
from jax.experimental.pallas import tpu as pltpu
from jax.sharding import PartitionSpec as P

F32 = jnp.float32
BF16 = jnp.bfloat16
CH = 128
PAD = 16


def mm(a, b):
    return jnp.dot(a.astype(BF16), b.astype(BF16), preferred_element_type=F32)


def mm_nt(a, b):
    return lax.dot_general(
        a.astype(BF16), b.astype(BF16), (((1,), (1,)), ((), ())), preferred_element_type=F32
    )


def mm_tn(a, b):
    return lax.dot_general(
        a.astype(BF16), b.astype(BF16), (((0,), (0,)), ((), ())), preferred_element_type=F32
    )


def split(a):
    high = a.astype(BF16)
    return high, (a - high.astype(F32)).astype(BF16)


def mm_fine(a, b):
    ah, al = split(a)
    bh, bl = split(b)
    return jnp.dot(
        jnp.concatenate([ah, al, ah], axis=1),
        jnp.concatenate([bh, bh, bl], axis=0),
        preferred_element_type=F32,
    )


def unit_lower_inverses(lowers, row, col, product):
    each = lambda f, *lists: [f(*items) for items in zip(*lists)]
    near = (row >> 3) == (col >> 3)
    eye = (row == col).astype(F32)
    first = [jnp.where(near, lower, 0.0) for lower in lowers]
    second = each(product, first, first)
    fourth = each(product, second, second)
    third = each(product, first, second)
    inverses = each(lambda a, b, c: eye - a + b - c, first, second, third)
    last = each(product, inverses, fourth)
    inverses = each(lambda a, b: a + b, inverses, last)
    for bits in (3, 4, 5, 6):
        joining = ((row >> (bits + 1)) == (col >> (bits + 1))) & ((row >> bits) != (col >> bits))
        below = [jnp.where(joining, lower, 0.0) for lower in lowers]
        below = each(product, below, inverses)
        below = each(product, inverses, below)
        inverses = each(lambda a, b: a - b, inverses, below)
    return inverses


def sigmoid(v):
    return 1.0 / (1.0 + jnp.exp(-v))


def chunk_masks(c, dcol, drow):
    start = pl.multiple_of(c * CH, CH)
    docs = dcol[pl.ds(start + PAD, CH), :]
    before = dcol[pl.ds(start + PAD - 8, 8), :][7:8, :]
    last = docs[CH - 1 :, :]
    same = docs == drow[pl.ds(c, 1), :]
    live = (docs == before).astype(F32)
    tail = (docs == last).astype(F32)
    live_last = (last == before).astype(F32)
    return docs, same, live, tail, live_last


def conv_chunk(c, joined, dcol, taps, docs):
    start = pl.multiple_of(c * CH, CH)
    window = joined[pl.ds(start, CH + PAD), : taps.shape[1]].astype(F32)
    ids = dcol[pl.ds(start, CH + PAD), :]
    total = window[PAD:, :] * taps[3:4, :]
    for lag in (1, 2, 3):
        keep = (ids[PAD - lag : PAD - lag + CH, :] == docs).astype(F32)
        keep = jnp.concatenate([keep] * (taps.shape[1] // CH), axis=1)
        total = total + window[PAD - lag : PAD - lag + CH, :] * keep * taps[3 - lag : 4 - lag, :]
    return total


def raw_chunk(c, joined, taps):
    rows = pl.ds(pl.multiple_of(c * CH + PAD, PAD), CH)
    return joined[rows, taps.shape[1] :].astype(F32)


def normal_parts(act):
    query, keys, values = act[:, :CH], act[:, CH : 2 * CH], act[:, 2 * CH :]
    q_scale = lax.rsqrt(jnp.sum(query * query, axis=-1, keepdims=True) + 1e-06)
    k_scale = lax.rsqrt(jnp.sum(keys * keys, axis=-1, keepdims=True) + 1e-06)
    return query * q_scale * CH**-0.5, keys * k_scale, values, q_scale, k_scale


def mixer_fwd_kernel(
    heads, chunks, normed, weight, cot, w_out, w_down, out_side, f_side,
    dcol, drow, taps, gain,
    mixed, o_out, t_out, d_out, s_out, partial, joined_out, everyone, wo, wd,
    joined, rows_v, weight_v, wo_v, q_s, k_s, u_s, w_s, p_s, sem, send, recv, local,
):
    loads = [
        pltpu.make_async_copy(weight, weight_v, sem.at[0]),
        pltpu.make_async_copy(normed, rows_v, sem.at[1]),
    ]
    for copy in loads:
        copy.start()
    greet(ring_peers(), line_peers())
    feed = Feed(
        Line(send, recv, local), cot, (w_out, w_down), (out_side, f_side), everyone, (wo, wd)
    )
    feed.start()
    joined[pl.ds(0, PAD), :] = jnp.zeros((PAD, joined.shape[1]), BF16)
    for copy in loads:
        copy.wait()
    batch = 2 * CH

    def project(step):
        rows = pl.multiple_of(step * batch, batch)
        joined[pl.ds(rows + PAD, batch), :] = mm(
            rows_v[pl.ds(rows, batch), :], weight_v[...]
        ).astype(BF16)

    project(0)
    row = lax.broadcasted_iota(jnp.int32, (CH, CH), 0)
    col = lax.broadcasted_iota(jnp.int32, (CH, CH), 1)

    def prepare(items):
        lowers, parts = [], []
        for c, docs, same, live, act, raws in items:
            for h in range(heads):
                query, keys, values, _, _ = normal_parts(act[:, h * 3 * CH : (h + 1) * 3 * CH])
                beta = sigmoid(raws[:, h : h + 1])
                inner = mm_nt(keys, keys)
                lowers.append(jnp.where(same & (row > col), inner * beta, 0.0))
                rows = pl.ds(pl.multiple_of(c * CH, CH), CH)
                scores = jnp.where(same & (row >= col), mm_nt(query, keys), 0.0)
                p_s[h, rows, :] = scores.astype(BF16)
                q_s[h, rows, :] = (query * live).astype(BF16)
                k_s[h, rows, :] = keys
                targets = jnp.concatenate([values * beta, keys * (beta * live)], axis=1)
                parts.append((h, rows, targets.astype(BF16)))
        inverses = unit_lower_inverses(lowers, row, col, mm_fine)
        for inverse, (h, rows, targets) in zip(inverses, parts):
            inverse = inverse.astype(BF16)
            t_out[h, rows, :] = inverse
            both = mm(inverse, targets)
            u_s[h, rows, :] = both[:, :CH]
            w_s[h, rows, :] = both[:, CH:].astype(BF16)

    def first(step, carry):
        feed.stage(step)
        parts = []
        for part in range(2):
            c = step * 2 + part
            docs, same, live, tail, live_last = chunk_masks(c, dcol, drow)
            conv = conv_chunk(c, joined, dcol, taps, docs)
            act = conv * sigmoid(conv)
            parts.append((c, docs, same, live, act, raw_chunk(c, joined, taps)))
        project(jnp.minimum(step + 1, chunks // 2 - 1))
        prepare(parts)
        return carry

    lax.fori_loop(0, chunks // 2, first, 0)
    kept = pltpu.make_async_copy(joined.at[pl.ds(PAD, chunks * CH), :], joined_out, sem.at[0])
    kept.start()
    feed.third()

    def second(c, states):
        rows = pl.ds(pl.multiple_of(c * CH, CH), CH)
        docs, same, live, tail, live_last = chunk_masks(c, dcol, drow)
        for h in range(heads):
            s_out[h, rows, :] = states[h].astype(BF16)
        recalled = [mm(w_s[h, rows, :], states[h]) for h in range(heads)]
        updates = [u_s[h, rows, :] - recalled[h] for h in range(heads)]
        added = [mm_tn(k_s[h, rows, :] * tail, updates[h]) for h in range(heads)]
        for h in range(heads):
            d_out[h, rows, :] = updates[h].astype(BF16)
        return tuple(states[h] * live_last + added[h] for h in range(heads))

    zero = jnp.zeros((CH, CH), F32)
    lax.fori_loop(0, chunks, second, (zero,) * heads)
    feed.fourth()
    last = pltpu.make_async_copy(wo, wo_v, sem.at[1])
    last.start()
    last.wait()

    def third(c, carry):
        rows = pl.ds(pl.multiple_of(c * CH, CH), CH)
        outs = [
            mm(
                jnp.concatenate([q_s[h, rows, :], p_s[h, rows, :]], axis=1),
                jnp.concatenate(
                    [s_out[h, rows, :], d_out[h, rows, :]], axis=0
                ),
            )
            for h in range(heads)
        ]
        for h, out in enumerate(outs):
            o_out[h, rows, :] = out
            scale = lax.rsqrt(jnp.mean(out * out, axis=-1, keepdims=True) + 1e-05)
            mixed[rows, h * CH : (h + 1) * CH] = (out * scale * gain[...]).astype(BF16)
        partial[c] = mm(mixed[rows, :], wo_v[...]).astype(BF16)
        return carry

    lax.fori_loop(0, chunks, third, 0)
    kept.wait()
    feed.finish()


def mixer_fwd(
    normed, weight, cot, w_out, w_down, out_side, f_side, dcol, drow, taps, gain
):
    tokens, across = normed.shape
    wide = weight.shape[1]
    heads = wide // (3 * CH)
    chunks = tokens // CH
    seq = lax.axis_size("seq")
    out = lambda *shape: jax.ShapeDtypeStruct(shape, BF16)
    square = out(heads, tokens, CH)
    share, part = f_side.shape[0], out_side.shape[0]
    return pl.pallas_call(
        functools.partial(mixer_fwd_kernel, heads, chunks),
        out_shape=(
            out(tokens, heads * CH), jax.ShapeDtypeStruct(square.shape, F32), square, square, square,
            out(chunks, CH, across), out(tokens, wide), out(seq, *cot.shape),
            out(part, across), out(share, across),
        ),
        in_specs=[ANY] * 7 + [VMEM] * 4,
        out_specs=(VMEM,) * 6 + (ANY,) * 4,
        scratch_shapes=[
            pltpu.VMEM((tokens + PAD, wide), BF16),
            pltpu.VMEM((tokens, across), BF16),
            pltpu.VMEM((across, wide), BF16),
            pltpu.VMEM((part, across), BF16),
            pltpu.VMEM((heads, tokens, CH), BF16),
            pltpu.VMEM((heads, tokens, CH), F32),
            pltpu.VMEM((heads, tokens, CH), F32),
            pltpu.VMEM((heads, tokens, CH), BF16),
            pltpu.VMEM((heads, tokens, CH), BF16),
            pltpu.SemaphoreType.DMA((2,)),
        ]
        + sems(Feed.COPIES, Feed.LOCAL),
        compiler_params=comm_params(1, 62),
        name="mixer_fwd",
    )(normed, weight, cot, w_out, w_down, out_side, f_side, dcol, drow, taps, gain)


def mixer_bwd_kernel(
    heads, chunks, source, partial, early, normed, weight, cot, q_side, values, up,
    dcol, drow, taps, gain, grad, o_in, t_in, d_in, s_in, tokens, grad_middle, down, attn_gain,
    chosen, layer_out, input_grad, early_whole, up_whole, low_whole,
    joined, e_s, f_s, w_s, x_s, ds_s, go_s, dj_s, side_v, weight_v, sem,
    total, own, stage, relay, away, back, early_pieces, early_sum, early_ring,
    back_partial, stage2, relay2, away2, back2, inner, inners, sides,
    up_pieces, up_sum, low_pieces, low_sum,
    send, recv, local,
):
    loads = [
        pltpu.make_async_copy(source, joined.at[pl.ds(PAD, source.shape[0]), :], sem.at[0]),
        pltpu.make_async_copy(weight, weight_v, sem.at[1]),
        pltpu.make_async_copy(
            normed.at[:, pl.ds(normed.shape[1] - SIDE, SIDE)], side_v, sem.at[2]
        ),
    ]
    for copy in loads:
        copy.start()
    greet(all_seq(), line_peers())
    line = Line(send, recv, local)
    ring = RingSum(line, partial, (own, stage, relay, away, back))
    sums = EarlySum(line, early, early_pieces, early_sum, early_ring)
    second_sum = RingSum(line, back_partial, (None, stage2, relay2, away2, back2))
    s, partner, _, _, _ = seq_places()
    f = lax.axis_index("fsdp")
    core = lax.rem(s, 2)
    inner_spread = Spread(line, "seq", 8, inner, lambda t: inners.at[t])
    up_ring = RingGather(line, up_sum, up_whole)
    low_ring = RingGather(line, low_sum, low_whole)

    def early_place(t, half, quarter):
        first = core * 4 + half * 2 + (quarter or 0)
        return early_whole.at[t, pl.ds(first, 2 if quarter is None else 1)]

    def piece_place(pieces):
        def place(t, half, quarter):
            first = half * 2 + (quarter or 0)
            return pieces.at[t, pl.ds(first, 2 if quarter is None else 1)]

        return place

    early_plane = PlaneGather(line, early_place)
    up_plane = PlaneGather(line, piece_place(up_pieces))
    low_plane = PlaneGather(line, piece_place(low_pieces))
    at, local_at = line.take(1, 3)
    half_slices = pl.ds(core * 4, 4)
    retain = line.local(local_at, early_ring.at[half_slices], early_whole.at[f, half_slices])
    share = line.copy(
        at, early_whole.at[:, half_slices], early_whole.at[:, half_slices], {"seq": partner}
    )
    part = sides.shape[1] // 2
    mine = pl.ds(pl.multiple_of(s * part, 128), part)
    fetch = [
        line.local(local_at + 1, normed.at[:, mine], sides.at[:, pl.ds(0, part)]),
        line.local(local_at + 2, cot.at[:, mine], sides.at[:, pl.ds(part, part)]),
    ]
    for copy in fetch:
        copy.start()
    ring.start()
    sums.start()
    joined[pl.ds(0, PAD), :] = jnp.zeros((PAD, joined.shape[1]), BF16)
    dj_s[pl.ds((chunks - 2) * CH, 2 * CH), :] = jnp.zeros((2 * CH, dj_s.shape[1]), BF16)
    for copy in loads:
        copy.wait()
    row = lax.broadcasted_iota(jnp.int32, (CH, CH), 0)
    col = lax.broadcasted_iota(jnp.int32, (CH, CH), 1)
    width = 3 * CH

    def revive(c):
        docs, same, live, tail, live_last = chunk_masks(c, dcol, drow)
        conv = conv_chunk(c, joined, dcol, taps, docs)
        raws = raw_chunk(c, joined, taps)
        return docs, same, live, tail, live_last, conv, raws

    def first(step, carry):
        pl.when(step == 2)(sums.plane.second)
        items = []
        for part in range(2):
            c = step * 2 + part
            docs, same, live, tail, live_last, conv, raws = revive(c)
            act = conv * sigmoid(conv)
            rows = pl.ds(pl.multiple_of(c * CH, CH), CH)
            for h in range(heads):
                query, keys, values, _, _ = normal_parts(act[:, h * width : (h + 1) * width])
                beta = sigmoid(raws[:, h : h + 1])
                out = o_in[h, rows, :]
                weighted = grad[rows, h * CH : (h + 1) * CH].astype(F32) * gain[...]
                scale = lax.rsqrt(jnp.mean(out * out, axis=-1, keepdims=True) + 1e-05)
                grad_o = scale * weighted - out * (
                    scale * scale * scale * jnp.mean(weighted * out, axis=-1, keepdims=True)
                )
                go_s[h, rows, :] = grad_o
                x_s[h, rows, :] = keys * tail
                known = (keys * (beta * live)).astype(BF16)
                items.append((h, rows, same, query, keys, (query * live), grad_o, known))
        scores = [mm_nt(query, keys) for _, _, _, query, keys, _, _, _ in items]
        recalls = [mm(t_in[h, rows, :], known) for h, rows, _, _, _, _, _, known in items]
        scores = [
            jnp.where(item[2] & (row >= col), score, 0.0) for item, score in zip(items, scores)
        ]
        both = [
            mm_tn(jnp.concatenate([score, item[5]], axis=1), item[6])
            for item, score in zip(items, scores)
        ]
        for (h, rows, *_), ef, recall in zip(items, both, recalls):
            e_s[h, rows, :] = ef[:CH]
            f_s[h, rows, :] = ef[CH:]
            w_s[h, rows, :] = recall.astype(BF16)
        return carry

    lax.fori_loop(0, chunks // 2, first, 0)
    ring.middle()
    sums.plane.third()

    def second(step, states):
        c = chunks - 1 - step
        rows = pl.ds(pl.multiple_of(c * CH, CH), CH)
        docs, same, live, tail, live_last = chunk_masks(c, dcol, drow)
        for h in range(heads):
            ds_s[h, rows, :] = states[h]
        passed = [mm(x_s[h, rows, :], states[h]) for h in range(heads)]
        grads = [e_s[h, rows, :] + passed[h] for h in range(heads)]
        taken = [mm_tn(w_s[h, rows, :], grads[h]) for h in range(heads)]
        for h in range(heads):
            x_s[h, rows, :] = grads[h]
        return tuple(
            states[h] * live_last + f_s[h, rows, :] - taken[h] for h in range(heads)
        )

    zero = jnp.zeros((CH, CH), F32)
    lax.fori_loop(0, chunks, second, (zero,) * heads)

    sums.plane.fourth()

    def project(c):
        rows = pl.ds(pl.multiple_of(c * CH, CH), CH)
        grads = dj_s[rows, :]
        back_partial[c] = mm_nt(grads, weight_v[...]).astype(BF16)

    def send_near(chip, ready):
        for k, d in enumerate((2, 1, 3, 0)):
            here = ready & (lax.rem(s // 2 + d, 4) == chip)
            pl.when(here)(lambda: second_sum.near(k).start())

    def third(step, after):
        pl.when(step == 0)(sums.add)
        pl.when(step == 1)(ring.last)
        pl.when(step == 1)(sums.ring.middle)

        @pl.when(step == 2)
        def _():
            sums.ring.finish()
            retain.start()
            retain.wait()
            early_plane.first()

        pl.when(step == 3)(early_plane.second)
        later = chunks - 1 - 2 * step
        for part in range(2):
            project(jnp.minimum(later + 2 - part, chunks - 1 - part))
        send_near(jnp.minimum(later + 1, chunks) // 2, step > 0)
        chunk_items, items = [], []
        for part in range(2):
            c = later - part
            docs, same, live, tail, live_last, conv, raws = revive(c)
            gate = sigmoid(conv)
            act = conv * gate
            slope = gate * (1.0 + conv * (1.0 - gate))
            rows = pl.ds(pl.multiple_of(c * CH, CH), CH)
            chunk_items.append((c, rows, slope))
            for h in range(heads):
                cut = act[:, h * width : (h + 1) * width]
                beta = sigmoid(raws[:, h : h + 1])
                items.append((h, rows, same, live, tail, beta, cut) + normal_parts(cut))
        targets = [mm_tn(t_in[h, rows, :], x_s[h, rows, :]) for h, rows, *_ in items]
        pairs = [
            mm_nt(jnp.concatenate([target, go_s[h, rows, :]], axis=0), d_in[h, rows, :])
            for (h, rows, *_), target in zip(items, targets)
        ]
        backs = [
            mm_nt(
                jnp.concatenate([go_s[h, rows, :] * live, -target * (beta * live)], axis=0),
                s_in[h, rows, :],
            )
            for (h, rows, _, live, _, beta, *_), target in zip(items, targets)
        ]
        inners = [mm_nt(item[8], item[8]) for item in items]
        recalls = [mm(item[8], s_in[item[0], item[1], :]) for item in items]
        ends = [
            mm_nt(d_in[h, rows, :].astype(F32) * tail, ds_s[h, rows, :])
            for h, rows, _, _, tail, *_ in items
        ]
        lowers = [
            jnp.where(item[2] & (row > col), -pair[:CH], 0.0) for item, pair in zip(items, pairs)
        ]
        scores = [
            jnp.where(item[2] & (row >= col), pair[CH:], 0.0) for item, pair in zip(items, pairs)
        ]
        grad_inners = [lower * item[5] for item, lower in zip(items, lowers)]
        turned = [
            mm_tn(
                jnp.concatenate([score, grad_inner], axis=0),
                jnp.concatenate([item[7], item[8]], axis=0),
            )
            for item, score, grad_inner in zip(items, scores, grad_inners)
        ]
        straight = [
            mm(jnp.concatenate([score, grad_inner], axis=0), item[8])
            for item, score, grad_inner in zip(items, scores, grad_inners)
        ]
        lane = lax.broadcasted_iota(jnp.int32, (CH, CH), 1)
        for part, (c, rows, slope) in enumerate(chunk_items):
            grads, grad_raw = [], jnp.zeros((CH, CH), F32)
            for h in range(heads):
                k = part * heads + h
                _, _, _, live, _, beta, cut, query, keys, values, q_scale, k_scale = items[k]
                target, back = targets[k], backs[k]
                grad_beta = jnp.sum(
                    lowers[k] * inners[k] + target * (values - live * recalls[k]),
                    axis=-1,
                    keepdims=True,
                )
                grad_query = (back[:CH] + straight[k][:CH]) * CH**-0.5
                grad_keys = back[CH:] + turned[k] + straight[k][CH:] + ends[k]
                raw_q, raw_k = cut[:, :CH], cut[:, CH : 2 * CH]
                grad_q = q_scale * grad_query - raw_q * (
                    q_scale * q_scale * q_scale
                    * jnp.sum(grad_query * raw_q, axis=-1, keepdims=True)
                )
                grad_k = k_scale * grad_keys - raw_k * (
                    k_scale * k_scale * k_scale
                    * jnp.sum(grad_keys * raw_k, axis=-1, keepdims=True)
                )
                grads += [grad_q, grad_k, target * beta]
                grad_raw = jnp.where(lane == h, grad_beta * beta * (1.0 - beta), grad_raw)
            dj_s[rows, heads * width :] = grad_raw.astype(BF16)
            grads = jnp.concatenate(grads, axis=1) * slope
            window = jnp.concatenate([grads, after], axis=0)
            ids = dcol[pl.ds(pl.multiple_of(c * CH + PAD, PAD), CH + PAD), :]
            total_ = grads * taps[3:4, :]
            for lag in (1, 2, 3):
                keep = (ids[lag : lag + CH] == ids[:CH]).astype(F32)
                keep = jnp.concatenate([keep] * (heads * 3), axis=1)
                total_ = total_ + window[lag : lag + CH] * keep * taps[3 - lag : 4 - lag, :]
            dj_s[rows, : heads * width] = total_.astype(BF16)
            after = grads[:8]
        return after

    lax.fori_loop(0, chunks // 2, third, jnp.zeros((8, heads * width), F32))
    project(1)
    project(0)
    send_near(0, s >= 0)
    rank, n = inner.shape[1:]

    def put(pieces, piece):
        size = pieces.shape[3]
        for q in range(4):
            pieces[f, q] = piece[:, q * size : (q + 1) * size]

    up_piece = mm_tn(side_v[...], dj_s[:, : heads * width])[rank : 2 * rank].astype(BF16)
    put(up_pieces, jnp.concatenate([up_piece, chosen[...], chosen[...]], axis=1))
    up_plane.first()
    ring.finish(total)
    across = values.shape[1]
    q_inner = mm_nt(q_side[...], dj_s[...])[rank : 2 * rank].astype(BF16)
    f_inner = total[:, across:].T[:rank].astype(BF16)
    inner[0] = q_inner[:, :n]
    rest = 2 * n - q_inner.shape[1] - f_inner.shape[1]
    inner[1] = jnp.concatenate([q_inner[:, n:], f_inner, jnp.zeros((rank, rest), BF16)], axis=1)
    inner_spread.start()
    second_sum.middle()
    early_plane.third()
    up_plane.second()

    def layer_rows(rows):
        inner = total[rows, across:].astype(BF16)
        layer_out[rows, :] = (
            values[rows, :] + (total[rows, :across] + mm(inner, up[...]))
        ).astype(BF16)

    by_rows(values.shape[0], layer_rows)
    for copy in fetch:
        copy.wait()
    inner_spread.arrive()
    tokens_here = tokens.shape[0]
    ahead = sides.shape[0] - n
    added, beside = [None, None], []
    for t in range(inners.shape[0]):
        parts = inners[t, 0].astype(F32), inners[t, 1].astype(F32)[:, :ahead]
        added = [p if sum_ is None else sum_ + p for p, sum_ in zip(parts, added)]
        beside.append(inners[t, 1][:, ahead : ahead + tokens_here])
    down_piece = mm(jnp.concatenate(added, axis=1), sides[:, :part])
    ff_piece = mm(jnp.concatenate(beside, axis=1), sides[:, part:])
    put(low_pieces, jnp.concatenate([down_piece, ff_piece], axis=1).astype(BF16))
    low_plane.first()
    up_plane.third()
    second_sum.last()
    low_plane.second()
    up_plane.fourth()
    early_plane.fourth()
    up_plane.finish()
    marks = up_pieces.at[:, 3]
    by_adapter(up_pieces, marks, 0, up_sum)
    up_ring.start()
    low_plane.third()
    low_plane.fourth()
    early_plane.finish()
    share.start()
    low_plane.finish()
    by_adapter(low_pieces, marks, 0, low_sum)
    low_ring.start()
    second_sum.finish(total)

    def input_rows(rows):
        grad_normed = total[rows, :across] + mm(total[rows, across:], down[...])
        input_grad[rows, :] = (
            grad_middle[rows, :]
            + norm_back_rows(tokens[rows, :].astype(F32), attn_gain[...], grad_normed)
        ).astype(BF16)

    by_rows(tokens_here, input_rows)
    up_ring.middle()
    low_ring.middle()
    up_ring.finish()
    low_ring.finish()
    share.wait()
    inner_spread.finish()


def mixer_bwd(
    joined, partial, early, normed, weight, cot, q_side, values, up, dcol, drow, taps, gain,
    grad, o, t, d, s, tokens, grad_middle, down, attn_gain, chosen, count,
):
    length, wide = joined.shape
    heads = wide // (3 * CH)
    chunks = length // CH
    square = (heads, length, CH)
    rows, across = values.shape
    seq, fsdp, rank = lax.axis_size("seq"), 16, early.shape[2]
    part = across // seq
    columns = heads * 3 * CH
    out = lambda *shape: jax.ShapeDtypeStruct(shape, BF16)
    bf16 = lambda *shape: pltpu.VMEM(shape, BF16)
    f32 = lambda *shape: pltpu.VMEM(shape, F32)
    buffers = sum_buffers(rows, across + SIDE)
    copies = 2 * RingSum.COPIES + EarlySum.COPIES + 2 * RingGather.COPIES + 3 * PlaneGather.COPIES
    return pl.pallas_call(
        functools.partial(mixer_bwd_kernel, heads, chunks),
        out_shape=(
            out(rows, across), out(rows, across),
            out(fsdp, seq, *early.shape[1:]),
            out(seq, count, rank, columns), out(seq, count, rank, 2 * part),
        ),
        in_specs=[ANY] * 6 + [VMEM] * 17,
        out_specs=(VMEM, VMEM, ANY, ANY, ANY),
        scratch_shapes=[
            bf16(length + PAD, wide), f32(*square), f32(*square), bf16(*square), f32(*square),
            f32(*square), f32(*square), bf16(length, wide), bf16(length, SIDE),
            bf16(*weight.shape), pltpu.SemaphoreType.DMA((3,)), f32(rows, across + SIDE),
        ]
        + buffers
        + [
            bf16(fsdp, *early.shape), bf16(*early.shape[1:]), bf16(seq, *early.shape[1:]),
            bf16(seq, rows, across + SIDE),
        ]
        + buffers[1:]
        + [
            bf16(2, rank, 640), bf16(seq, 2, rank, 640), bf16(length, 2 * part),
            bf16(fsdp, 4, rank, (columns + 2 * SIDE) // 4), bf16(count, rank, columns),
            bf16(fsdp, 4, rank, part // 2), bf16(count, rank, 2 * part),
        ]
        + sems(copies + 7 + 1, 2 * RingSum.LOCAL + EarlySum.LOCAL + 3 + 3),
        compiler_params=comm_params(4, 60),
        name="mixer_bwd",
    )(
        joined, partial, early, normed, weight, cot, q_side, values, up, dcol, drow, taps, gain,
        grad, o, t, d, s, tokens, grad_middle, down, attn_gain, chosen,
    )

MESH = pl.DeviceIdType.MESH
SIDE = 128
ANY = pl.BlockSpec(memory_space=pl.ANY)
VMEM = pl.BlockSpec(memory_space=pltpu.VMEM)
SMEM = pl.BlockSpec(memory_space=pltpu.SMEM)


class Line:
    def __init__(self, send_sems, recv_sems, local_sems):
        self.send_sems, self.recv_sems, self.local_sems = send_sems, recv_sems, local_sems
        self.used, self.used_local = 0, 0

    def take(self, copies, local=0):
        at = self.used, self.used_local
        self.used += copies
        self.used_local += local
        return at

    def copy(self, at, src, dst, device):
        return pltpu.make_async_remote_copy(
            src_ref=src, dst_ref=dst, send_sem=self.send_sems.at[at],
            recv_sem=self.recv_sems.at[at], device_id=device, device_id_type=MESH,
        )

    def local(self, at, src, dst):
        return pltpu.make_async_copy(src, dst, self.local_sems.at[at])


def sems(copies, local):
    return [
        pltpu.SemaphoreType.DMA((copies,)),
        pltpu.SemaphoreType.DMA((copies,)),
        pltpu.SemaphoreType.DMA((local,)),
    ]


def seq_places():
    s = lax.axis_index("seq")
    x, core = s // 2, lax.rem(s, 2)
    there = lambda d: lax.rem(x + d, 4) * 2 + core
    return s, x * 2 + 1 - core, there(1), there(3), there(2)


def plane_places():
    f = lax.axis_index("fsdp")
    return f, f // 4, lax.rem(f, 4)


def ring_peers():
    s, partner, right, left, far = seq_places()
    return [partner, right, left]


def all_seq():
    s = lax.axis_index("seq")
    return [lax.rem(s + d, 8) for d in range(1, 8)]


def all_plane():
    f = lax.axis_index("fsdp")
    return [lax.rem(f + d, 16) for d in range(1, 16)]


def line_peers():
    f, y, z = plane_places()
    return [y * 4 + lax.rem(z + d, 4) for d in (1, 3)] + [
        lax.rem(y + d, 4) * 4 + z for d in (1, 3)
    ]


def greet(seq_peers, plane_peers):
    barrier = pltpu.get_barrier_semaphore()
    for p in seq_peers:
        pl.semaphore_signal(barrier, inc=1, device_id={"seq": p}, device_id_type=MESH)
    for p in plane_peers:
        pl.semaphore_signal(barrier, inc=1, device_id={"fsdp": p}, device_id_type=MESH)
    pl.semaphore_wait(barrier, len(seq_peers) + len(plane_peers))


class RingGather:
    COPIES, LOCAL = 13, 1

    def __init__(self, line, block, out, first=0, rows=None):
        self.line, self.placed, self.out = line, block is None, out
        self.block = out.at[lax.axis_index("seq")] if self.placed else block
        rows = rows or self.block.shape[0]
        half = rows // 2
        self.low, self.high = pl.ds(first, half), pl.ds(first + half, half)
        self.all = pl.ds(first, rows)
        self.at, self.local_at = line.take(self.COPIES, self.LOCAL)

    def mine(self, i, rows, peer):
        s = lax.axis_index("seq")
        return self.line.copy(
            self.at + i, self.block.at[rows], self.out.at[s, rows], {"seq": peer}
        )

    def pass_on(self, i, s, rows, peer):
        ref = self.out.at[s, rows]
        return self.line.copy(self.at + i, ref, ref, {"seq": peer})

    def copy(self, i):
        s, partner, right, left, far = seq_places()
        low, high = self.low, self.high
        if i < 4:
            return self.mine(i, *((low, right), (high, left), (high, right), (low, left))[i])
        if i == 4:
            return self.mine(4, self.all, partner)
        return self.pass_on(
            i,
            *(
                (left, low, right), (left, low, partner), (right, high, left),
                (right, high, partner), (left, high, partner), (right, low, partner),
                (far, low, partner), (far, high, partner),
            )[i - 5],
        )

    def own(self):
        s = lax.axis_index("seq")
        return self.line.local(self.local_at, self.block, self.out.at[s])

    def start(self):
        for i in range(5):
            self.copy(i).start()
        if not self.placed:
            self.own().start()

    def middle(self):
        for arrived, onward in ((0, (5, 6)), (1, (7, 8)), (2, (9,)), (3, (10,))):
            self.copy(arrived).wait_recv()
            for i in onward:
                self.copy(i).start()

    def finish(self):
        self.copy(5).wait_recv()
        self.copy(11).start()
        self.copy(7).wait_recv()
        self.copy(12).start()
        for i in (0, 1, 2, 3, 5, 7):
            self.copy(i).wait_send()
        for i in (4, 6, 8, 9, 10, 11, 12):
            self.copy(i).wait()
        if not self.placed:
            self.own().wait()

    def reach(self, step):
        @pl.when(step == 0)
        def _():
            self.copy(4).wait_recv()

        @pl.when(step == 1)
        def _():
            self.middle()
            self.copy(8).wait_recv()
            self.copy(10).wait_recv()

        @pl.when(step == 2)
        def _():
            self.copy(6).wait_recv()
            self.copy(9).wait_recv()

        @pl.when(step == 3)
        def _():
            self.copy(5).wait_recv()
            self.copy(11).start()
            self.copy(7).wait_recv()
            self.copy(12).start()
            self.copy(11).wait_recv()
            self.copy(12).wait_recv()

    def sent(self):
        for i in range(self.COPIES):
            self.copy(i).wait_send()


class PlaneGather:
    COPIES, LOCAL = 40, 0

    def __init__(self, line, place):
        self.line, self.place = line, place
        self.at, _ = line.take(self.COPIES)

    def by(self, half, along, across):
        f, y, z = plane_places()
        dy, dz = (across, along) if half == 0 else (along, across)
        return lax.rem(y + dy + 4, 4) * 4 + lax.rem(z + dz + 4, 4)

    def send(self, at, ref, peer):
        return self.line.copy(self.at + at, ref, ref, {"fsdp": peer})

    def one(self, half, i):
        ref = self.place(lax.axis_index("fsdp"), half, None)
        return self.send(half * 20 + i, ref, self.by(half, (1, -1)[i], 0))

    def one_on(self, half, i):
        d = (1, -1)[i]
        ref = self.place(self.by(half, -d, 0), half, i)
        return self.send(half * 20 + 2 + i, ref, self.by(half, d, 0))

    def two(self, half, k, i):
        ref = self.place(self.by(half, (0, -1, 1, 2)[k], 0), half, None)
        return self.send(half * 20 + 4 + k * 2 + i, ref, self.by(half, 0, (1, -1)[i]))

    def two_on(self, half, k, i):
        d = (1, -1)[i]
        ref = self.place(self.by(half, (0, -1, 1, 2)[k], -d), half, i)
        return self.send(half * 20 + 12 + k * 2 + i, ref, self.by(half, 0, d))

    def first(self):
        for half in (0, 1):
            for i in (0, 1):
                self.one(half, i).start()

    def second(self):
        for half in (0, 1):
            for i in (0, 1):
                self.two(half, 0, i).start()
        for half in (0, 1):
            for i in (0, 1):
                self.one(half, i).wait_recv()
                self.one_on(half, i).start()
                for j in (0, 1):
                    self.two(half, 1 + i, j).start()

    def third(self):
        for half in (0, 1):
            for i in (0, 1):
                self.one_on(half, i).wait_recv()
            for i in (0, 1):
                self.two(half, 3, i).start()
        for k in range(3):
            for half in (0, 1):
                self.cross(half, k)

    def cross(self, half, k):
        for i in (0, 1):
            self.two(half, k, i).wait_recv()
            self.two_on(half, k, i).start()

    def fourth(self):
        for half in (0, 1):
            self.cross(half, 3)

    def finish(self):
        for half in (0, 1):
            for i in (0, 1):
                self.one(half, i).wait_send()
                self.one_on(half, i).wait_send()
                for k in range(4):
                    self.two(half, k, i).wait_send()
                    self.two_on(half, k, i).wait()


class Scatter:
    COPIES, LOCAL = 17, 2

    def __init__(self, line, sources, source_block, into):
        self.line, self.sources = line, sources
        self.source_block, self.into = source_block, into
        self.at, self.local_at = line.take(self.COPIES, self.LOCAL)

    def copy(self, j, d):
        f, _, _ = plane_places()
        t = lax.rem(f + d, 16)
        line = self.line
        return pltpu.make_async_remote_copy(
            src_ref=self.source_block(t), dst_ref=self.into(t, j),
            send_sem=line.send_sems.at[self.at + d], recv_sem=line.recv_sems.at[self.at + j],
            device_id={"fsdp": t}, device_id_type=MESH,
        )

    def keep(self, j):
        f, _, _ = plane_places()
        return self.line.local(self.local_at + j, self.source_block(f), self.into(f, j))

    def start(self):
        f, _, _ = plane_places()
        for j, source in enumerate(self.sources):
            @pl.when(f == source)
            def _():
                for d in range(1, 16):
                    self.copy(j, d).start()
                self.keep(j).start()

    def arrive(self):
        f, _, _ = plane_places()
        for j, source in enumerate(self.sources):
            @pl.when(f == source)
            def _():
                self.keep(j).wait()

            @pl.when(f != source)
            def _():
                ref = self.into(f, j)
                pltpu.make_async_remote_copy(
                    src_ref=ref, dst_ref=ref, send_sem=self.line.send_sems.at[self.at],
                    recv_sem=self.line.recv_sems.at[self.at + j],
                    device_id={"fsdp": lax.rem(f + 1, 16)}, device_id_type=MESH,
                ).wait_recv()

    def finish(self):
        f, _, _ = plane_places()
        for j, source in enumerate(self.sources):
            @pl.when(f == source)
            def _():
                for d in range(1, 16):
                    self.copy(j, d).wait_send()


class Spread:
    def __init__(self, line, axis, count, block, slot):
        self.line, self.axis, self.count, self.block, self.slot = line, axis, count, block, slot
        self.at, self.local_at = line.take(count - 1, 1)

    def copy(self, d):
        me = lax.axis_index(self.axis)
        return self.line.copy(
            self.at + d - 1, self.block, self.slot(me), {self.axis: lax.rem(me + d, self.count)}
        )

    def own(self):
        return self.line.local(self.local_at, self.block, self.slot(lax.axis_index(self.axis)))

    def start(self):
        for d in range(1, self.count):
            self.copy(d).start()
        self.own().start()

    def arrive(self):
        for d in range(1, self.count):
            self.copy(d).wait_recv()
        self.own().wait()

    def finish(self):
        for d in range(1, self.count):
            self.copy(d).wait_send()


def rows_of(total, half, quarter):
    if quarter is None:
        return pl.ds(half * (total // 2), total // 2)
    return pl.ds(half * (total // 2) + quarter * (total // 4), total // 4)


def columns_place(out):
    return lambda f, half, quarter: out.at[
        rows_of(out.shape[0], half, quarter), pl.ds(pl.multiple_of(f * 128, 128), 128)
    ]


def block_of(ref, t):
    return ref.at[:, pl.ds(pl.multiple_of(t * 128, 128), 128)]


ADD_ROWS = 16


def add_rows(dst, sources, first, count):
    def step(i, carry):
        rows = pl.ds(pl.multiple_of(first + i * ADD_ROWS, ADD_ROWS), ADD_ROWS)
        total = None
        for source, offset in sources:
            at = pl.ds(pl.multiple_of(first - offset + i * ADD_ROWS, ADD_ROWS), ADD_ROWS)
            item = source[at, :].astype(F32)
            total = item if total is None else total + item
        dst[rows, :] = total.astype(dst.dtype)
        return carry

    lax.fori_loop(0, count // ADD_ROWS, step, 0)


class RingSum:
    COPIES, LOCAL = 10, 4

    def __init__(self, line, partial, buffers, first=0):
        self.line, self.partial, self.first = line, partial, first
        self.own, self.stage, self.relay, self.away, self.back = buffers
        self.rows = self.stage.shape[1]
        self.block = pl.ds(first, self.rows)
        self.half = self.rows // 2
        self.low, self.high = pl.ds(0, self.half), pl.ds(self.half, self.half)
        self.at, self.local_at = line.take(self.COPIES, self.LOCAL)

    def near(self, k):
        s, partner, right, left, far = seq_places()
        p = (far, right, left, s)[k]
        return self.line.copy(
            self.at + k, self.partial.at[p + partner - s, self.block], self.stage.at[k],
            {"seq": partner},
        )

    def kept(self, k):
        s, partner, right, left, far = seq_places()
        p = (far, right, left, s)[k]
        return self.line.local(self.local_at + k, self.partial.at[p, self.block], self.own.at[k])

    def go(self, i):
        s, partner, right, left, far = seq_places()
        away, relay, back, low, high = self.away, self.relay, self.back, self.low, self.high
        src, dst, peer = (
            (away.at[0, low], relay.at[0], right),
            (away.at[0, high], relay.at[1], left),
            (away.at[1, high], back.at[0, high], right),
            (away.at[2, low], back.at[1, low], left),
            (away.at[1, low], back.at[0, low], right),
            (away.at[2, high], back.at[1, high], left),
        )[i]
        return self.line.copy(self.at + 4 + i, src, dst, {"seq": peer})

    def start(self):
        for k in range(4):
            self.near(k).start()
            if self.own is not None:
                self.kept(k).start()

    def ready(self, k):
        self.near(k).wait_recv()
        if self.own is not None:
            self.kept(k).wait()

    def pair(self, k):
        if self.own is not None:
            return [(self.own.at[k], 0), (self.stage.at[k], 0)]
        s, partner, right, left, far = seq_places()
        return [(self.partial.at[(far, right, left, s)[k]], -self.first), (self.stage.at[k], 0)]

    def far(self):
        half, away = self.half, self.away
        self.ready(0)
        add_rows(away.at[0], self.pair(0), 0, half)
        self.go(0).start()
        add_rows(away.at[0], self.pair(0), half, half)
        self.go(1).start()

    def beside(self, k):
        half = self.half
        self.ready(k)
        add_rows(self.away.at[k], self.pair(k), half if k == 1 else 0, half)
        self.go(1 + k).start()

    def middle(self):
        self.far()
        self.beside(1)
        self.beside(2)

    def send_step(self, step):
        @pl.when(step == 0)
        def _():
            self.near(3).start()

        @pl.when(step == 1)
        def _():
            self.near(1).start()

        @pl.when(step == 2)
        def _():
            self.near(2).start()
            self.beside(1)

        @pl.when(step == 3)
        def _():
            self.near(0).start()
            self.beside(2)

    def last(self):
        half, away, relay = self.half, self.away, self.relay
        self.go(0).wait_recv()
        add_rows(away.at[1], self.pair(1) + [(relay.at[0], 0)], 0, half)
        self.go(4).start()
        self.go(1).wait_recv()
        add_rows(away.at[2], self.pair(2) + [(relay.at[1], half)], half, half)
        self.go(5).start()

    def finish(self, total):
        self.ready(3)
        for i in (2, 3, 4, 5):
            self.go(i).wait_recv()
        sources = self.pair(3) + [(self.back.at[0], 0), (self.back.at[1], 0)]
        add_rows(total.at[self.block], sources, 0, self.rows)
        for k in range(4):
            self.near(k).wait_send()
        for i in range(6):
            self.go(i).wait_send()


def sum_buffers(rows, width):
    return [
        pltpu.VMEM((4, rows, width), BF16),
        pltpu.VMEM((4, rows, width), BF16),
        pltpu.VMEM((2, rows // 2, width), BF16),
        pltpu.VMEM((3, rows, width), BF16),
        pltpu.VMEM((2, rows, width), BF16),
    ]


MID_ROWS = 32


def by_rows(rows, step, first=0):
    def run(i, carry):
        step(pl.ds(pl.multiple_of(first + i * MID_ROWS, MID_ROWS), MID_ROWS))
        return carry

    lax.fori_loop(0, rows // MID_ROWS, run, 0)


def norm_back_rows(values, gain, grad):
    scale = lax.rsqrt(jnp.mean(values * values, axis=-1, keepdims=True) + 1e-05)
    weighted = grad * gain
    return scale * weighted - values * (
        scale * scale * scale * jnp.mean(weighted * values, axis=-1, keepdims=True)
    )


def comm_params(cid, limit=48):
    return pltpu.CompilerParams(
        collective_id=cid, has_side_effects=True, vmem_limit_bytes=limit << 20
    )


def start_kernel(
    payload, w_qkv, gate_t, q_side, beta_side, everyone, wq, blocks, send, recv, local
):
    s = lax.axis_index("seq")
    greet(ring_peers(), all_plane())
    line = Line(send, recv, local)
    depth, width = w_qkv.shape
    scatter = Scatter(
        line, (2 * s, 2 * s + 1),
        lambda t: w_qkv.at[pl.ds(t * 128, 128), :],
        lambda t, j: wq.at[pl.ds(t * 128, 128), pl.ds(j * width, width)],
    )
    others = [
        Scatter(line, (s + 8 * i,), lambda t: block_of(gate_t, t), lambda t, j, i=i: blocks.at[i])
        for i in (0, 1)
    ]
    ring = RingGather(line, payload, everyone)
    _, at = line.take(0, 2)
    sides = [
        line.local(at, q_side, wq.at[pl.ds(depth, SIDE), :]),
        line.local(at + 1, beta_side, wq.at[pl.ds(0, depth), pl.ds(2 * width, SIDE)]),
    ]

    def place(t, half, quarter):
        size = 64 if quarter is None else 32
        return wq.at[
            pl.ds(t * 128 + half * 64 + (quarter or 0) * 32, size), pl.ds(0, 2 * width)
        ]

    qkv = PlaneGather(line, place)
    scatter.start()
    ring.start()
    for copy in sides:
        copy.start()
    scatter.arrive()
    qkv.first()
    qkv.second()
    ring.middle()
    qkv.third()
    for item in others:
        item.start()
    qkv.fourth()
    ring.finish()
    qkv.finish()
    for item in others:
        item.arrive()
    for item in [scatter] + others:
        item.finish()
    for copy in sides:
        copy.wait()


def start_gather(payload, w_qkv, gate_t, q_side, beta_side):
    seq, wide = lax.axis_size("seq"), payload.shape[1]
    copies = RingGather.COPIES + 3 * Scatter.COPIES + PlaneGather.COPIES
    return pl.pallas_call(
        start_kernel,
        out_shape=(
            jax.ShapeDtypeStruct((seq,) + payload.shape, BF16),
            jax.ShapeDtypeStruct((wide, q_side.shape[1]), BF16),
            jax.ShapeDtypeStruct((2, gate_t.shape[0], 128), BF16),
        ),
        in_specs=[ANY] * 5,
        out_specs=(ANY,) * 3,
        scratch_shapes=sems(copies, 10),
        compiler_params=comm_params(0, 62),
        name="start_gather",
    )(payload, w_qkv, gate_t, q_side, beta_side)


class Feed:
    COPIES = RingGather.COPIES + 2 * PlaneGather.COPIES
    LOCAL = RingGather.LOCAL + 4

    def __init__(self, line, cot, sources, sides, everyone, outs):
        self.line, self.sources, self.sides, self.outs = line, sources, sides, outs
        self.ring = RingGather(line, cot, everyone)
        self.gathers = [PlaneGather(line, columns_place(o)) for o in outs]
        _, self.at = line.take(0, 4)

    def place(self, i):
        s, f = lax.axis_index("seq"), lax.axis_index("fsdp")
        out = self.outs[i % 2]
        if i < 2:
            share = out.shape[0]
            src = self.sources[i].at[pl.ds(pl.multiple_of(s * share, 16), share), :]
            dst = block_of(out, f)
        else:
            src, dst = self.sides[i - 2], out.at[:, pl.ds(out.shape[1] - SIDE, SIDE)]
        return self.line.local(self.at + i, src, dst)

    def start(self):
        for i in range(4):
            self.place(i).start()
        self.ring.start()
        for i, gather in enumerate(self.gathers):
            self.place(i).wait()
            gather.first()

    def stage(self, step):
        @pl.when(step == 1)
        def _():
            for gather in self.gathers:
                gather.second()

        @pl.when(step == 3)
        def _():
            for gather in self.gathers:
                gather.third()
            self.ring.middle()

    def third(self):
        for gather in self.gathers:
            gather.fourth()

    def fourth(self):
        self.gathers[0].finish()
        self.place(2).wait()

    def finish(self):
        self.ring.finish()
        self.gathers[1].finish()
        self.place(3).wait()


def chip_at(step):
    x = lax.axis_index("seq") // 2
    d = jnp.where(step == 2, 3, jnp.where(step == 3, 2, step))
    return lax.rem(x + d, 4)


def feed_forward_kernel(
    partial, blocks, g_side, u_side, wd_in, cot_in,
    tokens, cot, mixed, wo, up, gain, down, chosen,
    middle, grad_middle, partial_down, grad_mixed, early,
    rows2, rows3, cots, wg, wu, wd, partial2, total,
    gate_s, upper_s, hidden_s, gg_s, gu_s, gate_e, upper_e, down_e, *rest,
):
    greet(ring_peers(), line_peers())
    buffers, (send, recv, local) = rest[:-3], rest[-3:]
    line = Line(send, recv, local)
    s = lax.axis_index("seq")
    f = lax.axis_index("fsdp")
    rows = tokens.shape[0]
    firsts = (0, rows // 2)
    first_sum = [
        RingSum(line, partial, buffers[5 * i : 5 * i + 5], first)
        for i, first in enumerate(firsts)
    ]
    second_sum = [
        RingSum(line, partial2, (None,) + buffers[10 + 4 * i : 14 + 4 * i], first)
        for i, first in enumerate(firsts)
    ]
    first_gather = [RingGather(line, None, rows2, first, rows // 2) for first in firsts]
    second_gather = [RingGather(line, None, rows3, first, rows // 2) for first in firsts]
    weights = [PlaneGather(line, columns_place(o)) for o in (wg, wu)]
    width = tokens.shape[1]
    _, at = line.take(0, 6)
    mine = [line.local(at + i, blocks.at[i], block_of(o, f)) for i, o in enumerate((wg, wu))]
    others = [
        line.local(at + 2, g_side, wg.at[:, pl.ds(width, SIDE)]),
        line.local(at + 3, u_side, wu.at[:, pl.ds(width, SIDE)]),
        line.local(at + 4, wd_in, wd),
        line.local(at + 5, cot_in, cots),
    ]
    for copy in mine:
        copy.start()
    for item in first_sum:
        item.start()
    for copy, item in zip(mine, weights):
        copy.wait()
        item.first()
    for copy in others:
        copy.start()
    for item in first_sum:
        item.middle()
    for item in weights:
        item.second()
    for item in first_sum:
        item.last()

    def norm_rows(rows):
        inner = total[rows, width:].astype(BF16)
        value = tokens[rows, :].astype(F32) + (total[rows, :width] + mm(inner, up[...]))
        middle[rows, :] = value
        scale = lax.rsqrt(jnp.mean(value * value, axis=-1, keepdims=True) + 1e-05)
        normed = (value * scale * gain[...]).astype(BF16)
        rows2[s, rows, :width] = normed
        rows2[s, rows, width:] = (inner.astype(F32) + mm_nt(normed, down[...])).astype(BF16)

    first_sum[0].finish(total)
    by_rows(rows // 2, norm_rows)
    first_gather[0].start()
    for item in weights:
        item.third()
    first_sum[1].finish(total)
    by_rows(rows // 2, norm_rows, rows // 2)
    first_gather[1].start()
    for item in weights:
        item.fourth()
    for item in weights:
        item.finish()
    for copy in others:
        copy.wait()
    pair = 2 * rows

    def chip(step, carry):
        for item in first_gather:
            item.reach(step)
        k = chip_at(step)
        both = pl.ds(k * 2, 2)
        normed = rows2[both].reshape(pair, width + SIDE)
        grads = cots[both].reshape(pair, width + SIDE)
        gate_s[...] = mm_nt(normed, wg[...])
        upper_s[...] = mm_nt(normed, wu[...])
        hidden = mm_nt(grads, wd[...])
        gate, upper = gate_s[...], upper_s[...]
        sigma = sigmoid(gate)
        silu = gate * sigma
        hidden_s[k] = (silu * upper).astype(BF16)
        gg_s[k] = (hidden * upper * sigma * (1.0 + gate * (1.0 - sigma))).astype(BF16)
        gu_s[k] = (hidden * silu).astype(BF16)
        partial2[both] = (
            (mm(gg_s[k], wg[...]) + mm(gu_s[k], wu[...]))
            .astype(BF16)
            .reshape(2, pair // 2, width + SIDE)
        )
        for item in second_sum:
            item.send_step(step)
        return carry

    lax.fori_loop(0, 4, chip, 0)
    for item in second_sum:
        item.far()
    for item in second_sum:
        item.last()

    def back_rows(rows):
        inner = total[rows, width:].astype(BF16)
        grad = total[rows, :width] + mm(inner, down[...])
        result = cot[rows, :].astype(F32) + norm_back_rows(middle[rows, :], gain[...], grad)
        grad_middle[rows, :] = result
        low = result.astype(BF16)
        rows3[s, rows, :width] = low
        rows3[s, rows, width:] = (inner.astype(F32) + mm_nt(low, up[...])).astype(BF16)

    second_sum[0].finish(total)
    by_rows(rows // 2, back_rows)
    second_gather[0].start()
    second_sum[1].finish(total)
    by_rows(rows // 2, back_rows, rows // 2)
    second_gather[1].start()
    gate_e[...] = jnp.zeros_like(gate_e)
    upper_e[...] = jnp.zeros_like(upper_e)
    down_e[...] = jnp.zeros_like(down_e)

    def down_project(k, carry):
        both = pl.ds(k * 2, 2)
        partial_down[both] = (
            mm(hidden_s[k], wd[...]).astype(BF16).reshape(2, rows, width + SIDE)
        )
        side = rows2[both, :, width:].reshape(pair, SIDE)
        gate_e[...] += mm_tn(side, gg_s[k])
        upper_e[...] += mm_tn(side, gu_s[k])
        down_e[...] += mm_tn(cots[both, :, width:].reshape(pair, SIDE), hidden_s[k])
        return carry

    lax.fori_loop(0, 4, down_project, 0)
    for item in first_gather:
        item.sent()

    def out_back(step, carry):
        for item in second_gather:
            item.reach(step)
        k = chip_at(step)
        grads = rows3[pl.ds(k * 2, 2)].reshape(pair, width + SIDE)
        grad_mixed[pl.ds(pl.multiple_of(k * pair, pair), pair), :] = mm_nt(grads, wo[...]).astype(
            BF16
        )
        return carry

    lax.fori_loop(0, 4, out_back, 0)
    rank = early.shape[2]
    part = mixed.shape[1]
    own_part = pl.ds(pl.multiple_of(s * part, 128), part)
    flat = lambda v: v.reshape(-1, v.shape[-1])
    side2, side3 = flat(rows2[:, :, width:]), flat(rows3[:, :, width:])
    first = [
        gate_e[rank : 2 * rank, :].astype(BF16),
        upper_e[rank : 2 * rank, :].astype(BF16),
        chosen[...],
    ]
    second = [
        mm_tn(side3, mixed[...])[:rank].astype(BF16),
        mm_tn(side2, flat(rows3[:, :, own_part]))[:rank].astype(BF16),
        mm_tn(side3, flat(rows2[:, :, own_part]))[rank : 2 * rank].astype(BF16),
        down_e[:rank, :].astype(BF16),
        chosen[:, : SIDE // 2],
    ]
    n = early.shape[3]
    for half, parts in enumerate((first, second)):
        piece = jnp.concatenate(parts, axis=1)
        early[half, 0] = piece[:, :n]
        early[half, 1] = piece[:, n:]
    for item in second_gather:
        item.sent()


def feed_forward(
    partial, blocks, g_side, u_side, wd, cots, tokens, cot, mixed, wo, up, gain, down, chosen
):
    seq, rows, wide = partial.shape
    share = g_side.shape[0]
    rank, part = chosen.shape[0], mixed.shape[1]
    whole = pltpu.VMEM((seq, rows, wide), BF16)
    weight = pltpu.VMEM((share, wide), BF16)
    buffers = sum_buffers(rows // 2, wide)
    f32_rows = pltpu.VMEM((2 * rows, share), F32)
    bf16_rows = pltpu.VMEM((seq // 2, 2 * rows, share), BF16)
    extra = pltpu.VMEM((SIDE, share), F32)
    return pl.pallas_call(
        feed_forward_kernel,
        out_shape=(
            jax.ShapeDtypeStruct((rows, wide - SIDE), F32),
            jax.ShapeDtypeStruct((rows, wide - SIDE), F32),
            jax.ShapeDtypeStruct((seq, rows, wide), BF16),
            jax.ShapeDtypeStruct((seq * rows, part), BF16),
            jax.ShapeDtypeStruct((2, 2, rank, share + SIDE // 2), BF16),
        ),
        in_specs=[ANY] * 6 + [VMEM] * 8,
        out_specs=(VMEM,) * 5,
        scratch_shapes=[whole, whole, whole, weight, weight, weight, whole]
        + [pltpu.VMEM((rows, wide), F32)]
        + [f32_rows, f32_rows, bf16_rows, bf16_rows, bf16_rows, extra, extra, extra]
        + buffers * 2
        + buffers[1:] * 2
        + sems(4 * RingSum.COPIES + 4 * RingGather.COPIES + 2 * PlaneGather.COPIES, 26),
        compiler_params=comm_params(2, 63),
        name="feed_forward",
    )(partial, blocks, g_side, u_side, wd, cots, tokens, cot, mixed, wo, up, gain, down, chosen)


class EarlySum:
    COPIES, LOCAL = PlaneGather.COPIES + RingGather.COPIES, 1 + RingGather.LOCAL

    def __init__(self, line, early, pieces, total, out):
        self.line, self.early, self.pieces, self.total = line, early, pieces, total
        _, self.local_at = line.take(0, 1)
        self.ring = RingGather(line, total, out)

        def place(f, half, quarter):
            return pieces.at[f, half] if quarter is None else pieces.at[f, half, quarter]

        self.plane = PlaneGather(line, place)

    def start(self):
        own = self.line.local(
            self.local_at, self.early, self.pieces.at[lax.axis_index("fsdp")]
        )
        own.start()
        own.wait()
        self.plane.first()

    def add(self):
        self.plane.finish()
        f = lax.axis_index("fsdp")
        half = lax.rem(f, 2)
        lane = lax.broadcasted_iota(jnp.int32, (1, SIDE), 1)
        mark = jnp.where(half == 0, 0, SIDE // 2) + f // 2
        totals = [None, None]
        for t in range(16):
            pair = [self.pieces[t, half, q].astype(F32) for q in (0, 1)]
            marks = pair[1][:1, -SIDE:]
            uses = jnp.sum(jnp.where(lane == mark, marks, 0.0), axis=1, keepdims=True)
            totals = [
                p * uses if total is None else total + p * uses for p, total in zip(pair, totals)
            ]
        self.total[0] = totals[0].astype(BF16)
        self.total[1] = totals[1].astype(BF16)
        self.ring.start()


def by_adapter(plane, marks, first, out):
    count, wide = out.shape[0], out.shape[2]
    fsdp, parts, _, n = plane.shape
    uses = [marks[f].astype(F32)[:1] for f in range(fsdp)]
    for q in range(parts):
        cut = min(n, wide - q * n)
        if cut <= 0:
            continue
        items = [plane[f, q].astype(F32)[:, :cut] for f in range(fsdp)]
        for a in range(count):
            total = None
            for f in range(fsdp):
                item = items[f] * uses[f][:, first + a : first + a + 1]
                total = item if total is None else total + item
            out[a, :, q * n : q * n + cut] = total.astype(BF16)


def lay_out_early(whole, share, part):
    fsdp, seq, _, rank, n = whole.shape
    count = fsdp // 2

    def kernel(whole, gateup, mix_down, mix_up, gu_down, ff_down):
        for t in range(seq):
            first = jnp.concatenate([whole[0, t, 0], whole[0, t, 1]], axis=1).astype(F32)
            gateup[0, :, t * share : (t + 1) * share] = first[:, :share]
            at = (seq + t) * share
            gateup[0, :, at : at + share] = first[:, share : 2 * share]
            second = jnp.concatenate([whole[1, t, 0], whole[1, t, 1]], axis=1).astype(F32)
            for i, out in enumerate((mix_down, mix_up, gu_down)):
                out[0, :, t * part : (t + 1) * part] = second[:, i * part : (i + 1) * part]
            ff_down[0, :, t * share : (t + 1) * share] = second[:, 3 * part : 3 * part + share]

    widths = (2 * share * seq,) + (part * seq,) * 3 + (share * seq,)
    return pl.pallas_call(
        kernel,
        grid=(count,),
        out_shape=tuple(jax.ShapeDtypeStruct((count, rank, w), F32) for w in widths),
        in_specs=[pl.BlockSpec((2, seq, 2, rank, n), lambda a: (a, 0, 0, 0, 0))],
        out_specs=tuple(pl.BlockSpec((1, rank, w), lambda a: (a, 0, 0)) for w in widths),
        compiler_params=pltpu.CompilerParams(vmem_limit_bytes=32 << 20),
        name="lay_out_early",
    )(whole)


def lay_out_late(up, low, part):
    seq, count, rank, columns = up.shape

    def kernel(up, low, qkv_up, qkv_down, ff_up):
        for t in range(seq):
            qkv_up[0, :, t * columns : (t + 1) * columns] = up[t, 0].astype(F32)
            qkv_down[0, :, t * part : (t + 1) * part] = low[t, 0, :, :part].astype(F32)
            ff_up[0, :, t * part : (t + 1) * part] = low[t, 0, :, part:].astype(F32)

    widths = (columns * seq, part * seq, part * seq)
    cut = lambda n: pl.BlockSpec((seq, 1, rank, n), lambda a: (0, a, 0, 0))
    return pl.pallas_call(
        kernel,
        grid=(count,),
        out_shape=tuple(jax.ShapeDtypeStruct((count, rank, w), F32) for w in widths),
        in_specs=[cut(columns), cut(2 * part)],
        out_specs=tuple(pl.BlockSpec((1, rank, w), lambda a: (a, 0, 0)) for w in widths),
        compiler_params=pltpu.CompilerParams(vmem_limit_bytes=32 << 20),
        name="lay_out_late",
    )(up, low)


def prepare_kernel(
    places, tokens, cot, gain, q_down, q_up, m_down, m_up, g_down, gu_up, f_down, f_up, w_beta,
    conv, docs,
    payload, cots, q_side, beta_side, out_side, g_side, u_side, f_side,
    m_lines, g_lines, f_lines, q_lines, dcol, drow, taps, chosen,
):
    which, s = places[0], places[1]
    rank, width = q_down.shape[1], tokens.shape[1]
    share = g_side.shape[0]

    def lines(out, block, first):
        parts = [jnp.zeros((first, width), BF16)] if first else []
        parts += [block, jnp.zeros((SIDE - first - rank, width), BF16)]
        out[...] = jnp.concatenate(parts, axis=0)

    lines(m_lines, m_up[0], 0)
    lines(g_lines, g_down[0], rank)
    lines(f_lines, f_up[0], 0)
    lines(q_lines, q_down[0], rank)

    def turned(block, first):
        n = block.shape[1]
        parts = [jnp.zeros((first, n), F32)] if first else []
        parts += [block.astype(F32), jnp.zeros((SIDE - first - block.shape[0], n), F32)]
        return jnp.concatenate(parts, axis=0).T.astype(BF16)

    def window(ref, base):
        size = -(-share // 128) * 128
        tile = base // 128 + (s * share) // 128
        wide = ref[0, :, pl.ds(pl.multiple_of(tile * 128, 128), size)].astype(F32)
        late = jnp.concatenate([wide[:, 64:], wide[:, :64]], axis=1)
        return jnp.where(lax.rem(s, 2) == 1, late, wide)

    g_side[...] = turned(window(gu_up, 0), rank)[:share]
    u_side[...] = turned(window(gu_up, f_down.shape[2]), rank)[:share]
    f_side[...] = turned(window(f_down, 0), 0)[:share]
    out_side[...] = turned(m_down[0], 0)
    heads = taps.shape[1] // conv.shape[2]
    row = lax.broadcasted_iota(jnp.int32, w_beta.shape, 0)
    beta = w_beta[...].astype(F32)
    rows = [
        jnp.sum(jnp.where(row == s * heads + h, beta, 0.0), axis=0, keepdims=True)
        for h in range(heads)
    ]
    beta_side[...] = turned(jnp.concatenate(rows, axis=0), 0)
    q_side[...] = jnp.zeros_like(q_side)
    q_side[rank : 2 * rank, : q_up.shape[2]] = q_up[0]

    value = tokens[...].astype(F32)
    scale = lax.rsqrt(jnp.mean(value * value, axis=-1, keepdims=True) + 1e-05)
    normed = (value * scale * gain[...]).astype(BF16)
    payload[:, :width] = normed
    payload[:, width:] = mm_nt(normed, q_lines[...]).astype(BF16)
    cots[:, :width] = cot[...]
    cots[:, width:] = mm_nt(cot[...], f_lines[...]).astype(BF16)

    chunks = drow.shape[0]
    dcol[:PAD, :] = jnp.full((PAD, CH), -1, jnp.int32)
    dcol[PAD + chunks * CH :, :] = jnp.full((PAD, CH), -1, jnp.int32)
    for c in range(chunks):
        line = docs[:, c * CH : (c + 1) * CH]
        drow[c : c + 1, :] = line
        square = jnp.broadcast_to(line.astype(F32), (CH, CH)).T
        dcol[PAD + c * CH : PAD + (c + 1) * CH, :] = square.astype(jnp.int32)
    third = conv.shape[2]
    for t in range(conv.shape[0]):
        for h in range(heads):
            taps[t : t + 1, h * third : (h + 1) * third] = conv[t, pl.ds(s * heads + h, 1), :]
    lane = lax.broadcasted_iota(jnp.int32, chosen.shape, 1)
    chosen[...] = (lane == which).astype(F32).astype(BF16)


def prepare(
    places, tokens, cot, gain, q_down, q_up, m_down, m_up, g_down, gu_up, f_down, f_up, w_beta,
    conv, docs, seq,
):
    rows, width = tokens.shape
    rank = q_down.shape[1]
    columns, part, share = q_up.shape[2] // seq, width // seq, f_down.shape[2] // seq
    length = docs.shape[1]
    one = lambda n: pl.BlockSpec((1, rank, n), lambda i, p: (p[0], 0, 0))
    mine = lambda n: pl.BlockSpec((1, rank, n), lambda i, p: (p[0], 0, p[1]))
    full = lambda a: pl.BlockSpec(a.shape, lambda i, p, a=a: (0,) * a.ndim)
    S = jax.ShapeDtypeStruct
    outs = (
        S((rows, width + SIDE), BF16), S((rows, width + SIDE), BF16),
        S((SIDE, columns + SIDE), BF16), S((width, SIDE), BF16), S((part, SIDE), BF16),
        S((share, SIDE), BF16), S((share, SIDE), BF16), S((share, SIDE), BF16),
        S((SIDE, width), BF16), S((SIDE, width), BF16), S((SIDE, width), BF16),
        S((SIDE, width), BF16),
        S((length + 2 * PAD, CH), jnp.int32), S((length // CH, CH), jnp.int32),
        S((conv.shape[0], columns), F32), S((rank, SIDE), BF16),
    )
    return pl.pallas_call(
        prepare_kernel,
        out_shape=outs,
        grid_spec=pltpu.PrefetchScalarGridSpec(
            num_scalar_prefetch=1,
            grid=(1,),
            in_specs=[
                full(tokens), full(cot), full(gain), one(width), mine(columns), mine(part),
                one(width), one(width), one(gu_up.shape[2]), one(f_down.shape[2]), one(width),
                full(w_beta), full(conv), full(docs),
            ],
            out_specs=[pl.BlockSpec(o.shape, lambda i, p, o=o: (0,) * len(o.shape)) for o in outs],
        ),
        compiler_params=pltpu.CompilerParams(vmem_limit_bytes=62 << 20),
        name="prepare",
    )(places, tokens, cot, gain, q_down, q_up, m_down, m_up, g_down, gu_up, f_down, f_up, w_beta,
      conv, docs)


BOTH = ("fsdp", "seq")


def body(
    tokens,
    segments,
    adapter_index,
    attn_gain,
    w_qkv,
    w_beta,
    conv_weight,
    head_gain,
    w_out,
    ffn_gain,
    w_gateup,
    w_down,
    qkv_down,
    qkv_up,
    mixout_down,
    mixout_up,
    gateup_down,
    gateup_up,
    ffnout_down,
    ffnout_up,
    cotangent,
):
    seq = lax.axis_size("seq")
    s = lax.axis_index("seq")
    width = tokens.shape[1]
    count = qkv_down.shape[0]
    which = adapter_index[0]
    length = segments.shape[1]

    turn = lambda v: jnp.swapaxes(v, 1, 2)
    (
        payload, cots, q_side, beta_side, out_side, g_side, u_side, f_side,
        m_lines, g_lines, f_lines, q_lines, dcol, drow, taps, chosen,
    ) = prepare(
        jnp.stack([which, s]), tokens, cotangent, attn_gain[None],
        turn(qkv_down), qkv_up, turn(mixout_down), mixout_up, turn(gateup_down), gateup_up,
        turn(ffnout_down), ffnout_up, w_beta.T, conv_weight, segments, seq,
    )

    normed, wq, blocks = start_gather(payload, w_qkv, w_gateup.T, q_side, beta_side)
    normed = normed.reshape(length, -1)
    fixed = (dcol, drow, taps, head_gain[None])
    mixed, o_kept, t_kept, d_kept, s_kept, partial, joined, cot, wo, wd = mixer_fwd(
        normed, wq, cots, w_out, w_down, out_side, f_side, *fixed
    )

    middle, grad_middle, partial_down, grad_mixed, early = feed_forward(
        partial, blocks, g_side, u_side, wd, cot, tokens, cotangent, mixed, wo,
        m_lines, ffn_gain[None], g_lines, chosen,
    )

    layer_out, input_grad, early, up, low = mixer_bwd(
        joined, partial_down, early, normed, wq, cot.reshape(length, -1), q_side, middle, f_lines,
        *fixed, grad_mixed, o_kept, t_kept, d_kept, s_kept,
        tokens, grad_middle, q_lines, attn_gain[None], chosen, count,
    )
    gateup_g, mixdown_g, mixup_g, gudown_g, ffdown_g = lay_out_early(
        early, w_down.shape[0] // seq, width // seq
    )
    qkvup_g, qkvdown_g, ffup_g = lay_out_late(up, low, width // seq)
    return (
        layer_out,
        input_grad,
        turn(qkvdown_g),
        qkvup_g,
        turn(mixdown_g),
        mixup_g,
        turn(gudown_g),
        gateup_g,
        turn(ffdown_g),
        ffup_g,
    )


def solution(mesh):
    tokens, columns = P(BOTH, None), P(None, "fsdp")
    placed = (
        tokens, P("fsdp", None), P("fsdp"), P(), columns, P(), P(), P(), columns, P(), columns,
        columns, P(), P(), P(), P(), P(), P(), P(), P(), tokens,
    )
    return jax.shard_map(
        body,
        mesh=mesh,
        in_specs=placed,
        out_specs=(tokens, tokens) + (P(),) * 8,
        check_vma=False,
    )
```

```python
import functools
import jax
import jax.numpy as jnp
from jax import lax
from jax.experimental import pallas as pl
from jax.experimental.pallas import tpu as pltpu
from jax.sharding import PartitionSpec as P

F32 = jnp.float32
BF16 = jnp.bfloat16
CH = 128
PAD = 16


def mm(a, b):
    return jnp.dot(a.astype(BF16), b.astype(BF16), preferred_element_type=F32)


def mm_nt(a, b):
    return lax.dot_general(
        a.astype(BF16), b.astype(BF16), (((1,), (1,)), ((), ())), preferred_element_type=F32
    )


def mm_tn(a, b):
    return lax.dot_general(
        a.astype(BF16), b.astype(BF16), (((0,), (0,)), ((), ())), preferred_element_type=F32
    )


def split(a):
    high = a.astype(BF16)
    return high, (a - high.astype(F32)).astype(BF16)


def mm_fine(a, b):
    ah, al = split(a)
    bh, bl = split(b)
    return jnp.dot(
        jnp.concatenate([ah, al, ah], axis=1),
        jnp.concatenate([bh, bh, bl], axis=0),
        preferred_element_type=F32,
    )


def unit_lower_inverses(lowers, row, col, product):
    each = lambda f, *lists: [f(*items) for items in zip(*lists)]
    near = (row >> 3) == (col >> 3)
    eye = (row == col).astype(F32)
    first = [jnp.where(near, lower, 0.0) for lower in lowers]
    second = each(product, first, first)
    fourth = each(product, second, second)
    third = each(product, first, second)
    inverses = each(lambda a, b, c: eye - a + b - c, first, second, third)
    last = each(product, inverses, fourth)
    inverses = each(lambda a, b: a + b, inverses, last)
    for bits in (3, 4, 5, 6):
        joining = ((row >> (bits + 1)) == (col >> (bits + 1))) & ((row >> bits) != (col >> bits))
        below = [jnp.where(joining, lower, 0.0) for lower in lowers]
        below = each(product, below, inverses)
        below = each(product, inverses, below)
        inverses = each(lambda a, b: a - b, inverses, below)
    return inverses


def sigmoid(v):
    return 1.0 / (1.0 + jnp.exp(-v))


def chunk_masks(c, dcol, drow):
    start = pl.multiple_of(c * CH, CH)
    docs = dcol[pl.ds(start + PAD, CH), :]
    before = dcol[pl.ds(start + PAD - 8, 8), :][7:8, :]
    last = docs[CH - 1 :, :]
    same = docs == drow[pl.ds(c, 1), :]
    live = (docs == before).astype(F32)
    tail = (docs == last).astype(F32)
    live_last = (last == before).astype(F32)
    return docs, same, live, tail, live_last


def conv_chunk(c, joined, dcol, taps, docs):
    start = pl.multiple_of(c * CH, CH)
    window = joined[pl.ds(start, CH + PAD), : taps.shape[1]].astype(F32)
    ids = dcol[pl.ds(start, CH + PAD), :]
    total = window[PAD:, :] * taps[3:4, :]
    for lag in (1, 2, 3):
        keep = (ids[PAD - lag : PAD - lag + CH, :] == docs).astype(F32)
        keep = jnp.concatenate([keep] * (taps.shape[1] // CH), axis=1)
        total = total + window[PAD - lag : PAD - lag + CH, :] * keep * taps[3 - lag : 4 - lag, :]
    return total


def raw_chunk(c, joined, taps):
    rows = pl.ds(pl.multiple_of(c * CH + PAD, PAD), CH)
    return joined[rows, taps.shape[1] :].astype(F32)


def normal_parts(act):
    query, keys, values = act[:, :CH], act[:, CH : 2 * CH], act[:, 2 * CH :]
    q_scale = lax.rsqrt(jnp.sum(query * query, axis=-1, keepdims=True) + 1e-06)
    k_scale = lax.rsqrt(jnp.sum(keys * keys, axis=-1, keepdims=True) + 1e-06)
    return query * q_scale * CH**-0.5, keys * k_scale, values, q_scale, k_scale


def mixer_fwd_kernel(
    heads, chunks, normed, weight, cot, w_out, w_down, out_side, f_side,
    dcol, drow, taps, gain,
    mixed, o_out, t_out, d_out, s_out, partial, joined_out, everyone, wo, wd,
    joined, rows_v, weight_v, wo_v, q_s, k_s, u_s, w_s, p_s, sem, send, recv, local,
):
    loads = [
        pltpu.make_async_copy(weight, weight_v, sem.at[0]),
        pltpu.make_async_copy(normed, rows_v, sem.at[1]),
    ]
    for copy in loads:
        copy.start()
    greet(ring_peers(), line_peers())
    feed = Feed(
        Line(send, recv, local), cot, (w_out, w_down), (out_side, f_side), everyone, (wo, wd)
    )
    feed.start()
    joined[pl.ds(0, PAD), :] = jnp.zeros((PAD, joined.shape[1]), BF16)
    for copy in loads:
        copy.wait()
    batch = 2 * CH

    def project(step):
        rows = pl.multiple_of(step * batch, batch)
        joined[pl.ds(rows + PAD, batch), :] = mm(
            rows_v[pl.ds(rows, batch), :], weight_v[...]
        ).astype(BF16)

    project(0)
    row = lax.broadcasted_iota(jnp.int32, (CH, CH), 0)
    col = lax.broadcasted_iota(jnp.int32, (CH, CH), 1)

    def prepare(items):
        lowers, parts = [], []
        for c, docs, same, live, act, raws in items:
            for h in range(heads):
                query, keys, values, _, _ = normal_parts(act[:, h * 3 * CH : (h + 1) * 3 * CH])
                beta = sigmoid(raws[:, h : h + 1])
                inner = mm_nt(keys, keys)
                lowers.append(jnp.where(same & (row > col), inner * beta, 0.0))
                rows = pl.ds(pl.multiple_of(c * CH, CH), CH)
                scores = jnp.where(same & (row >= col), mm_nt(query, keys), 0.0)
                p_s[h, rows, :] = scores.astype(BF16)
                q_s[h, rows, :] = (query * live).astype(BF16)
                k_s[h, rows, :] = keys
                targets = jnp.concatenate([values * beta, keys * (beta * live)], axis=1)
                parts.append((h, rows, targets.astype(BF16)))
        inverses = unit_lower_inverses(lowers, row, col, mm_fine)
        for inverse, (h, rows, targets) in zip(inverses, parts):
            inverse = inverse.astype(BF16)
            t_out[h, rows, :] = inverse
            both = mm(inverse, targets)
            u_s[h, rows, :] = both[:, :CH]
            w_s[h, rows, :] = both[:, CH:].astype(BF16)

    def first(step, carry):
        feed.stage(step)
        parts = []
        for part in range(2):
            c = step * 2 + part
            docs, same, live, tail, live_last = chunk_masks(c, dcol, drow)
            conv = conv_chunk(c, joined, dcol, taps, docs)
            act = conv * sigmoid(conv)
            parts.append((c, docs, same, live, act, raw_chunk(c, joined, taps)))
        project(jnp.minimum(step + 1, chunks // 2 - 1))
        prepare(parts)
        return carry

    lax.fori_loop(0, chunks // 2, first, 0)
    kept = pltpu.make_async_copy(joined.at[pl.ds(PAD, chunks * CH), :], joined_out, sem.at[0])
    kept.start()
    feed.third()

    def second(c, states):
        rows = pl.ds(pl.multiple_of(c * CH, CH), CH)
        docs, same, live, tail, live_last = chunk_masks(c, dcol, drow)
        for h in range(heads):
            s_out[h, rows, :] = states[h].astype(BF16)
        recalled = [mm(w_s[h, rows, :], states[h]) for h in range(heads)]
        updates = [u_s[h, rows, :] - recalled[h] for h in range(heads)]
        added = [mm_tn(k_s[h, rows, :] * tail, updates[h]) for h in range(heads)]
        for h in range(heads):
            d_out[h, rows, :] = updates[h].astype(BF16)
        return tuple(states[h] * live_last + added[h] for h in range(heads))

    zero = jnp.zeros((CH, CH), F32)
    lax.fori_loop(0, chunks, second, (zero,) * heads)
    feed.fourth()
    last = pltpu.make_async_copy(wo, wo_v, sem.at[1])
    last.start()
    last.wait()

    def third(c, carry):
        rows = pl.ds(pl.multiple_of(c * CH, CH), CH)
        outs = [
            mm(
                jnp.concatenate([q_s[h, rows, :], p_s[h, rows, :]], axis=1),
                jnp.concatenate(
                    [s_out[h, rows, :], d_out[h, rows, :]], axis=0
                ),
            )
            for h in range(heads)
        ]
        for h, out in enumerate(outs):
            o_out[h, rows, :] = out
            scale = lax.rsqrt(jnp.mean(out * out, axis=-1, keepdims=True) + 1e-05)
            mixed[rows, h * CH : (h + 1) * CH] = (out * scale * gain[...]).astype(BF16)
        partial[c] = mm(mixed[rows, :], wo_v[...]).astype(BF16)
        return carry

    lax.fori_loop(0, chunks, third, 0)
    kept.wait()
    feed.finish()


def mixer_fwd(
    normed, weight, cot, w_out, w_down, out_side, f_side, dcol, drow, taps, gain
):
    tokens, across = normed.shape
    wide = weight.shape[1]
    heads = wide // (3 * CH)
    chunks = tokens // CH
    seq = lax.axis_size("seq")
    out = lambda *shape: jax.ShapeDtypeStruct(shape, BF16)
    square = out(heads, tokens, CH)
    share, part = f_side.shape[0], out_side.shape[0]
    return pl.pallas_call(
        functools.partial(mixer_fwd_kernel, heads, chunks),
        out_shape=(
            out(tokens, heads * CH), jax.ShapeDtypeStruct(square.shape, F32), square, square, square,
            out(chunks, CH, across), out(tokens, wide), out(seq, *cot.shape),
            out(part, across), out(share, across),
        ),
        in_specs=[ANY] * 7 + [VMEM] * 4,
        out_specs=(VMEM,) * 6 + (ANY,) * 4,
        scratch_shapes=[
            pltpu.VMEM((tokens + PAD, wide), BF16),
            pltpu.VMEM((tokens, across), BF16),
            pltpu.VMEM((across, wide), BF16),
            pltpu.VMEM((part, across), BF16),
            pltpu.VMEM((heads, tokens, CH), BF16),
            pltpu.VMEM((heads, tokens, CH), F32),
            pltpu.VMEM((heads, tokens, CH), F32),
            pltpu.VMEM((heads, tokens, CH), BF16),
            pltpu.VMEM((heads, tokens, CH), BF16),
            pltpu.SemaphoreType.DMA((2,)),
        ]
        + sems(Feed.COPIES, Feed.LOCAL),
        compiler_params=comm_params(1, 62),
        name="mixer_fwd",
    )(normed, weight, cot, w_out, w_down, out_side, f_side, dcol, drow, taps, gain)


def mixer_bwd_kernel(
    heads, chunks, source, partial, early, normed, weight, cot, q_side, values, up,
    dcol, drow, taps, gain, grad, o_in, t_in, d_in, s_in, tokens, grad_middle, down, attn_gain,
    chosen, layer_out, input_grad, early_whole, up_whole, low_whole,
    joined, e_s, f_s, w_s, x_s, ds_s, go_s, dj_s, side_v, weight_v, sem,
    total, own, stage, relay, away, back, early_pieces, early_sum, early_ring,
    back_partial, stage2, relay2, away2, back2, inner, inners, sides,
    up_pieces, up_sum, low_pieces, low_sum,
    send, recv, local,
):
    loads = [
        pltpu.make_async_copy(source, joined.at[pl.ds(PAD, source.shape[0]), :], sem.at[0]),
        pltpu.make_async_copy(weight, weight_v, sem.at[1]),
        pltpu.make_async_copy(
            normed.at[:, pl.ds(normed.shape[1] - SIDE, SIDE)], side_v, sem.at[2]
        ),
    ]
    for copy in loads:
        copy.start()
    greet(all_seq(), line_peers())
    line = Line(send, recv, local)
    ring = RingSum(line, partial, (own, stage, relay, away, back))
    sums = EarlySum(line, early, early_pieces, early_sum, early_ring)
    second_sum = RingSum(line, back_partial, (None, stage2, relay2, away2, back2))
    s, partner, _, _, _ = seq_places()
    f = lax.axis_index("fsdp")
    core = lax.rem(s, 2)
    inner_spread = Spread(line, "seq", 8, inner, lambda t: inners.at[t])
    up_ring = RingGather(line, up_sum, up_whole)
    low_ring = RingGather(line, low_sum, low_whole)

    def early_place(t, half, quarter):
        first = core * 4 + half * 2 + (quarter or 0)
        return early_whole.at[t, pl.ds(first, 2 if quarter is None else 1)]

    def piece_place(pieces):
        def place(t, half, quarter):
            first = half * 2 + (quarter or 0)
            return pieces.at[t, pl.ds(first, 2 if quarter is None else 1)]

        return place

    early_plane = PlaneGather(line, early_place)
    up_plane = PlaneGather(line, piece_place(up_pieces))
    low_plane = PlaneGather(line, piece_place(low_pieces))
    at, local_at = line.take(1, 3)
    half_slices = pl.ds(core * 4, 4)
    retain = line.local(local_at, early_ring.at[half_slices], early_whole.at[f, half_slices])
    share = line.copy(
        at, early_whole.at[:, half_slices], early_whole.at[:, half_slices], {"seq": partner}
    )
    part = sides.shape[1] // 2
    mine = pl.ds(pl.multiple_of(s * part, 128), part)
    fetch = [
        line.local(local_at + 1, normed.at[:, mine], sides.at[:, pl.ds(0, part)]),
        line.local(local_at + 2, cot.at[:, mine], sides.at[:, pl.ds(part, part)]),
    ]
    for copy in fetch:
        copy.start()
    ring.start()
    sums.start()
    joined[pl.ds(0, PAD), :] = jnp.zeros((PAD, joined.shape[1]), BF16)
    dj_s[pl.ds((chunks - 2) * CH, 2 * CH), :] = jnp.zeros((2 * CH, dj_s.shape[1]), BF16)
    for copy in loads:
        copy.wait()
    row = lax.broadcasted_iota(jnp.int32, (CH, CH), 0)
    col = lax.broadcasted_iota(jnp.int32, (CH, CH), 1)
    width = 3 * CH

    def revive(c):
        docs, same, live, tail, live_last = chunk_masks(c, dcol, drow)
        conv = conv_chunk(c, joined, dcol, taps, docs)
        raws = raw_chunk(c, joined, taps)
        return docs, same, live, tail, live_last, conv, raws

    def first(step, carry):
        pl.when(step == 2)(sums.plane.second)
        items = []
        for part in range(2):
            c = step * 2 + part
            docs, same, live, tail, live_last, conv, raws = revive(c)
            act = conv * sigmoid(conv)
            rows = pl.ds(pl.multiple_of(c * CH, CH), CH)
            for h in range(heads):
                query, keys, values, _, _ = normal_parts(act[:, h * width : (h + 1) * width])
                beta = sigmoid(raws[:, h : h + 1])
                out = o_in[h, rows, :]
                weighted = grad[rows, h * CH : (h + 1) * CH].astype(F32) * gain[...]
                scale = lax.rsqrt(jnp.mean(out * out, axis=-1, keepdims=True) + 1e-05)
                grad_o = scale * weighted - out * (
                    scale * scale * scale * jnp.mean(weighted * out, axis=-1, keepdims=True)
                )
                go_s[h, rows, :] = grad_o
                x_s[h, rows, :] = keys * tail
                known = (keys * (beta * live)).astype(BF16)
                items.append((h, rows, same, query, keys, (query * live), grad_o, known))
        scores = [mm_nt(query, keys) for _, _, _, query, keys, _, _, _ in items]
        recalls = [mm(t_in[h, rows, :], known) for h, rows, _, _, _, _, _, known in items]
        scores = [
            jnp.where(item[2] & (row >= col), score, 0.0) for item, score in zip(items, scores)
        ]
        both = [
            mm_tn(jnp.concatenate([score, item[5]], axis=1), item[6])
            for item, score in zip(items, scores)
        ]
        for (h, rows, *_), ef, recall in zip(items, both, recalls):
            e_s[h, rows, :] = ef[:CH]
            f_s[h, rows, :] = ef[CH:]
            w_s[h, rows, :] = recall.astype(BF16)
        return carry

    lax.fori_loop(0, chunks // 2, first, 0)
    ring.middle()
    sums.plane.third()

    def second(step, states):
        c = chunks - 1 - step
        rows = pl.ds(pl.multiple_of(c * CH, CH), CH)
        docs, same, live, tail, live_last = chunk_masks(c, dcol, drow)
        for h in range(heads):
            ds_s[h, rows, :] = states[h]
        passed = [mm(x_s[h, rows, :], states[h]) for h in range(heads)]
        grads = [e_s[h, rows, :] + passed[h] for h in range(heads)]
        taken = [mm_tn(w_s[h, rows, :], grads[h]) for h in range(heads)]
        for h in range(heads):
            x_s[h, rows, :] = grads[h]
        return tuple(
            states[h] * live_last + f_s[h, rows, :] - taken[h] for h in range(heads)
        )

    zero = jnp.zeros((CH, CH), F32)
    lax.fori_loop(0, chunks, second, (zero,) * heads)

    sums.plane.fourth()

    def project(c):
        rows = pl.ds(pl.multiple_of(c * CH, CH), CH)
        grads = dj_s[rows, :]
        back_partial[c] = mm_nt(grads, weight_v[...]).astype(BF16)

    def send_near(chip, ready):
        for k, d in enumerate((2, 1, 3, 0)):
            here = ready & (lax.rem(s // 2 + d, 4) == chip)
            pl.when(here)(lambda: second_sum.near(k).start())

    def third(step, after):
        pl.when(step == 0)(sums.add)
        pl.when(step == 1)(ring.last)
        pl.when(step == 1)(sums.ring.middle)

        @pl.when(step == 2)
        def _():
            sums.ring.finish()
            retain.start()
            retain.wait()
            early_plane.first()

        pl.when(step == 3)(early_plane.second)
        later = chunks - 1 - 2 * step
        for part in range(2):
            project(jnp.minimum(later + 2 - part, chunks - 1 - part))
        send_near(jnp.minimum(later + 1, chunks) // 2, step > 0)
        chunk_items, items = [], []
        for part in range(2):
            c = later - part
            docs, same, live, tail, live_last, conv, raws = revive(c)
            gate = sigmoid(conv)
            act = conv * gate
            slope = gate * (1.0 + conv * (1.0 - gate))
            rows = pl.ds(pl.multiple_of(c * CH, CH), CH)
            chunk_items.append((c, rows, slope))
            for h in range(heads):
                cut = act[:, h * width : (h + 1) * width]
                beta = sigmoid(raws[:, h : h + 1])
                items.append((h, rows, same, live, tail, beta, cut) + normal_parts(cut))
        targets = [mm_tn(t_in[h, rows, :], x_s[h, rows, :]) for h, rows, *_ in items]
        pairs = [
            mm_nt(jnp.concatenate([target, go_s[h, rows, :]], axis=0), d_in[h, rows, :])
            for (h, rows, *_), target in zip(items, targets)
        ]
        backs = [
            mm_nt(
                jnp.concatenate([go_s[h, rows, :] * live, -target * (beta * live)], axis=0),
                s_in[h, rows, :],
            )
            for (h, rows, _, live, _, beta, *_), target in zip(items, targets)
        ]
        inners = [mm_nt(item[8], item[8]) for item in items]
        recalls = [mm(item[8], s_in[item[0], item[1], :]) for item in items]
        ends = [
            mm_nt(d_in[h, rows, :].astype(F32) * tail, ds_s[h, rows, :])
            for h, rows, _, _, tail, *_ in items
        ]
        lowers = [
            jnp.where(item[2] & (row > col), -pair[:CH], 0.0) for item, pair in zip(items, pairs)
        ]
        scores = [
            jnp.where(item[2] & (row >= col), pair[CH:], 0.0) for item, pair in zip(items, pairs)
        ]
        grad_inners = [lower * item[5] for item, lower in zip(items, lowers)]
        turned = [
            mm_tn(
                jnp.concatenate([score, grad_inner], axis=0),
                jnp.concatenate([item[7], item[8]], axis=0),
            )
            for item, score, grad_inner in zip(items, scores, grad_inners)
        ]
        straight = [
            mm(jnp.concatenate([score, grad_inner], axis=0), item[8])
            for item, score, grad_inner in zip(items, scores, grad_inners)
        ]
        lane = lax.broadcasted_iota(jnp.int32, (CH, CH), 1)
        for part, (c, rows, slope) in enumerate(chunk_items):
            grads, grad_raw = [], jnp.zeros((CH, CH), F32)
            for h in range(heads):
                k = part * heads + h
                _, _, _, live, _, beta, cut, query, keys, values, q_scale, k_scale = items[k]
                target, back = targets[k], backs[k]
                grad_beta = jnp.sum(
                    lowers[k] * inners[k] + target * (values - live * recalls[k]),
                    axis=-1,
                    keepdims=True,
                )
                grad_query = (back[:CH] + straight[k][:CH]) * CH**-0.5
                grad_keys = back[CH:] + turned[k] + straight[k][CH:] + ends[k]
                raw_q, raw_k = cut[:, :CH], cut[:, CH : 2 * CH]
                grad_q = q_scale * grad_query - raw_q * (
                    q_scale * q_scale * q_scale
                    * jnp.sum(grad_query * raw_q, axis=-1, keepdims=True)
                )
                grad_k = k_scale * grad_keys - raw_k * (
                    k_scale * k_scale * k_scale
                    * jnp.sum(grad_keys * raw_k, axis=-1, keepdims=True)
                )
                grads += [grad_q, grad_k, target * beta]
                grad_raw = jnp.where(lane == h, grad_beta * beta * (1.0 - beta), grad_raw)
            dj_s[rows, heads * width :] = grad_raw.astype(BF16)
            grads = jnp.concatenate(grads, axis=1) * slope
            window = jnp.concatenate([grads, after], axis=0)
            ids = dcol[pl.ds(pl.multiple_of(c * CH + PAD, PAD), CH + PAD), :]
            total_ = grads * taps[3:4, :]
            for lag in (1, 2, 3):
                keep = (ids[lag : lag + CH] == ids[:CH]).astype(F32)
                keep = jnp.concatenate([keep] * (heads * 3), axis=1)
                total_ = total_ + window[lag : lag + CH] * keep * taps[3 - lag : 4 - lag, :]
            dj_s[rows, : heads * width] = total_.astype(BF16)
            after = grads[:8]
        return after

    lax.fori_loop(0, chunks // 2, third, jnp.zeros((8, heads * width), F32))
    project(1)
    project(0)
    send_near(0, s >= 0)
    rank, n = inner.shape[1:]

    def put(pieces, piece):
        size = pieces.shape[3]
        for q in range(4):
            pieces[f, q] = piece[:, q * size : (q + 1) * size]

    up_piece = mm_tn(side_v[...], dj_s[:, : heads * width])[rank : 2 * rank].astype(BF16)
    put(up_pieces, jnp.concatenate([up_piece, chosen[...], chosen[...]], axis=1))
    up_plane.first()
    ring.finish(total)
    across = values.shape[1]
    q_inner = mm_nt(q_side[...], dj_s[...])[rank : 2 * rank].astype(BF16)
    f_inner = total[:, across:].T[:rank].astype(BF16)
    inner[0] = q_inner[:, :n]
    rest = 2 * n - q_inner.shape[1] - f_inner.shape[1]
    inner[1] = jnp.concatenate([q_inner[:, n:], f_inner, jnp.zeros((rank, rest), BF16)], axis=1)
    inner_spread.start()
    second_sum.middle()
    early_plane.third()
    up_plane.second()

    def layer_rows(rows):
        inner = total[rows, across:].astype(BF16)
        layer_out[rows, :] = (
            values[rows, :] + (total[rows, :across] + mm(inner, up[...]))
        ).astype(BF16)

    by_rows(values.shape[0], layer_rows)
    for copy in fetch:
        copy.wait()
    inner_spread.arrive()
    tokens_here = tokens.shape[0]
    ahead = sides.shape[0] - n
    added, beside = [None, None], []
    for t in range(inners.shape[0]):
        parts = inners[t, 0].astype(F32), inners[t, 1].astype(F32)[:, :ahead]
        added = [p if sum_ is None else sum_ + p for p, sum_ in zip(parts, added)]
        beside.append(inners[t, 1][:, ahead : ahead + tokens_here])
    down_piece = mm(jnp.concatenate(added, axis=1), sides[:, :part])
    ff_piece = mm(jnp.concatenate(beside, axis=1), sides[:, part:])
    put(low_pieces, jnp.concatenate([down_piece, ff_piece], axis=1).astype(BF16))
    low_plane.first()
    up_plane.third()
    second_sum.last()
    low_plane.second()
    up_plane.fourth()
    early_plane.fourth()
    up_plane.finish()
    marks = up_pieces.at[:, 3]
    by_adapter(up_pieces, marks, 0, up_sum)
    up_ring.start()
    low_plane.third()
    low_plane.fourth()
    early_plane.finish()
    share.start()
    low_plane.finish()
    by_adapter(low_pieces, marks, 0, low_sum)
    low_ring.start()
    second_sum.finish(total)

    def input_rows(rows):
        grad_normed = total[rows, :across] + mm(total[rows, across:], down[...])
        input_grad[rows, :] = (
            grad_middle[rows, :]
            + norm_back_rows(tokens[rows, :].astype(F32), attn_gain[...], grad_normed)
        ).astype(BF16)

    by_rows(tokens_here, input_rows)
    up_ring.middle()
    low_ring.middle()
    up_ring.finish()
    low_ring.finish()
    share.wait()
    inner_spread.finish()


def mixer_bwd(
    joined, partial, early, normed, weight, cot, q_side, values, up, dcol, drow, taps, gain,
    grad, o, t, d, s, tokens, grad_middle, down, attn_gain, chosen, count,
):
    length, wide = joined.shape
    heads = wide // (3 * CH)
    chunks = length // CH
    square = (heads, length, CH)
    rows, across = values.shape
    seq, fsdp, rank = lax.axis_size("seq"), 16, early.shape[2]
    part = across // seq
    columns = heads * 3 * CH
    out = lambda *shape: jax.ShapeDtypeStruct(shape, BF16)
    bf16 = lambda *shape: pltpu.VMEM(shape, BF16)
    f32 = lambda *shape: pltpu.VMEM(shape, F32)
    buffers = sum_buffers(rows, across + SIDE)
    copies = 2 * RingSum.COPIES + EarlySum.COPIES + 2 * RingGather.COPIES + 3 * PlaneGather.COPIES
    return pl.pallas_call(
        functools.partial(mixer_bwd_kernel, heads, chunks),
        out_shape=(
            out(rows, across), out(rows, across),
            out(fsdp, seq, *early.shape[1:]),
            out(seq, count, rank, columns), out(seq, count, rank, 2 * part),
        ),
        in_specs=[ANY] * 6 + [VMEM] * 17,
        out_specs=(VMEM, VMEM, ANY, ANY, ANY),
        scratch_shapes=[
            bf16(length + PAD, wide), f32(*square), f32(*square), bf16(*square), f32(*square),
            f32(*square), f32(*square), bf16(length, wide), bf16(length, SIDE),
            bf16(*weight.shape), pltpu.SemaphoreType.DMA((3,)), f32(rows, across + SIDE),
        ]
        + buffers
        + [
            bf16(fsdp, *early.shape), bf16(*early.shape[1:]), bf16(seq, *early.shape[1:]),
            bf16(seq, rows, across + SIDE),
        ]
        + buffers[1:]
        + [
            bf16(2, rank, 640), bf16(seq, 2, rank, 640), bf16(length, 2 * part),
            bf16(fsdp, 4, rank, (columns + 2 * SIDE) // 4), bf16(count, rank, columns),
            bf16(fsdp, 4, rank, part // 2), bf16(count, rank, 2 * part),
        ]
        + sems(copies + 7 + 1, 2 * RingSum.LOCAL + EarlySum.LOCAL + 3 + 3),
        compiler_params=comm_params(4, 60),
        name="mixer_bwd",
    )(
        joined, partial, early, normed, weight, cot, q_side, values, up, dcol, drow, taps, gain,
        grad, o, t, d, s, tokens, grad_middle, down, attn_gain, chosen,
    )

MESH = pl.DeviceIdType.MESH
SIDE = 128
ANY = pl.BlockSpec(memory_space=pl.ANY)
VMEM = pl.BlockSpec(memory_space=pltpu.VMEM)
SMEM = pl.BlockSpec(memory_space=pltpu.SMEM)


class Line:
    def __init__(self, send_sems, recv_sems, local_sems):
        self.send_sems, self.recv_sems, self.local_sems = send_sems, recv_sems, local_sems
        self.used, self.used_local = 0, 0

    def take(self, copies, local=0):
        at = self.used, self.used_local
        self.used += copies
        self.used_local += local
        return at

    def copy(self, at, src, dst, device):
        return pltpu.make_async_remote_copy(
            src_ref=src, dst_ref=dst, send_sem=self.send_sems.at[at],
            recv_sem=self.recv_sems.at[at], device_id=device, device_id_type=MESH,
        )

    def local(self, at, src, dst):
        return pltpu.make_async_copy(src, dst, self.local_sems.at[at])


def sems(copies, local):
    return [
        pltpu.SemaphoreType.DMA((copies,)),
        pltpu.SemaphoreType.DMA((copies,)),
        pltpu.SemaphoreType.DMA((local,)),
    ]


def seq_places():
    s = lax.axis_index("seq")
    x, core = s // 2, lax.rem(s, 2)
    there = lambda d: lax.rem(x + d, 4) * 2 + core
    return s, x * 2 + 1 - core, there(1), there(3), there(2)


def plane_places():
    f = lax.axis_index("fsdp")
    return f, f // 4, lax.rem(f, 4)


def ring_peers():
    s, partner, right, left, far = seq_places()
    return [partner, right, left]


def all_seq():
    s = lax.axis_index("seq")
    return [lax.rem(s + d, 8) for d in range(1, 8)]


def all_plane():
    f = lax.axis_index("fsdp")
    return [lax.rem(f + d, 16) for d in range(1, 16)]


def line_peers():
    f, y, z = plane_places()
    return [y * 4 + lax.rem(z + d, 4) for d in (1, 3)] + [
        lax.rem(y + d, 4) * 4 + z for d in (1, 3)
    ]


def greet(seq_peers, plane_peers):
    barrier = pltpu.get_barrier_semaphore()
    for p in seq_peers:
        pl.semaphore_signal(barrier, inc=1, device_id={"seq": p}, device_id_type=MESH)
    for p in plane_peers:
        pl.semaphore_signal(barrier, inc=1, device_id={"fsdp": p}, device_id_type=MESH)
    pl.semaphore_wait(barrier, len(seq_peers) + len(plane_peers))


class RingGather:
    COPIES, LOCAL = 13, 1

    def __init__(self, line, block, out, first=0, rows=None):
        self.line, self.placed, self.out = line, block is None, out
        self.block = out.at[lax.axis_index("seq")] if self.placed else block
        rows = rows or self.block.shape[0]
        half = rows // 2
        self.low, self.high = pl.ds(first, half), pl.ds(first + half, half)
        self.all = pl.ds(first, rows)
        self.at, self.local_at = line.take(self.COPIES, self.LOCAL)

    def mine(self, i, rows, peer):
        s = lax.axis_index("seq")
        return self.line.copy(
            self.at + i, self.block.at[rows], self.out.at[s, rows], {"seq": peer}
        )

    def pass_on(self, i, s, rows, peer):
        ref = self.out.at[s, rows]
        return self.line.copy(self.at + i, ref, ref, {"seq": peer})

    def copy(self, i):
        s, partner, right, left, far = seq_places()
        low, high = self.low, self.high
        if i < 4:
            return self.mine(i, *((low, right), (high, left), (high, right), (low, left))[i])
        if i == 4:
            return self.mine(4, self.all, partner)
        return self.pass_on(
            i,
            *(
                (left, low, right), (left, low, partner), (right, high, left),
                (right, high, partner), (left, high, partner), (right, low, partner),
                (far, low, partner), (far, high, partner),
            )[i - 5],
        )

    def own(self):
        s = lax.axis_index("seq")
        return self.line.local(self.local_at, self.block, self.out.at[s])

    def start(self):
        for i in range(5):
            self.copy(i).start()
        if not self.placed:
            self.own().start()

    def middle(self):
        for arrived, onward in ((0, (5, 6)), (1, (7, 8)), (2, (9,)), (3, (10,))):
            self.copy(arrived).wait_recv()
            for i in onward:
                self.copy(i).start()

    def finish(self):
        self.copy(5).wait_recv()
        self.copy(11).start()
        self.copy(7).wait_recv()
        self.copy(12).start()
        for i in (0, 1, 2, 3, 5, 7):
            self.copy(i).wait_send()
        for i in (4, 6, 8, 9, 10, 11, 12):
            self.copy(i).wait()
        if not self.placed:
            self.own().wait()

    def reach(self, step):
        @pl.when(step == 0)
        def _():
            self.copy(4).wait_recv()

        @pl.when(step == 1)
        def _():
            self.middle()
            self.copy(8).wait_recv()
            self.copy(10).wait_recv()

        @pl.when(step == 2)
        def _():
            self.copy(6).wait_recv()
            self.copy(9).wait_recv()

        @pl.when(step == 3)
        def _():
            self.copy(5).wait_recv()
            self.copy(11).start()
            self.copy(7).wait_recv()
            self.copy(12).start()
            self.copy(11).wait_recv()
            self.copy(12).wait_recv()

    def sent(self):
        for i in range(self.COPIES):
            self.copy(i).wait_send()


class PlaneGather:
    COPIES, LOCAL = 40, 0

    def __init__(self, line, place):
        self.line, self.place = line, place
        self.at, _ = line.take(self.COPIES)

    def by(self, half, along, across):
        f, y, z = plane_places()
        dy, dz = (across, along) if half == 0 else (along, across)
        return lax.rem(y + dy + 4, 4) * 4 + lax.rem(z + dz + 4, 4)

    def send(self, at, ref, peer):
        return self.line.copy(self.at + at, ref, ref, {"fsdp": peer})

    def one(self, half, i):
        ref = self.place(lax.axis_index("fsdp"), half, None)
        return self.send(half * 20 + i, ref, self.by(half, (1, -1)[i], 0))

    def one_on(self, half, i):
        d = (1, -1)[i]
        ref = self.place(self.by(half, -d, 0), half, i)
        return self.send(half * 20 + 2 + i, ref, self.by(half, d, 0))

    def two(self, half, k, i):
        ref = self.place(self.by(half, (0, -1, 1, 2)[k], 0), half, None)
        return self.send(half * 20 + 4 + k * 2 + i, ref, self.by(half, 0, (1, -1)[i]))

    def two_on(self, half, k, i):
        d = (1, -1)[i]
        ref = self.place(self.by(half, (0, -1, 1, 2)[k], -d), half, i)
        return self.send(half * 20 + 12 + k * 2 + i, ref, self.by(half, 0, d))

    def first(self):
        for half in (0, 1):
            for i in (0, 1):
                self.one(half, i).start()

    def second(self):
        for half in (0, 1):
            for i in (0, 1):
                self.two(half, 0, i).start()
        for half in (0, 1):
            for i in (0, 1):
                self.one(half, i).wait_recv()
                self.one_on(half, i).start()
                for j in (0, 1):
                    self.two(half, 1 + i, j).start()

    def third(self):
        for half in (0, 1):
            for i in (0, 1):
                self.one_on(half, i).wait_recv()
            for i in (0, 1):
                self.two(half, 3, i).start()
        for k in range(3):
            for half in (0, 1):
                self.cross(half, k)

    def cross(self, half, k):
        for i in (0, 1):
            self.two(half, k, i).wait_recv()
            self.two_on(half, k, i).start()

    def fourth(self):
        for half in (0, 1):
            self.cross(half, 3)

    def finish(self):
        for half in (0, 1):
            for i in (0, 1):
                self.one(half, i).wait_send()
                self.one_on(half, i).wait_send()
                for k in range(4):
                    self.two(half, k, i).wait_send()
                    self.two_on(half, k, i).wait()


class Scatter:
    COPIES, LOCAL = 17, 2

    def __init__(self, line, sources, source_block, into):
        self.line, self.sources = line, sources
        self.source_block, self.into = source_block, into
        self.at, self.local_at = line.take(self.COPIES, self.LOCAL)

    def copy(self, j, d):
        f, _, _ = plane_places()
        t = lax.rem(f + d, 16)
        line = self.line
        return pltpu.make_async_remote_copy(
            src_ref=self.source_block(t), dst_ref=self.into(t, j),
            send_sem=line.send_sems.at[self.at + d], recv_sem=line.recv_sems.at[self.at + j],
            device_id={"fsdp": t}, device_id_type=MESH,
        )

    def keep(self, j):
        f, _, _ = plane_places()
        return self.line.local(self.local_at + j, self.source_block(f), self.into(f, j))

    def start(self):
        f, _, _ = plane_places()
        for j, source in enumerate(self.sources):
            @pl.when(f == source)
            def _():
                for d in range(1, 16):
                    self.copy(j, d).start()
                self.keep(j).start()

    def arrive(self):
        f, _, _ = plane_places()
        for j, source in enumerate(self.sources):
            @pl.when(f == source)
            def _():
                self.keep(j).wait()

            @pl.when(f != source)
            def _():
                ref = self.into(f, j)
                pltpu.make_async_remote_copy(
                    src_ref=ref, dst_ref=ref, send_sem=self.line.send_sems.at[self.at],
                    recv_sem=self.line.recv_sems.at[self.at + j],
                    device_id={"fsdp": lax.rem(f + 1, 16)}, device_id_type=MESH,
                ).wait_recv()

    def finish(self):
        f, _, _ = plane_places()
        for j, source in enumerate(self.sources):
            @pl.when(f == source)
            def _():
                for d in range(1, 16):
                    self.copy(j, d).wait_send()


class Spread:
    def __init__(self, line, axis, count, block, slot):
        self.line, self.axis, self.count, self.block, self.slot = line, axis, count, block, slot
        self.at, self.local_at = line.take(count - 1, 1)

    def copy(self, d):
        me = lax.axis_index(self.axis)
        return self.line.copy(
            self.at + d - 1, self.block, self.slot(me), {self.axis: lax.rem(me + d, self.count)}
        )

    def own(self):
        return self.line.local(self.local_at, self.block, self.slot(lax.axis_index(self.axis)))

    def start(self):
        for d in range(1, self.count):
            self.copy(d).start()
        self.own().start()

    def arrive(self):
        for d in range(1, self.count):
            self.copy(d).wait_recv()
        self.own().wait()

    def finish(self):
        for d in range(1, self.count):
            self.copy(d).wait_send()


def rows_of(total, half, quarter):
    if quarter is None:
        return pl.ds(half * (total // 2), total // 2)
    return pl.ds(half * (total // 2) + quarter * (total // 4), total // 4)


def columns_place(out):
    return lambda f, half, quarter: out.at[
        rows_of(out.shape[0], half, quarter), pl.ds(pl.multiple_of(f * 128, 128), 128)
    ]


def block_of(ref, t):
    return ref.at[:, pl.ds(pl.multiple_of(t * 128, 128), 128)]


ADD_ROWS = 16


def add_rows(dst, sources, first, count):
    def step(i, carry):
        rows = pl.ds(pl.multiple_of(first + i * ADD_ROWS, ADD_ROWS), ADD_ROWS)
        total = None
        for source, offset in sources:
            at = pl.ds(pl.multiple_of(first - offset + i * ADD_ROWS, ADD_ROWS), ADD_ROWS)
            item = source[at, :].astype(F32)
            total = item if total is None else total + item
        dst[rows, :] = total.astype(dst.dtype)
        return carry

    lax.fori_loop(0, count // ADD_ROWS, step, 0)


class RingSum:
    COPIES, LOCAL = 10, 4

    def __init__(self, line, partial, buffers, first=0):
        self.line, self.partial, self.first = line, partial, first
        self.own, self.stage, self.relay, self.away, self.back = buffers
        self.rows = self.stage.shape[1]
        self.block = pl.ds(first, self.rows)
        self.half = self.rows // 2
        self.low, self.high = pl.ds(0, self.half), pl.ds(self.half, self.half)
        self.at, self.local_at = line.take(self.COPIES, self.LOCAL)

    def near(self, k):
        s, partner, right, left, far = seq_places()
        p = (far, right, left, s)[k]
        return self.line.copy(
            self.at + k, self.partial.at[p + partner - s, self.block], self.stage.at[k],
            {"seq": partner},
        )

    def kept(self, k):
        s, partner, right, left, far = seq_places()
        p = (far, right, left, s)[k]
        return self.line.local(self.local_at + k, self.partial.at[p, self.block], self.own.at[k])

    def go(self, i):
        s, partner, right, left, far = seq_places()
        away, relay, back, low, high = self.away, self.relay, self.back, self.low, self.high
        src, dst, peer = (
            (away.at[0, low], relay.at[0], right),
            (away.at[0, high], relay.at[1], left),
            (away.at[1, high], back.at[0, high], right),
            (away.at[2, low], back.at[1, low], left),
            (away.at[1, low], back.at[0, low], right),
            (away.at[2, high], back.at[1, high], left),
        )[i]
        return self.line.copy(self.at + 4 + i, src, dst, {"seq": peer})

    def start(self):
        for k in range(4):
            self.near(k).start()
            if self.own is not None:
                self.kept(k).start()

    def ready(self, k):
        self.near(k).wait_recv()
        if self.own is not None:
            self.kept(k).wait()

    def pair(self, k):
        if self.own is not None:
            return [(self.own.at[k], 0), (self.stage.at[k], 0)]
        s, partner, right, left, far = seq_places()
        return [(self.partial.at[(far, right, left, s)[k]], -self.first), (self.stage.at[k], 0)]

    def far(self):
        half, away = self.half, self.away
        self.ready(0)
        add_rows(away.at[0], self.pair(0), 0, half)
        self.go(0).start()
        add_rows(away.at[0], self.pair(0), half, half)
        self.go(1).start()

    def beside(self, k):
        half = self.half
        self.ready(k)
        add_rows(self.away.at[k], self.pair(k), half if k == 1 else 0, half)
        self.go(1 + k).start()

    def middle(self):
        self.far()
        self.beside(1)
        self.beside(2)

    def send_step(self, step):
        @pl.when(step == 0)
        def _():
            self.near(3).start()

        @pl.when(step == 1)
        def _():
            self.near(1).start()

        @pl.when(step == 2)
        def _():
            self.near(2).start()
            self.beside(1)

        @pl.when(step == 3)
        def _():
            self.near(0).start()
            self.beside(2)

    def last(self):
        half, away, relay = self.half, self.away, self.relay
        self.go(0).wait_recv()
        add_rows(away.at[1], self.pair(1) + [(relay.at[0], 0)], 0, half)
        self.go(4).start()
        self.go(1).wait_recv()
        add_rows(away.at[2], self.pair(2) + [(relay.at[1], half)], half, half)
        self.go(5).start()

    def finish(self, total):
        self.ready(3)
        for i in (2, 3, 4, 5):
            self.go(i).wait_recv()
        sources = self.pair(3) + [(self.back.at[0], 0), (self.back.at[1], 0)]
        add_rows(total.at[self.block], sources, 0, self.rows)
        for k in range(4):
            self.near(k).wait_send()
        for i in range(6):
            self.go(i).wait_send()


def sum_buffers(rows, width):
    return [
        pltpu.VMEM((4, rows, width), BF16),
        pltpu.VMEM((4, rows, width), BF16),
        pltpu.VMEM((2, rows // 2, width), BF16),
        pltpu.VMEM((3, rows, width), BF16),
        pltpu.VMEM((2, rows, width), BF16),
    ]


MID_ROWS = 32


def by_rows(rows, step, first=0):
    def run(i, carry):
        step(pl.ds(pl.multiple_of(first + i * MID_ROWS, MID_ROWS), MID_ROWS))
        return carry

    lax.fori_loop(0, rows // MID_ROWS, run, 0)


def norm_back_rows(values, gain, grad):
    scale = lax.rsqrt(jnp.mean(values * values, axis=-1, keepdims=True) + 1e-05)
    weighted = grad * gain
    return scale * weighted - values * (
        scale * scale * scale * jnp.mean(weighted * values, axis=-1, keepdims=True)
    )


def comm_params(cid, limit=48):
    return pltpu.CompilerParams(
        collective_id=cid, has_side_effects=True, vmem_limit_bytes=limit << 20
    )


def start_kernel(
    payload, w_qkv, gate_t, q_side, beta_side, everyone, wq, blocks, send, recv, local
):
    s = lax.axis_index("seq")
    greet(ring_peers(), all_plane())
    line = Line(send, recv, local)
    depth, width = w_qkv.shape
    scatter = Scatter(
        line, (2 * s, 2 * s + 1),
        lambda t: w_qkv.at[pl.ds(t * 128, 128), :],
        lambda t, j: wq.at[pl.ds(t * 128, 128), pl.ds(j * width, width)],
    )
    others = [
        Scatter(line, (s + 8 * i,), lambda t: block_of(gate_t, t), lambda t, j, i=i: blocks.at[i])
        for i in (0, 1)
    ]
    ring = RingGather(line, payload, everyone)
    _, at = line.take(0, 2)
    sides = [
        line.local(at, q_side, wq.at[pl.ds(depth, SIDE), :]),
        line.local(at + 1, beta_side, wq.at[pl.ds(0, depth), pl.ds(2 * width, SIDE)]),
    ]

    def place(t, half, quarter):
        size = 64 if quarter is None else 32
        return wq.at[
            pl.ds(t * 128 + half * 64 + (quarter or 0) * 32, size), pl.ds(0, 2 * width)
        ]

    qkv = PlaneGather(line, place)
    scatter.start()
    ring.start()
    for copy in sides:
        copy.start()
    scatter.arrive()
    qkv.first()
    qkv.second()
    ring.middle()
    qkv.third()
    for item in others:
        item.start()
    qkv.fourth()
    ring.finish()
    qkv.finish()
    for item in others:
        item.arrive()
    for item in [scatter] + others:
        item.finish()
    for copy in sides:
        copy.wait()


def start_gather(payload, w_qkv, gate_t, q_side, beta_side):
    seq, wide = lax.axis_size("seq"), payload.shape[1]
    copies = RingGather.COPIES + 3 * Scatter.COPIES + PlaneGather.COPIES
    return pl.pallas_call(
        start_kernel,
        out_shape=(
            jax.ShapeDtypeStruct((seq,) + payload.shape, BF16),
            jax.ShapeDtypeStruct((wide, q_side.shape[1]), BF16),
            jax.ShapeDtypeStruct((2, gate_t.shape[0], 128), BF16),
        ),
        in_specs=[ANY] * 5,
        out_specs=(ANY,) * 3,
        scratch_shapes=sems(copies, 10),
        compiler_params=comm_params(0, 62),
        name="start_gather",
    )(payload, w_qkv, gate_t, q_side, beta_side)


class Feed:
    COPIES = RingGather.COPIES + 2 * PlaneGather.COPIES
    LOCAL = RingGather.LOCAL + 4

    def __init__(self, line, cot, sources, sides, everyone, outs):
        self.line, self.sources, self.sides, self.outs = line, sources, sides, outs
        self.ring = RingGather(line, cot, everyone)
        self.gathers = [PlaneGather(line, columns_place(o)) for o in outs]
        _, self.at = line.take(0, 4)

    def place(self, i):
        s, f = lax.axis_index("seq"), lax.axis_index("fsdp")
        out = self.outs[i % 2]
        if i < 2:
            share = out.shape[0]
            src = self.sources[i].at[pl.ds(pl.multiple_of(s * share, 16), share), :]
            dst = block_of(out, f)
        else:
            src, dst = self.sides[i - 2], out.at[:, pl.ds(out.shape[1] - SIDE, SIDE)]
        return self.line.local(self.at + i, src, dst)

    def start(self):
        for i in range(4):
            self.place(i).start()
        self.ring.start()
        for i, gather in enumerate(self.gathers):
            self.place(i).wait()
            gather.first()

    def stage(self, step):
        @pl.when(step == 1)
        def _():
            for gather in self.gathers:
                gather.second()

        @pl.when(step == 3)
        def _():
            for gather in self.gathers:
                gather.third()
            self.ring.middle()

    def third(self):
        for gather in self.gathers:
            gather.fourth()

    def fourth(self):
        self.gathers[0].finish()
        self.place(2).wait()

    def finish(self):
        self.ring.finish()
        self.gathers[1].finish()
        self.place(3).wait()


def chip_at(step):
    x = lax.axis_index("seq") // 2
    d = jnp.where(step == 2, 3, jnp.where(step == 3, 2, step))
    return lax.rem(x + d, 4)


def feed_forward_kernel(
    partial, blocks, g_side, u_side, wd_in, cot_in,
    tokens, cot, mixed, wo, up, gain, down, chosen,
    middle, grad_middle, partial_down, grad_mixed, early,
    rows2, rows3, cots, wgu, wd, partial2, total,
    both_s, hidden_s, grads_s, both_e, down_e, *rest,
):
    greet(ring_peers(), line_peers())
    buffers, (send, recv, local) = rest[:-3], rest[-3:]
    line = Line(send, recv, local)
    s = lax.axis_index("seq")
    f = lax.axis_index("fsdp")
    rows = tokens.shape[0]
    firsts = (0, rows // 2)
    first_sum = [
        RingSum(line, partial, buffers[5 * i : 5 * i + 5], first)
        for i, first in enumerate(firsts)
    ]
    second_sum = [
        RingSum(line, partial2, (None,) + buffers[10 + 4 * i : 14 + 4 * i], first)
        for i, first in enumerate(firsts)
    ]
    first_gather = [RingGather(line, None, rows2, first, rows // 2) for first in firsts]
    second_gather = [RingGather(line, None, rows3, first, rows // 2) for first in firsts]
    share = g_side.shape[0]
    wg, wu = wgu.at[pl.ds(0, share), :], wgu.at[pl.ds(share, share), :]
    weights = [PlaneGather(line, columns_place(o)) for o in (wg, wu)]
    width = tokens.shape[1]
    _, at = line.take(0, 6)
    mine = [line.local(at + i, blocks.at[i], block_of(o, f)) for i, o in enumerate((wg, wu))]
    others = [
        line.local(at + 2, g_side, wg.at[:, pl.ds(width, SIDE)]),
        line.local(at + 3, u_side, wu.at[:, pl.ds(width, SIDE)]),
        line.local(at + 4, wd_in, wd),
        line.local(at + 5, cot_in, cots),
    ]
    for copy in mine:
        copy.start()
    for item in first_sum:
        item.start()
    for copy, item in zip(mine, weights):
        copy.wait()
        item.first()
    for copy in others:
        copy.start()
    first_sum[0].middle()
    for item in weights:
        item.second()
    first_sum[1].middle()
    for item in first_sum:
        item.last()

    def norm_rows(rows):
        inner = total[rows, width:].astype(BF16)
        value = tokens[rows, :].astype(F32) + (total[rows, :width] + mm(inner, up[...]))
        middle[rows, :] = value
        scale = lax.rsqrt(jnp.mean(value * value, axis=-1, keepdims=True) + 1e-05)
        normed = (value * scale * gain[...]).astype(BF16)
        rows2[s, rows, :width] = normed
        rows2[s, rows, width:] = (inner.astype(F32) + mm_nt(normed, down[...])).astype(BF16)

    first_sum[0].finish(total)
    by_rows(rows // 2, norm_rows)
    first_gather[0].start()
    weights[0].third()
    first_sum[1].finish(total)
    by_rows(rows // 2, norm_rows, rows // 2)
    first_gather[1].start()
    weights[1].third()
    for item in weights:
        item.fourth()
    for item in weights:
        item.finish()
    for copy in others:
        copy.wait()
    pair = 2 * rows

    def chip(step, carry):
        for item in first_gather:
            item.reach(step)
        k = chip_at(step)
        both = pl.ds(k * 2, 2)
        normed = rows2[both].reshape(pair, width + SIDE)
        grads = cots[both].reshape(pair, width + SIDE)
        both_s[...] = mm_nt(normed, wgu[...])
        hidden = mm_nt(grads, wd[...])
        gate, upper = both_s[:, :share], both_s[:, share:]
        sigma = sigmoid(gate)
        silu = gate * sigma
        hidden_s[k] = (silu * upper).astype(BF16)
        grads_s[k, :, :share] = (hidden * upper * sigma * (1.0 + gate * (1.0 - sigma))).astype(BF16)
        grads_s[k, :, share:] = (hidden * silu).astype(BF16)
        partial2[both] = (
            mm(grads_s[k], wgu[...])
            .astype(BF16)
            .reshape(2, pair // 2, width + SIDE)
        )
        for item in second_sum:
            item.send_step(step)
        return carry

    lax.fori_loop(0, 4, chip, 0)
    for item in second_sum:
        item.far()
    for item in second_sum:
        item.last()

    def back_rows(rows):
        inner = total[rows, width:].astype(BF16)
        grad = total[rows, :width] + mm(inner, down[...])
        result = cot[rows, :].astype(F32) + norm_back_rows(middle[rows, :], gain[...], grad)
        grad_middle[rows, :] = result
        low = result.astype(BF16)
        rows3[s, rows, :width] = low
        rows3[s, rows, width:] = (inner.astype(F32) + mm_nt(low, up[...])).astype(BF16)

    second_sum[0].finish(total)
    by_rows(rows // 2, back_rows)
    second_gather[0].start()
    second_sum[1].finish(total)
    by_rows(rows // 2, back_rows, rows // 2)
    second_gather[1].start()
    both_e[...] = jnp.zeros_like(both_e)
    down_e[...] = jnp.zeros_like(down_e)

    def down_project(k, carry):
        both = pl.ds(k * 2, 2)
        partial_down[both] = (
            mm(hidden_s[k], wd[...]).astype(BF16).reshape(2, rows, width + SIDE)
        )
        side = rows2[both, :, width:].reshape(pair, SIDE)
        both_e[...] += mm_tn(side, grads_s[k])
        down_e[...] += mm_tn(cots[both, :, width:].reshape(pair, SIDE), hidden_s[k])
        return carry

    lax.fori_loop(0, 4, down_project, 0)
    for item in first_gather:
        item.sent()

    def out_back(step, carry):
        for item in second_gather:
            item.reach(step)
        k = chip_at(step)
        grads = rows3[pl.ds(k * 2, 2)].reshape(pair, width + SIDE)
        grad_mixed[pl.ds(pl.multiple_of(k * pair, pair), pair), :] = mm_nt(grads, wo[...]).astype(
            BF16
        )
        return carry

    lax.fori_loop(0, 4, out_back, 0)
    rank = early.shape[2]
    part = mixed.shape[1]
    own_part = pl.ds(pl.multiple_of(s * part, 128), part)
    flat = lambda v: v.reshape(-1, v.shape[-1])
    side2, side3 = flat(rows2[:, :, width:]), flat(rows3[:, :, width:])
    first = [both_e[rank : 2 * rank, :].astype(BF16), chosen[...]]
    second = [
        mm_tn(side3, mixed[...])[:rank].astype(BF16),
        mm_tn(side2, flat(rows3[:, :, own_part]))[:rank].astype(BF16),
        mm_tn(side3, flat(rows2[:, :, own_part]))[rank : 2 * rank].astype(BF16),
        down_e[:rank, :].astype(BF16),
        chosen[:, : SIDE // 2],
    ]
    n = early.shape[3]
    for half, parts in enumerate((first, second)):
        piece = jnp.concatenate(parts, axis=1)
        early[half, 0] = piece[:, :n]
        early[half, 1] = piece[:, n:]
    for item in second_gather:
        item.sent()


def feed_forward(
    partial, blocks, g_side, u_side, wd, cots, tokens, cot, mixed, wo, up, gain, down, chosen
):
    seq, rows, wide = partial.shape
    share = g_side.shape[0]
    rank, part = chosen.shape[0], mixed.shape[1]
    whole = pltpu.VMEM((seq, rows, wide), BF16)
    weight = pltpu.VMEM((share, wide), BF16)
    buffers = sum_buffers(rows // 2, wide)
    scratch = [
        pltpu.VMEM((2 * rows, 2 * share), F32),
        pltpu.VMEM((seq // 2, 2 * rows, share), BF16),
        pltpu.VMEM((seq // 2, 2 * rows, 2 * share), BF16),
        pltpu.VMEM((SIDE, 2 * share), F32),
        pltpu.VMEM((SIDE, share), F32),
    ]
    return pl.pallas_call(
        feed_forward_kernel,
        out_shape=(
            jax.ShapeDtypeStruct((rows, wide - SIDE), F32),
            jax.ShapeDtypeStruct((rows, wide - SIDE), F32),
            jax.ShapeDtypeStruct((seq, rows, wide), BF16),
            jax.ShapeDtypeStruct((seq * rows, part), BF16),
            jax.ShapeDtypeStruct((2, 2, rank, share + SIDE // 2), BF16),
        ),
        in_specs=[ANY] * 6 + [VMEM] * 8,
        out_specs=(VMEM,) * 5,
        scratch_shapes=[whole, whole, whole, pltpu.VMEM((2 * share, wide), BF16), weight, whole]
        + [pltpu.VMEM((rows, wide), F32)]
        + scratch
        + buffers * 2
        + buffers[1:] * 2
        + sems(4 * RingSum.COPIES + 4 * RingGather.COPIES + 2 * PlaneGather.COPIES, 26),
        compiler_params=comm_params(2, 63),
        name="feed_forward",
    )(partial, blocks, g_side, u_side, wd, cots, tokens, cot, mixed, wo, up, gain, down, chosen)


class EarlySum:
    COPIES, LOCAL = PlaneGather.COPIES + RingGather.COPIES, 1 + RingGather.LOCAL

    def __init__(self, line, early, pieces, total, out):
        self.line, self.early, self.pieces, self.total = line, early, pieces, total
        _, self.local_at = line.take(0, 1)
        self.ring = RingGather(line, total, out)

        def place(f, half, quarter):
            return pieces.at[f, half] if quarter is None else pieces.at[f, half, quarter]

        self.plane = PlaneGather(line, place)

    def start(self):
        own = self.line.local(
            self.local_at, self.early, self.pieces.at[lax.axis_index("fsdp")]
        )
        own.start()
        own.wait()
        self.plane.first()

    def add(self):
        self.plane.finish()
        f = lax.axis_index("fsdp")
        half = lax.rem(f, 2)
        lane = lax.broadcasted_iota(jnp.int32, (1, SIDE), 1)
        mark = jnp.where(half == 0, 0, SIDE // 2) + f // 2
        totals = [None, None]
        for t in range(16):
            pair = [self.pieces[t, half, q].astype(F32) for q in (0, 1)]
            marks = pair[1][:1, -SIDE:]
            uses = jnp.sum(jnp.where(lane == mark, marks, 0.0), axis=1, keepdims=True)
            totals = [
                p * uses if total is None else total + p * uses for p, total in zip(pair, totals)
            ]
        self.total[0] = totals[0].astype(BF16)
        self.total[1] = totals[1].astype(BF16)
        self.ring.start()


def by_adapter(plane, marks, first, out):
    count, wide = out.shape[0], out.shape[2]
    fsdp, parts, _, n = plane.shape
    uses = [marks[f].astype(F32)[:1] for f in range(fsdp)]
    for q in range(parts):
        cut = min(n, wide - q * n)
        if cut <= 0:
            continue
        items = [plane[f, q].astype(F32)[:, :cut] for f in range(fsdp)]
        for a in range(count):
            total = None
            for f in range(fsdp):
                item = items[f] * uses[f][:, first + a : first + a + 1]
                total = item if total is None else total + item
            out[a, :, q * n : q * n + cut] = total.astype(BF16)


def lay_out_early(whole, share, part):
    fsdp, seq, _, rank, n = whole.shape
    count = fsdp // 2

    def kernel(whole, gateup, mix_down, mix_up, gu_down, ff_down):
        for t in range(seq):
            first = jnp.concatenate([whole[0, t, 0], whole[0, t, 1]], axis=1).astype(F32)
            gateup[0, :, t * share : (t + 1) * share] = first[:, :share]
            at = (seq + t) * share
            gateup[0, :, at : at + share] = first[:, share : 2 * share]
            second = jnp.concatenate([whole[1, t, 0], whole[1, t, 1]], axis=1).astype(F32)
            for i, out in enumerate((mix_down, mix_up, gu_down)):
                out[0, :, t * part : (t + 1) * part] = second[:, i * part : (i + 1) * part]
            ff_down[0, :, t * share : (t + 1) * share] = second[:, 3 * part : 3 * part + share]

    widths = (2 * share * seq,) + (part * seq,) * 3 + (share * seq,)
    return pl.pallas_call(
        kernel,
        grid=(count,),
        out_shape=tuple(jax.ShapeDtypeStruct((count, rank, w), F32) for w in widths),
        in_specs=[pl.BlockSpec((2, seq, 2, rank, n), lambda a: (a, 0, 0, 0, 0))],
        out_specs=tuple(pl.BlockSpec((1, rank, w), lambda a: (a, 0, 0)) for w in widths),
        compiler_params=pltpu.CompilerParams(vmem_limit_bytes=32 << 20),
        name="lay_out_early",
    )(whole)


def lay_out_late(up, low, part):
    seq, count, rank, columns = up.shape

    def kernel(up, low, qkv_up, qkv_down, ff_up):
        for t in range(seq):
            qkv_up[0, :, t * columns : (t + 1) * columns] = up[t, 0].astype(F32)
            qkv_down[0, :, t * part : (t + 1) * part] = low[t, 0, :, :part].astype(F32)
            ff_up[0, :, t * part : (t + 1) * part] = low[t, 0, :, part:].astype(F32)

    widths = (columns * seq, part * seq, part * seq)
    cut = lambda n: pl.BlockSpec((seq, 1, rank, n), lambda a: (0, a, 0, 0))
    return pl.pallas_call(
        kernel,
        grid=(count,),
        out_shape=tuple(jax.ShapeDtypeStruct((count, rank, w), F32) for w in widths),
        in_specs=[cut(columns), cut(2 * part)],
        out_specs=tuple(pl.BlockSpec((1, rank, w), lambda a: (a, 0, 0)) for w in widths),
        compiler_params=pltpu.CompilerParams(vmem_limit_bytes=32 << 20),
        name="lay_out_late",
    )(up, low)


def prepare_kernel(
    places, tokens, cot, gain, q_down, q_up, m_down, m_up, g_down, gu_up, f_down, f_up, w_beta,
    conv, docs,
    payload, cots, q_side, beta_side, out_side, g_side, u_side, f_side,
    m_lines, g_lines, f_lines, q_lines, dcol, drow, taps, chosen,
):
    which, s = places[0], places[1]
    rank, width = q_down.shape[1], tokens.shape[1]
    share = g_side.shape[0]

    def lines(out, block, first):
        parts = [jnp.zeros((first, width), BF16)] if first else []
        parts += [block, jnp.zeros((SIDE - first - rank, width), BF16)]
        out[...] = jnp.concatenate(parts, axis=0)

    lines(m_lines, m_up[0], 0)
    lines(g_lines, g_down[0], rank)
    lines(f_lines, f_up[0], 0)
    lines(q_lines, q_down[0], rank)

    def turned(block, first):
        n = block.shape[1]
        parts = [jnp.zeros((first, n), F32)] if first else []
        parts += [block.astype(F32), jnp.zeros((SIDE - first - block.shape[0], n), F32)]
        return jnp.concatenate(parts, axis=0).T.astype(BF16)

    def window(ref, base):
        size = -(-share // 128) * 128
        tile = base // 128 + (s * share) // 128
        wide = ref[0, :, pl.ds(pl.multiple_of(tile * 128, 128), size)].astype(F32)
        late = jnp.concatenate([wide[:, 64:], wide[:, :64]], axis=1)
        return jnp.where(lax.rem(s, 2) == 1, late, wide)

    g_side[...] = turned(window(gu_up, 0), rank)[:share]
    u_side[...] = turned(window(gu_up, f_down.shape[2]), rank)[:share]
    f_side[...] = turned(window(f_down, 0), 0)[:share]
    out_side[...] = turned(m_down[0], 0)
    heads = taps.shape[1] // conv.shape[2]
    row = lax.broadcasted_iota(jnp.int32, w_beta.shape, 0)
    beta = w_beta[...].astype(F32)
    rows = [
        jnp.sum(jnp.where(row == s * heads + h, beta, 0.0), axis=0, keepdims=True)
        for h in range(heads)
    ]
    beta_side[...] = turned(jnp.concatenate(rows, axis=0), 0)
    q_side[...] = jnp.zeros_like(q_side)
    q_side[rank : 2 * rank, : q_up.shape[2]] = q_up[0]

    value = tokens[...].astype(F32)
    scale = lax.rsqrt(jnp.mean(value * value, axis=-1, keepdims=True) + 1e-05)
    normed = (value * scale * gain[...]).astype(BF16)
    payload[:, :width] = normed
    payload[:, width:] = mm_nt(normed, q_lines[...]).astype(BF16)
    cots[:, :width] = cot[...]
    cots[:, width:] = mm_nt(cot[...], f_lines[...]).astype(BF16)

    chunks = drow.shape[0]
    dcol[:PAD, :] = jnp.full((PAD, CH), -1, jnp.int32)
    dcol[PAD + chunks * CH :, :] = jnp.full((PAD, CH), -1, jnp.int32)
    for c in range(chunks):
        line = docs[:, c * CH : (c + 1) * CH]
        drow[c : c + 1, :] = line
        square = jnp.broadcast_to(line.astype(F32), (CH, CH)).T
        dcol[PAD + c * CH : PAD + (c + 1) * CH, :] = square.astype(jnp.int32)
    third = conv.shape[2]
    for t in range(conv.shape[0]):
        for h in range(heads):
            taps[t : t + 1, h * third : (h + 1) * third] = conv[t, pl.ds(s * heads + h, 1), :]
    lane = lax.broadcasted_iota(jnp.int32, chosen.shape, 1)
    chosen[...] = (lane == which).astype(F32).astype(BF16)


def prepare(
    places, tokens, cot, gain, q_down, q_up, m_down, m_up, g_down, gu_up, f_down, f_up, w_beta,
    conv, docs, seq,
):
    rows, width = tokens.shape
    rank = q_down.shape[1]
    columns, part, share = q_up.shape[2] // seq, width // seq, f_down.shape[2] // seq
    length = docs.shape[1]
    one = lambda n: pl.BlockSpec((1, rank, n), lambda i, p: (p[0], 0, 0))
    mine = lambda n: pl.BlockSpec((1, rank, n), lambda i, p: (p[0], 0, p[1]))
    full = lambda a: pl.BlockSpec(a.shape, lambda i, p, a=a: (0,) * a.ndim)
    S = jax.ShapeDtypeStruct
    outs = (
        S((rows, width + SIDE), BF16), S((rows, width + SIDE), BF16),
        S((SIDE, columns + SIDE), BF16), S((width, SIDE), BF16), S((part, SIDE), BF16),
        S((share, SIDE), BF16), S((share, SIDE), BF16), S((share, SIDE), BF16),
        S((SIDE, width), BF16), S((SIDE, width), BF16), S((SIDE, width), BF16),
        S((SIDE, width), BF16),
        S((length + 2 * PAD, CH), jnp.int32), S((length // CH, CH), jnp.int32),
        S((conv.shape[0], columns), F32), S((rank, SIDE), BF16),
    )
    return pl.pallas_call(
        prepare_kernel,
        out_shape=outs,
        grid_spec=pltpu.PrefetchScalarGridSpec(
            num_scalar_prefetch=1,
            grid=(1,),
            in_specs=[
                full(tokens), full(cot), full(gain), one(width), mine(columns), mine(part),
                one(width), one(width), one(gu_up.shape[2]), one(f_down.shape[2]), one(width),
                full(w_beta), full(conv), full(docs),
            ],
            out_specs=[pl.BlockSpec(o.shape, lambda i, p, o=o: (0,) * len(o.shape)) for o in outs],
        ),
        compiler_params=pltpu.CompilerParams(vmem_limit_bytes=62 << 20),
        name="prepare",
    )(places, tokens, cot, gain, q_down, q_up, m_down, m_up, g_down, gu_up, f_down, f_up, w_beta,
      conv, docs)


BOTH = ("fsdp", "seq")


def body(
    tokens,
    segments,
    adapter_index,
    attn_gain,
    w_qkv,
    w_beta,
    conv_weight,
    head_gain,
    w_out,
    ffn_gain,
    w_gateup,
    w_down,
    qkv_down,
    qkv_up,
    mixout_down,
    mixout_up,
    gateup_down,
    gateup_up,
    ffnout_down,
    ffnout_up,
    cotangent,
):
    seq = lax.axis_size("seq")
    s = lax.axis_index("seq")
    width = tokens.shape[1]
    count = qkv_down.shape[0]
    which = adapter_index[0]
    length = segments.shape[1]

    turn = lambda v: jnp.swapaxes(v, 1, 2)
    (
        payload, cots, q_side, beta_side, out_side, g_side, u_side, f_side,
        m_lines, g_lines, f_lines, q_lines, dcol, drow, taps, chosen,
    ) = prepare(
        jnp.stack([which, s]), tokens, cotangent, attn_gain[None],
        turn(qkv_down), qkv_up, turn(mixout_down), mixout_up, turn(gateup_down), gateup_up,
        turn(ffnout_down), ffnout_up, w_beta.T, conv_weight, segments, seq,
    )

    normed, wq, blocks = start_gather(payload, w_qkv, w_gateup.T, q_side, beta_side)
    normed = normed.reshape(length, -1)
    fixed = (dcol, drow, taps, head_gain[None])
    mixed, o_kept, t_kept, d_kept, s_kept, partial, joined, cot, wo, wd = mixer_fwd(
        normed, wq, cots, w_out, w_down, out_side, f_side, *fixed
    )

    middle, grad_middle, partial_down, grad_mixed, early = feed_forward(
        partial, blocks, g_side, u_side, wd, cot, tokens, cotangent, mixed, wo,
        m_lines, ffn_gain[None], g_lines, chosen,
    )

    layer_out, input_grad, early, up, low = mixer_bwd(
        joined, partial_down, early, normed, wq, cot.reshape(length, -1), q_side, middle, f_lines,
        *fixed, grad_mixed, o_kept, t_kept, d_kept, s_kept,
        tokens, grad_middle, q_lines, attn_gain[None], chosen, count,
    )
    gateup_g, mixdown_g, mixup_g, gudown_g, ffdown_g = lay_out_early(
        early, w_down.shape[0] // seq, width // seq
    )
    qkvup_g, qkvdown_g, ffup_g = lay_out_late(up, low, width // seq)
    return (
        layer_out,
        input_grad,
        turn(qkvdown_g),
        qkvup_g,
        turn(mixdown_g),
        mixup_g,
        turn(gudown_g),
        gateup_g,
        turn(ffdown_g),
        ffup_g,
    )


def solution(mesh):
    tokens, columns = P(BOTH, None), P(None, "fsdp")
    placed = (
        tokens, P("fsdp", None), P("fsdp"), P(), columns, P(), P(), P(), columns, P(), columns,
        columns, P(), P(), P(), P(), P(), P(), P(), P(), tokens,
    )
    return jax.shard_map(
        body,
        mesh=mesh,
        in_specs=placed,
        out_specs=(tokens, tokens) + (P(),) * 8,
        check_vma=False,
    )
```
